32 devices in a mesh: rows: 8 (over z, x), hid: 4 (over y, core).
Axes of the slice: x: 2, y: 2, z: 4, core: 2. Of those that a mesh axis runs over, the one named last changes fastest.
Arguments:
- char_ids: int32 [512, 8], P('rows'), may hold values from 0 to 274
- lang_ids: int32 [512], P('rows'), may hold values from 0 to 7, as said below
- vocab_masks: int32 [8, 275], replicated, may hold values from 0 to 1, as said below
- targets: int32 [2, 512, 8], P(None, 'rows'), may hold values from 0 to 274, as said below
- embedding: bfloat16 [2, 275, 100], replicated, may hold values from -6 to 6
- w_in: bfloat16 [2, 100, 4, 2048], P(None, None, None, 'hid'), may hold values from -0.625 to 0.625
- w_rec: bfloat16 [2, 2048, 4, 2048], P(None, 'rows', None, 'hid'), may hold values from -0.5 to 0.5
- b_in: bfloat16 [2, 4, 2048], P(None, None, 'hid'), may hold values from -3 to 3
- b_rec: bfloat16 [2, 4, 2048], P(None, None, 'hid'), may hold values from -3 to 3
- w_dec: bfloat16 [2, 2048, 275], P(None, 'hid'), may hold values from -0.5 to 0.5
- b_dec: bfloat16 [2, 275], replicated, may hold values from -6 to 6
Outputs:
- total_loss: float32 [], replicated
- grad_embedding: float32 [2, 275, 100], replicated
- grad_w_in: float32 [2, 100, 4, 2048], P(None, None, None, 'hid')
- grad_w_rec: float32 [2, 2048, 4, 2048], P(None, 'rows', None, 'hid')
- grad_b_in: float32 [2, 4, 2048], P(None, None, 'hid')
- grad_b_rec: float32 [2, 4, 2048], P(None, None, 'hid')
- grad_w_dec: float32 [2, 2048, 275], P(None, 'hid')
- grad_b_dec: float32 [2, 275], replicated
The draws below stay inside these ranges and needn't reach their ends.
Inputs may be any that keep to these rules, and one draw needn't show every extreme that they name: `lang_ids`: rows stand in order of language, and every language has a row. `vocab_masks`: each language allows exactly 192 characters. `targets`: every target is a character that its row's language allows.
All inputs are finite; a program needn't handle non-finite values.
Results may differ from the reference program's by a relative error of at most 0.014.
Values may be sent and summed in bfloat16 or wider, within the bound.
A program may use at most 192 MiB of HBM per device.

```python
import math
import jax
import jax.numpy as jnp
from jax import lax

H = 2048
E = 100
V = 275
LANGS = 8
KEEP = 192
SEQ = 8
ROWS = 512


def language_tables(key):
    lang_key = jax.random.fold_in(key, 11)
    order_key = jax.random.fold_in(key, 12)
    raw_ids = jax.random.randint(lang_key, (ROWS,), 0, LANGS)
    raw_ids = raw_ids.at[:LANGS].set(jnp.arange(LANGS, dtype=jnp.int32))
    lang_ids = jnp.sort(raw_ids)
    order_keys = jax.random.split(order_key, LANGS)
    orders = jax.vmap(lambda one_key: jax.random.permutation(one_key, V))(order_keys)
    return (lang_ids.astype(jnp.int32), orders.astype(jnp.int32))


def draw_lang_ids(key, part):
    lang_ids, orders = language_tables(key)
    return lang_ids


def draw_vocab_masks(key, part):
    lang_ids, orders = language_tables(key)
    positions = jnp.argsort(orders, axis=1, stable=True)
    return (positions < KEEP).astype(jnp.int32)


def draw_targets(key, part):
    lang_ids, orders = language_tables(key)
    key = jax.random.fold_in(key, 3)
    pick_index = jax.random.randint(key, (2, ROWS, SEQ), 0, KEEP)
    row_orders = jnp.broadcast_to(orders[lang_ids][None], (2, ROWS, V))
    return jnp.take_along_axis(row_orders, pick_index, axis=2).astype(jnp.int32)


def with_ends(values, own_key, least, top_value):
    index_at = [jax.random.randint(jax.random.fold_in(own_key, axis), (), 0, length) for axis, length in enumerate(values.shape)]
    main_axis = values.shape.index(max(values.shape))
    beside = index_at[:main_axis] + [(index_at[main_axis] + 1) % values.shape[main_axis]] + index_at[main_axis + 1:]
    return values.at[tuple(index_at)].set(least).at[tuple(beside)].set(top_value)


def level_of(rng, extent, cuts, smallest, largest):
    loudness, own = 1.0, jax.random.fold_in(rng, 6)
    for axis_at, shards_of in cuts:
        steps = jnp.exp(jax.random.uniform(jax.random.fold_in(own, axis_at), (shards_of,), jnp.float32, smallest / len(cuts), largest / len(cuts)))
        loudness = loudness * jnp.repeat(steps, extent[axis_at] // shards_of).reshape([-1 if axis == axis_at else 1 for axis in range(len(extent))])
    return loudness


def normal_values(stream_key, dims, deviation, limit, cuts=(), kind=jnp.bfloat16):
    entries = jax.random.normal(stream_key, dims, jnp.float32) * deviation
    if len(cuts) > 0:
        entries = level_of(stream_key, dims, cuts, -0.22, 0.18) * entries
    return jnp.clip(entries, min=-limit, max=limit).astype(kind)


def setup_inputs(seed: int = 0) -> dict:
    keys = jax.random.split(jax.random.key(seed), 12)
    return {
        "char_ids": with_ends(jax.random.randint(keys[0], (ROWS, SEQ), 0, V), jax.random.fold_in(keys[0], 1), 0, V - 1).astype(jnp.int32),
        "lang_ids": draw_lang_ids(jax.random.fold_in(keys[11], 71), 0),
        "vocab_masks": draw_vocab_masks(jax.random.fold_in(keys[11], 71), 0),
        "targets": draw_targets(jax.random.fold_in(keys[11], 71), 0),
        "embedding": normal_values(keys[4], (2, V, E), 1.0, 6.0),
        "w_in": normal_values(keys[5], (2, E, 4, H), E ** -0.5, 0.625, ((3, 4),)),
        "w_rec": normal_values(keys[6], (2, H, 4, H), (H // 16) ** -0.5, 0.5, ((1, 8), (3, 4))),
        "b_in": normal_values(keys[7], (2, 4, H), 0.5, 3.0, ((2, 4),)),
        "b_rec": normal_values(keys[8], (2, 4, H), 0.5, 3.0, ((2, 4),)),
        "w_dec": normal_values(keys[9], (2, H, V), (H // 16) ** -0.5, 0.5, ((1, 4),)),
        "b_dec": normal_values(keys[10], (2, V), 1.0, 6.0),
    }


@jax.custom_vjp
def low(v):
    return lax.optimization_barrier(v.astype(jnp.bfloat16)).astype(jnp.float32)

@jax.custom_vjp
def low_back(v):
    return v

def low_keep(v):
    return (low(v), None)

def low_pass(kept, grad):
    return (grad,)

def back_keep(v):
    return (v, None)

def back_low(kept, grad):
    return (low(grad),)
low.defvjp(low_keep, low_pass)
low_back.defvjp(back_keep, back_low)
highest = lax.Precision.HIGHEST

def direction_loss(embedding, w_in, w_rec, b_in, b_rec, w_dec, b_dec, seq_chars, seq_targets, allowed, loss_scale):
    inputs_seq = low(embedding)[seq_chars.T]
    in_matrix = low(w_in).reshape(E, 4 * H)
    gates_in = jnp.einsum('lge,ef->lgf', inputs_seq, in_matrix, precision=highest) + (b_in + b_rec).reshape(4 * H)
    recurrent_matrix = low(w_rec).reshape(H, 4 * H)

    def forward_step(state_pair, gate_input):
        state_low, cell_state = state_pair
        preact = low_back(gate_input + jnp.dot(state_low, recurrent_matrix, precision=highest))
        gate_parts = preact.reshape(preact.shape[0], 4, H)
        in_gate = jax.nn.sigmoid(gate_parts[:, 0])
        forget_gate = jax.nn.sigmoid(gate_parts[:, 1])
        cell_gate = jnp.tanh(gate_parts[:, 2])
        out_gate = jax.nn.sigmoid(gate_parts[:, 3])
        cell_next = forget_gate * cell_state + in_gate * cell_gate
        state_next = low(out_gate * jnp.tanh(cell_next))
        return ((state_next, cell_next), state_next)
    row_total = seq_chars.shape[0]
    start_pair = (jnp.zeros((row_total, H), gates_in.dtype), jnp.zeros((row_total, H), gates_in.dtype))
    _, states = lax.scan(jax.checkpoint(forward_step), start_pair, gates_in)
    logits = low_back(jnp.einsum('lgh,hv->lgv', states, low(w_dec), precision=highest) + b_dec)
    masked = jnp.where(allowed[None] > 0, logits, -1000000000.0)
    log_total = jax.nn.logsumexp(masked, axis=-1)
    picked = jnp.take_along_axis(logits, seq_targets.T[..., None], axis=-1)[..., 0]
    return jnp.sum(log_total - picked) * loss_scale

def full_loss(weights, character_rows, target_rows, allowed, loss_scale):
    total_value = 0.0
    for direction in range(2):
        if direction == 0:
            seq_chars = character_rows
            seq_targets = target_rows[0]
        else:
            seq_chars = character_rows[:, ::-1]
            seq_targets = target_rows[1][:, ::-1]
        pieces = [weight[direction] for weight in weights]
        total_value = total_value + direction_loss(*pieces, seq_chars, seq_targets, allowed, loss_scale)
    return total_value

def reference(char_ids, lang_ids, vocab_masks, targets, embedding, w_in, w_rec, b_in, b_rec, w_dec, b_dec):
    weights = tuple((weight.astype(jnp.float32) for weight in (embedding, w_in, w_rec, b_in, b_rec, w_dec, b_dec)))
    allowed_rows = vocab_masks[lang_ids]
    group_rows = math.gcd(ROWS, max(1, 4096 // SEQ))
    group_count = ROWS // group_rows
    loss_scale = 1.0 / (ROWS * SEQ)
    char_groups = char_ids.reshape(group_count, group_rows, SEQ)
    target_groups = jnp.transpose(targets.reshape(2, group_count, group_rows, SEQ), (1, 0, 2, 3))
    allowed_groups = allowed_rows.reshape(group_count, group_rows, V)

    def accumulate(state_pair, group_data):
        character_rows, target_rows, allowed = group_data
        loss_value, pullback = jax.vjp(lambda both: full_loss(both, character_rows, target_rows, allowed, loss_scale), weights)
        gradients = pullback(jnp.ones_like(loss_value))[0]
        return ((state_pair[0] + loss_value, jax.tree.map(jnp.add, state_pair[1], gradients)), None)
    start_state = (jnp.zeros((), jnp.float32), jax.tree.map(jnp.zeros_like, weights))
    (total_loss, gradients), _ = lax.scan(accumulate, start_state, (char_groups, target_groups, allowed_groups))
    return (total_loss, gradients[0], gradients[1], gradients[2], gradients[3], gradients[4], gradients[5], gradients[6])
```

```python
import functools
from typing import NamedTuple

import jax
import jax.numpy as jnp
from jax import lax
from jax.experimental import pallas as pl
from jax.experimental.pallas import tpu as pltpu
from jax.sharding import PartitionSpec as P

MESH = pl.DeviceIdType.MESH
F32 = jnp.float32
BF16 = jnp.bfloat16
masked_value = -1000000000.0


def ceil_to(n, m):
    return (n + m - 1) // m * m


class Dims(NamedTuple):
    R: int
    RR: int
    Hy: int
    H: int
    KR: int
    U: int
    RL: int
    L: int
    V: int
    E: int
    LANGS: int
    scale: float

    @property
    def U2(self):
        return 2 * self.U

    @property
    def NR(self):
        return 2 * self.RL

    @property
    def VP(self):
        return ceil_to(self.V, 128)

    @property
    def VB(self):
        return ceil_to(self.V, 16)

    @property
    def EP(self):
        return ceil_to(self.E + 2, 128)

    @property
    def EW(self):
        return ceil_to(self.E + 2, 16)

    @property
    def V8(self):
        return ceil_to(self.V, 8)

    @property
    def VS(self):
        return self.V8 + 8

    @property
    def peers(self):
        far = [(1, k) for k in range(1, self.Hy)]
        beside = [(0, k) for k in range(1, self.Hy)]
        return far + beside + [(1, 0)]


Z_STEPS = ((1, 0), (1, 1), (0, 1))


def dot(a, b):
    return jnp.dot(a, b, preferred_element_type=F32)


def dot_nt(a, b):
    return lax.dot_general(a, b, (((1,), (1,)), ((), ())), preferred_element_type=F32)


def dot_tn(a, b):
    return lax.dot_general(a, b, (((0,), (0,)), ((), ())), preferred_element_type=F32)


def flip(bit, step):
    return 1 - bit if step else bit


def kernel(
    dims,
    ids_in, win_in, wrec_in, wdec_in, emb_ref, bdec_ref, mask_ref,
    grec_out, gwin_out, gwd_out, small_out,
    ids, win, W, wd, x, xp, allowed, acc, st, stp, gs, cell, lg, lgp, lossv, gb,
    dh, cg, pg, pgx, psend, precv, dW, gwin, gemb, gwd, gwd_s, gwd_r, gwin_s, gwin_r, recvB, esend, erecv,
    lsem, ids_s, ids_r, win_s2, win_r2, wdy_s, wdy_r, wdc_s, wdc_r, wz_s, wz_r, wx_s, wx_r, wc_s, wc_r, xp_s, xp_r,
    f_s, f_r, stp_s, stp_r, lgp_s, lgp_r, b_s, b_r, pgx_s, pgx_r,
    gwdr_s, gwdr_r, gwdz_s, gwdz_r, gwr_s, gwr_r, gwz_s, gwz_r, B_s, B_r, C_s, C_r, e_s, e_r,
):
    R, RR, Hy, U, U2, NR, L, VP = dims.R, dims.RR, dims.Hy, dims.U, dims.U2, dims.NR, dims.L, dims.VP
    KR, EW, VB, V8, VS = dims.KR, dims.EW, dims.VB, dims.V8, dims.VS
    peers = dims.peers
    rho, hid = lax.axis_index("rows"), lax.axis_index("hid")
    d, g, r = rho // (R // 2), lax.rem(rho // RR, 2), lax.rem(rho, RR)
    y, c = hid // 2, lax.rem(hid, 2)
    mine = y * 2 + g
    part = d * 2 + g

    def dev(dd, gg, rr, yy, cc):
        return (dd * (R // 2) + gg * RR + rr, yy * 2 + cc)

    def copy_to(src, dst, send, recv, device):
        return pltpu.make_async_remote_copy(
            src_ref=src, dst_ref=dst, send_sem=send, recv_sem=recv, device_id=device, device_id_type=MESH
        )

    def add_r(step):
        return lax.rem(r + step, RR)

    def add_y(step):
        return lax.rem(y + step, Hy)

    def rows_of(dd, gg, rr):
        index = dd * (R // 2) + gg * RR + rr
        per = U // KR
        block = index // per
        hid_of, g_of = block // 2, lax.rem(block, 2)
        chip = (hid_of // 2) * 2 + g_of
        row = chip * U2 + lax.rem(hid_of, 2) * U + lax.rem(index, per) * KR
        return pl.ds(pl.multiple_of(row, KR), KR)

    def chip_rows(m):
        return pl.ds(pl.multiple_of(m * U2, U2), U2)

    partner = dev(d, g, r, y, 1 - c)

    def z_dev(j):
        return dev(flip(d, Z_STEPS[j][0]), flip(g, Z_STEPS[j][1]), r, y, c)

    def r_dev(step):
        return dev(d, g, add_r(step), y, c)

    def y_dev(step):
        return dev(d, g, r, add_y(step), c)

    def peer_dev(p):
        return dev(d, flip(g, peers[p][0]), r, add_y(peers[p][1]), c)

    barrier = pltpu.get_barrier_semaphore()
    greeted = [z_dev(j) for j in range(3)] + [r_dev(k) for k in range(1, RR)] + [partner]
    greeted += [peer_dev(p) for p in range(len(peers)) if peers[p] != (1, 0)]
    for device in greeted:
        pl.semaphore_signal(barrier, inc=1, device_id=device, device_id_type=MESH)
    pl.semaphore_wait(barrier, len(greeted))

    def ids_copy(j):
        return copy_to(ids_in.at[flip(d, Z_STEPS[j][0]), c], ids.at[part], ids_s.at[j], ids_r.at[j], z_dev(j))

    def wz_copy(j):
        there = wrec_in.at[flip(d, Z_STEPS[j][0]), flip(g, Z_STEPS[j][1])]
        return copy_to(there, W.at[c, :, rows_of(d, g, r), :], wz_s.at[j], wz_r.at[j], z_dev(j))

    def z_block(j):
        steps = Z_STEPS[j] if j < 3 else (0, 0)
        return flip(d, steps[0]), flip(g, steps[1])

    def w_block(j, k):
        dd, gg = z_block(j)
        return W.at[c, :, rows_of(dd, gg, lax.rem(r + RR - k, RR)), :]

    def wx_copy(j, k):
        return copy_to(w_block(j, 0), w_block(j, 0), wx_s.at[j, k - 1], wx_r.at[j, k - 1], r_dev(k))

    def wc_copy(j, k):
        return copy_to(w_block(j, k), w_block(j, k), wc_s.at[j, k], wc_r.at[j, k], partner)

    def wd_rows(yy):
        return wd.at[pl.ds(yy * 2, 2), c]

    def wdy_copy(k):
        return copy_to(wdec_in.at[d], wd_rows(y), wdy_s.at[k - 1], wdy_r.at[k - 1], y_dev(k))

    def wdc_copy(k):
        yy = lax.rem(y + Hy - k, Hy)
        return copy_to(wd_rows(yy), wd_rows(yy), wdc_s.at[k], wdc_r.at[k], partner)

    win_copy = copy_to(win_in.at[d, g], win.at[c], win_s2.at[0], win_r2.at[0], partner)
    own_ids = pltpu.make_async_copy(ids_in.at[d, c], ids.at[part], lsem.at[0])
    own_win = pltpu.make_async_copy(win_in.at[d, g], win.at[c], lsem.at[1])
    own_wd = pltpu.make_async_copy(wdec_in.at[d], wd_rows(y), lsem.at[2])
    own_w = pltpu.make_async_copy(wrec_in.at[d, g], w_block(3, 0), lsem.at[3])

    own_ids.start()
    own_win.start()
    own_w.start()
    own_wd.start()
    for j in range(3):
        ids_copy(j).start()
    win_copy.start()
    for j in range(3):
        wz_copy(j).start()
    for k in range(1, Hy):
        wdy_copy(k).start()

    dW[...] = jnp.zeros_like(dW)
    gwin[...] = jnp.zeros_like(gwin)
    gemb[...] = jnp.zeros_like(gemb)
    lossv[...] = jnp.zeros_like(lossv)
    gb[...] = jnp.zeros_like(gb)
    cg[...] = jnp.zeros_like(cg)
    cell[0] = jnp.zeros_like(cell[0])

    own_w.wait()
    for k in range(1, RR):
        wx_copy(3, k).start()
    wc_copy(3, 0).start()

    own_ids.wait()
    for j in range(3):
        ids_copy(j).wait_recv()

    lane = lax.broadcasted_iota(jnp.int32, (NR, 128), 1)
    vocab = lax.broadcasted_iota(jnp.int32, (NR, VP), 1).astype(F32)

    def id_column(at):
        held = ids[...].reshape(NR, 128)
        return jnp.sum(jnp.where(lane == at, held, 0.0), axis=1, keepdims=True)

    def char_hot(t):
        return jnp.where(vocab == id_column(t), 1.0, 0.0).astype(BF16)

    lang_lane = lax.broadcasted_iota(jnp.int32, (NR, mask_ref.shape[0]), 1).astype(F32)
    lang_hot = jnp.where(lang_lane == id_column(2 * L), 1.0, 0.0).astype(BF16)
    allowed[...] = dot(lang_hot, mask_ref[...])

    @pl.loop(0, L)
    def _(t):
        x[t] = dot(char_hot(t), emb_ref[d]).astype(BF16)

    xp_copy = copy_to(x, xp, xp_s.at[0], xp_r.at[0], partner)
    xp_copy.start()

    own_wd.wait()
    wdc_copy(0).start()
    own_win.wait()
    win_copy.wait_recv()

    def f_copy(t, p):
        slot = lax.rem(t, 2)
        return copy_to(st.at[t, mine], st.at[t, mine], f_s.at[slot, p], f_r.at[slot, p], peer_dev(p))

    def gates(t):
        for cc in range(2):
            si = jax.nn.sigmoid(acc[cc, 0])
            sf = jax.nn.sigmoid(acc[cc, 1])
            tg = jnp.tanh(acc[cc, 2])
            so = jax.nn.sigmoid(acc[cc, 3])
            new = sf * cell[t, cc] + si * tg
            cell[t + 1, cc] = new
            st[t, mine, :, cc * U : (cc + 1) * U] = (so * jnp.tanh(new)).astype(BF16)
            gs[t, 0, cc] = si
            gs[t, 1, cc] = sf
            gs[t, 2, cc] = tg
            gs[t, 3, cc] = so

    def peer_block(p):
        yy = lax.rem(y + Hy - peers[p][1], Hy)
        return yy * 2 + flip(g, peers[p][0])

    for cc in range(2):
        for q in range(4):
            acc[cc, q] = dot(x[0], win[cc, q])
    gates(0)
    for p in range(len(peers)):
        f_copy(0, p).start()

    order = (2, 0, 1)
    for k in range(1, Hy):
        wdy_copy(k).wait_recv()
        wdc_copy(k).start()
    done = [3]
    for j in order:
        wz_copy(j).wait_recv()
        for k in range(1, RR):
            wx_copy(j, k).start()
        wc_copy(j, 0).start()
        last = done[-1]
        for k in range(1, RR):
            wx_copy(last, k).wait_recv()
            wc_copy(last, k).start()
        done.append(j)
    for k in range(1, RR):
        wx_copy(done[-1], k).wait_recv()
        wc_copy(done[-1], k).start()
    for j in range(4):
        for k in range(RR):
            other = W.at[1 - c, :, rows_of(*z_block(j), lax.rem(r + RR - k, RR)), :]
            copy_to(other, other, wc_s.at[j, k], wc_r.at[j, k], partner).wait_recv()
    for k in range(Hy):
        yy = lax.rem(y + Hy - k, Hy)
        other = wd.at[pl.ds(yy * 2, 2), 1 - c]
        copy_to(other, other, wdc_s.at[k], wdc_r.at[k], partner).wait_recv()

    def stp_copy(t):
        return copy_to(st.at[t], stp.at[t], stp_s.at[t], stp_r.at[t], partner)

    def lgp_copy(t):
        return copy_to(lg.at[t], lgp.at[t], lgp_s.at[t], lgp_r.at[t], partner)

    def decode(t):
        stp_copy(t).start()
        logits = bdec_ref[d]
        for m in range(2 * Hy):
            logits = logits + dot(st[t, m], wd[m].reshape(U2, VP))
        masked = jnp.where(allowed[...] > 0.5, logits, masked_value)
        top = jnp.max(masked, axis=1, keepdims=True)
        powers = jnp.exp(masked - top)
        total = jnp.sum(powers, axis=1, keepdims=True)
        hot = vocab == id_column(L + t)
        picked = jnp.sum(jnp.where(hot, logits, 0.0), axis=1, keepdims=True)
        lossv[...] += jnp.broadcast_to(top + jnp.log(total) - picked, (NR, 128))
        grad = ((powers / total - jnp.where(hot, 1.0, 0.0)) * dims.scale).astype(BF16)
        lg[t] = grad
        gb[0:1, :] += jnp.sum(grad.astype(F32), axis=0, keepdims=True)
        lgp_copy(t).start()

    @pl.loop(1, L)
    def _(t):
        before = st.at[t - 1]
        for cc in range(2):
            for q in range(4):
                acc[cc, q] = dot(x[t], win[cc, q]) + dot(before[mine], W[cc, q, chip_rows(mine), :])
        for p in reversed(range(len(peers))):
            f_copy(t - 1, p).wait_recv()
            m = peer_block(p)
            for cc in range(2):
                for q in range(4):
                    acc[cc, q] += dot(before[m], W[cc, q, chip_rows(m), :])
        gates(t)
        for p in range(len(peers)):
            f_copy(t - 1, p).wait_send()
        for p in range(len(peers)):
            f_copy(t, p).start()
        decode(t - 1)

    for j in range(3):
        wz_copy(j).wait_send()
    for j in range(4):
        for k in range(1, RR):
            wx_copy(j, k).wait_send()
        for k in range(RR):
            wc_copy(j, k).wait_send()

    @pl.loop(0, dims.H // U)
    def _(k):
        rows = pl.ds(pl.multiple_of(k * U, U), U)
        for cc in range(2):
            for q in range(4):
                W[cc, q, rows, :] = W[cc, q, rows, :].T

    for p in reversed(range(len(peers))):
        f_copy(L - 1, p).wait_recv()
    decode(L - 1)

    def dec_back(t, cc):
        return dot_nt(lg[t], wd[mine, cc])

    def b_copy(t, p):
        slot = lax.rem(t, 2)
        return copy_to(psend.at[slot, p], precv.at[slot, p], b_s.at[slot, p], b_r.at[slot, p], peer_dev(p))

    def pgx_copy(t):
        slot = lax.rem(t, 2)
        return copy_to(pg.at[slot, 1 - c], pgx.at[slot], pgx_s.at[slot], pgx_r.at[slot], partner)

    def preact_grads(t):
        slot = lax.rem(t, 2)
        for cc in range(2):
            h = dh[cc]
            si, sf, tg, so = gs[t, 0, cc], gs[t, 1, cc], gs[t, 2, cc], gs[t, 3, cc]
            tc = jnp.tanh(cell[t + 1, cc])
            total = cg[cc] + h * so * (1.0 - tc * tc)
            pg[slot, cc, 0] = (total * tg * si * (1.0 - si)).astype(BF16)
            pg[slot, cc, 1] = (total * cell[t, cc] * sf * (1.0 - sf)).astype(BF16)
            pg[slot, cc, 2] = (total * si * (1.0 - tg * tg)).astype(BF16)
            pg[slot, cc, 3] = (h * tc * so * (1.0 - so)).astype(BF16)
            cg[cc] = total * sf
        pgx_copy(t).start()

    def partial(t, m, cc):
        slot = lax.rem(t, 2)
        rows = pl.ds(pl.multiple_of(m * U2 + cc * U, U), U)
        total = None
        for kk in range(2):
            for q in range(4):
                term = dot(pg[slot, kk, q], W[kk, q, rows, :])
                total = term if total is None else total + term
        return total

    def take_state_grad(t):
        slot = lax.rem(t, 2)
        for p in reversed(range(len(peers))):
            b_copy(t, p).wait_recv()
            for cc in range(2):
                dh[cc] += precv[slot, p, :, cc * U : (cc + 1) * U].astype(F32)

    def weight_grads(t, with_rec):
        slot = lax.rem(t, 2)
        pgx_copy(t).wait_recv()
        for q in range(4):
            both = jnp.concatenate([pg[slot, c, q], pgx[slot, q]], axis=0)
            gwin[q] += dot_tn(jnp.concatenate([x[t], xp[t]], axis=0), both)
            if with_rec:
                for m in range(2 * Hy):
                    states = jnp.concatenate([st[t - 1, m], stp[t - 1, m]], axis=0)
                    dW[q, m * U2 : (m + 1) * U2, :] += dot_tn(states, both)
        back = None
        for cc in range(2):
            for q in range(4):
                term = dot_nt(pg[slot, cc, q], win[cc, q])
                back = term if back is None else back + term
        high = back.astype(BF16)
        rest = (back - high.astype(F32)).astype(BF16)
        hot = char_hot(t)
        gemb[...] += dot_tn(hot, high) + dot_tn(hot, rest)

    def gwdr_copy(k):
        return copy_to(gwd_s.at[0], gwd_r.at[k - 1], gwdr_s.at[k - 1], gwdr_r.at[k - 1], r_dev(k))

    def gwdz_copy(j):
        return copy_to(gwd_s.at[1], gwd_out.at[part], gwdz_s.at[j], gwdz_r.at[j], z_dev(j))

    own_gwd = pltpu.make_async_copy(gwd_s.at[1], gwd_out.at[part], lsem.at[0])

    def decoder_grad():
        gwd[...] = jnp.zeros_like(gwd)

        @pl.loop(0, L)
        def _(t):
            columns = pl.ds(pl.multiple_of(c * U, U), U)
            states = jnp.concatenate([st[t, mine, :, columns], stp[t, mine, :, columns]], axis=0)
            gwd[...] += dot_tn(jnp.concatenate([lg[t], lgp[t]], axis=0), states)

        gwd_s[0] = gwd[0:VB].astype(BF16)
        for k in range(1, RR):
            gwdr_copy(k).start()

    def decoder_grad_sum():
        total = gwd[0:VB]
        for k in range(1, RR):
            gwdr_copy(k).wait_recv()
            total = total + gwd_r[k - 1].astype(F32)
        gwd_s[1] = total.astype(BF16)
        for j in range(3):
            gwdz_copy(j).start()
        own_gwd.start()

    for cc in range(2):
        dh[cc] = dec_back(L - 1, cc)

    @pl.loop(0, L)
    def _(t):
        stp_copy(t).wait()
        lgp_copy(t).wait()

    xp_copy.wait()

    @pl.loop(0, L - 1)
    def _(i):
        t = L - 1 - i

        @pl.when(i > 0)
        def _():
            take_state_grad(t + 1)

        @pl.when(i > 1)
        def _():
            pgx_copy(t + 2).wait_send()
            for p in range(len(peers)):
                b_copy(t + 2, p).wait_send()

        preact_grads(t)
        slot = lax.rem(t, 2)
        for p in range(len(peers)):
            m = add_y(peers[p][1]) * 2 + flip(g, peers[p][0])
            for cc in range(2):
                psend[slot, p, :, cc * U : (cc + 1) * U] = partial(t, m, cc).astype(BF16)
            b_copy(t, p).start()
        for cc in range(2):
            dh[cc] = partial(t, mine, cc) + dec_back(t - 1, cc)
        weight_grads(t, True)

        @pl.when(i == 1)
        def _():
            decoder_grad()

        @pl.when(i == 3)
        def _():
            decoder_grad_sum()

    out_steps = ((1, 0), (1, 1), (0, 1), (0, 0))

    def out_rows(i, step):
        dd, gg = flip(d, out_steps[i][0]), flip(g, out_steps[i][1])
        return rows_of(dd, gg, add_r(step))

    def b_out(i, k):
        return copy_to(W.at[0, :, out_rows(i, k), :], recvB.at[k - 1, i], B_s.at[k - 1, i], B_r.at[k - 1, i], r_dev(k))

    def c_out(i):
        return copy_to(W.at[1, :, out_rows(i, 0), :], grec_out.at[part], C_s.at[i], C_r.at[i], z_dev(i))

    own_out = pltpu.make_async_copy(W.at[1, :, out_rows(3, 0), :], grec_out.at[part], lsem.at[1])

    for i in range(4):
        for k in range(1, RR):
            for q in range(4):
                W[0, q, out_rows(i, k), :] = dW[q, out_rows(i, k), :].astype(BF16)
            b_out(i, k).start()

    take_state_grad(1)
    pgx_copy(2).wait_send()
    preact_grads(0)
    weight_grads(0, False)

    def gwr_copy(k):
        return copy_to(gwin_s.at[0], gwin_r.at[k - 1], gwr_s.at[k - 1], gwr_r.at[k - 1], r_dev(k))

    def gwz_copy(j):
        return copy_to(gwin_s.at[1], gwin_out.at[part], gwz_s.at[j], gwz_r.at[j], z_dev(j))

    own_gwin = pltpu.make_async_copy(gwin_s.at[1], gwin_out.at[part], lsem.at[2])

    gwin_s[0] = gwin[:, 0:EW, :].astype(BF16)
    for k in range(1, RR):
        gwr_copy(k).start()

    once = jnp.where(mine == 0, 1.0, 0.0).astype(F32)
    esend[0, 0:V8] = gemb[0:V8]
    esend[0, V8:VS] = jnp.zeros((8, 128), F32)
    for k in range(VP // 128):
        esend[0, V8 + k : V8 + k + 1] = gb[0:1, k * 128 : (k + 1) * 128] * once
    at = V8 + VP // 128
    esend[0, at : at + 1] = jnp.sum(lossv[...], axis=0, keepdims=True) * (once * dims.scale)

    stages = [[partner], [r_dev(k) for k in range(1, RR)], [y_dev(k) for k in range(1, Hy)], [dev(d, 1 - g, r, y, c)]]
    first = [sum(len(s) for s in stages[:n]) for n in range(len(stages) + 1)]

    def e_copy(n, k):
        at = first[n] + k
        return copy_to(esend.at[n], erecv.at[at], e_s.at[at], e_r.at[at], stages[n][k])

    def e_start(n):
        for k in range(len(stages[n])):
            e_copy(n, k).start()

    def e_take(n):
        total = esend[n]
        for k in range(len(stages[n])):
            e_copy(n, k).wait_recv()
            total = total + erecv[first[n] + k]
        esend[n + 1] = total

    e_last = copy_to(esend.at[4], small_out.at[d], e_s.at[first[4]], e_r.at[first[4]], dev(1 - d, g, r, y, c))
    own_small = pltpu.make_async_copy(esend.at[4], small_out.at[d], lsem.at[3])

    def send_rec(i):
        for k in range(1, RR):
            b_out(i, k).wait_recv()
        for q in range(4):
            total = dW[q, out_rows(i, 0), :]
            for k in range(1, RR):
                total = total + recvB[k - 1, i, q].astype(F32)
            W[1, q, out_rows(i, 0), :] = total.astype(BF16)
        if i < 3:
            c_out(i).start()
        else:
            own_out.start()

    e_start(0)
    send_rec(0)
    e_take(0)
    e_start(1)
    send_rec(1)
    total = gwin[:, 0:EW, :]
    for k in range(1, RR):
        gwr_copy(k).wait_recv()
        total = total + gwin_r[k - 1].astype(F32)
    gwin_s[1] = total.astype(BF16)
    for j in range(3):
        gwz_copy(j).start()
    own_gwin.start()
    e_take(1)
    e_start(2)
    send_rec(2)
    e_take(2)
    e_start(3)
    send_rec(3)
    e_take(3)
    e_last.start()
    own_small.start()

    for j in range(3):
        ids_copy(j).wait_send()
    win_copy.wait_send()
    for k in range(1, Hy):
        wdy_copy(k).wait_send()
    for k in range(Hy):
        wdc_copy(k).wait_send()
    for p in range(len(peers)):
        f_copy(L - 1, p).wait_send()
    for t in (2, 1):
        for p in range(len(peers)):
            b_copy(t, p).wait_send()
    pgx_copy(1).wait_send()
    pgx_copy(0).wait_send()
    for k in range(1, RR):
        gwdr_copy(k).wait_send()
        gwr_copy(k).wait_send()
        for i in range(4):
            b_out(i, k).wait_send()
    for n in range(4):
        for k in range(len(stages[n])):
            e_copy(n, k).wait_send()
    for j in range(3):
        gwdz_copy(j).wait()
        gwz_copy(j).wait()
        c_out(j).wait()
    e_last.wait()
    own_gwd.wait()
    own_gwin.wait()
    own_out.wait()
    own_small.wait()


def call_kernel(dims, ids, win, wrec, wdec, emb, bdec, mask):
    R, RR, Hy, U, U2, NR, L, VP = dims.R, dims.RR, dims.Hy, dims.U, dims.U2, dims.NR, dims.L, dims.VP
    KR, EW, EP, VB, VS, H = dims.KR, dims.EW, dims.EP, dims.VB, dims.VS, dims.H
    chips, peers = 2 * Hy, len(dims.peers)
    vmem, sem = pltpu.VMEM, pltpu.SemaphoreType.DMA
    apart = pl.BlockSpec(memory_space=pl.ANY)
    inside = pl.BlockSpec(memory_space=pltpu.VMEM)
    groups = max(RR - 1, 1)
    along = max(Hy - 1, 1)
    stages = 1 + (RR - 1) + (Hy - 1) + 1
    scratch = [
        vmem((4, dims.RL // 2, 128), F32),
        vmem((2, 4, EP, U), BF16),
        vmem((2, 4, H, U), BF16),
        vmem((chips, 2, U, VP), BF16),
        vmem((L, NR, EP), BF16),
        vmem((L, NR, EP), BF16),
        vmem((NR, VP), F32),
        vmem((2, 4, NR, U), F32),
        vmem((L, chips, NR, U2), BF16),
        vmem((L, chips, NR, U2), BF16),
        vmem((L, 4, 2, NR, U), F32),
        vmem((L + 1, 2, NR, U), F32),
        vmem((L, NR, VP), BF16),
        vmem((L, NR, VP), BF16),
        vmem((NR, 128), F32),
        vmem((8, VP), F32),
        vmem((2, NR, U), F32),
        vmem((2, NR, U), F32),
        vmem((2, 2, 4, NR, U), BF16),
        vmem((2, 4, NR, U), BF16),
        vmem((2, peers, NR, U2), BF16),
        vmem((2, peers, NR, U2), BF16),
        vmem((4, H, U), F32),
        vmem((4, EP, U), F32),
        vmem((VP, EP), F32),
        vmem((VP, U), F32),
        vmem((2, VB, U), BF16),
        vmem((groups, VB, U), BF16),
        vmem((2, 4, EW, U), BF16),
        vmem((groups, 4, EW, U), BF16),
        vmem((groups, 4, 4, KR, U), BF16),
        vmem((5, VS, 128), F32),
        vmem((stages, VS, 128), F32),
        sem((4,)),
        sem((3,)), sem((3,)),
        sem((1,)), sem((1,)),
        sem((along,)), sem((along,)),
        sem((Hy,)), sem((Hy,)),
        sem((3,)), sem((3,)),
        sem((4, groups)), sem((4, groups)),
        sem((4, RR)), sem((4, RR)),
        sem((1,)), sem((1,)),
        sem((2, peers)), sem((2, peers)),
        sem((L,)), sem((L,)),
        sem((L,)), sem((L,)),
        sem((2, peers)), sem((2, peers)),
        sem((2,)), sem((2,)),
        sem((groups,)), sem((groups,)),
        sem((3,)), sem((3,)),
        sem((groups,)), sem((groups,)),
        sem((3,)), sem((3,)),
        sem((groups, 4)), sem((groups, 4)),
        sem((3,)), sem((3,)),
        sem((stages + 1,)), sem((stages + 1,)),
    ]
    rows = NR * L
    flops = 2 * rows * (3 * H * 8 * U + 3 * H * VP)
    return pl.pallas_call(
        functools.partial(kernel, dims),
        out_shape=(
            jax.ShapeDtypeStruct((4, 4, KR, U), BF16),
            jax.ShapeDtypeStruct((4, 4, EW, U), BF16),
            jax.ShapeDtypeStruct((4, VB, U), BF16),
            jax.ShapeDtypeStruct((2, VS, 128), F32),
        ),
        in_specs=[apart, apart, apart, apart, inside, inside, inside],
        out_specs=(apart, apart, apart, apart),
        scratch_shapes=scratch,
        cost_estimate=pl.CostEstimate(flops=flops, bytes_accessed=8 << 20, transcendentals=rows * U2 * 8),
        compiler_params=pltpu.CompilerParams(
            collective_id=0, has_side_effects=True, vmem_limit_bytes=62 << 20
        ),
        name="train_step",
    )(ids, win, wrec, wdec, emb, bdec, mask)


def local(
    char_ids, lang_ids, vocab_masks, targets, embedding, w_in, w_rec, b_in, b_rec, w_dec, b_dec
):
    R, hid = lax.axis_size("rows"), lax.axis_size("hid")
    RL, L = char_ids.shape
    E, units = w_in.shape[1], w_in.shape[3]
    V = embedding.shape[1]
    KR = w_rec.shape[1]
    U = units // 2
    dims = Dims(
        R=R, RR=R // 4, Hy=hid // 2, H=units * hid, KR=KR, U=U, RL=RL, L=L, V=V, E=E,
        LANGS=vocab_masks.shape[0], scale=1.0 / (RL * R * L),
    )
    VP, EP = dims.VP, dims.EP

    lang = lang_ids[:, None]
    first = jnp.concatenate([char_ids, targets[0], lang], axis=1)
    second = jnp.concatenate([char_ids[:, ::-1], targets[1][:, ::-1], lang], axis=1)
    ids = jnp.stack([first, second]).astype(F32)
    ids = jnp.pad(ids, ((0, 0), (0, 0), (0, 128 - ids.shape[2]))).reshape(2, 2, RL // 2, 128)
    win = jnp.concatenate([w_in, b_in[:, None], b_rec[:, None]], axis=1)
    win = jnp.pad(win, ((0, 0), (0, EP - E - 2), (0, 0), (0, 0)))
    win = win.reshape(2, EP, 4, 2, U).transpose(0, 3, 2, 1, 4)
    wrec = w_rec.reshape(2, KR, 4, 2, U).transpose(0, 3, 2, 1, 4)
    wdec = jnp.pad(w_dec, ((0, 0), (0, 0), (0, VP - V))).reshape(2, 2, U, VP)
    emb = jnp.concatenate([embedding, jnp.ones((2, V, 2), BF16)], axis=2)
    emb = jnp.pad(emb, ((0, 0), (0, VP - V), (0, EP - E - 2)))
    bdec = jnp.pad(b_dec.astype(F32), ((0, 0), (0, VP - V)))[:, None, :]
    lang_rows = ceil_to(dims.LANGS, 16)
    mask = jnp.pad(vocab_masks.astype(BF16), ((0, lang_rows - dims.LANGS), (0, VP - V)))

    grec, gwin, gwd, small = call_kernel(dims, ids, win, wrec, wdec, emb, bdec, mask)

    grad_w_rec = grec.reshape(2, 2, 4, KR, U).transpose(0, 3, 2, 1, 4).reshape(2, KR, 4, units).astype(F32)
    gwin = gwin.reshape(2, 2, 4, dims.EW, U)
    grad_w_in = gwin[:, :, :, :E].transpose(0, 3, 2, 1, 4).reshape(2, E, 4, units).astype(F32)
    grad_bias = gwin[:, :, :, E].transpose(0, 2, 1, 3).reshape(2, 4, units).astype(F32)
    gwd = gwd.reshape(2, 2, dims.VB, U)[:, :, :V]
    grad_w_dec = gwd.transpose(0, 1, 3, 2).reshape(2, units, V).astype(F32)
    V8 = dims.V8
    grad_embedding = small[:, :V, :E]
    grad_b_dec = small[:, V8 : V8 + VP // 128].reshape(2, VP)[:, :V]
    total_loss = jnp.sum(small[:, V8 + VP // 128, 0])
    return (
        total_loss,
        grad_embedding,
        grad_w_in,
        grad_w_rec,
        grad_bias,
        grad_bias,
        grad_w_dec,
        grad_b_dec,
    )


def solution(mesh):
    placed = (
        P("rows", None),
        P("rows"),
        P(),
        P(None, "rows", None),
        P(),
        P(None, None, None, "hid"),
        P(None, "rows", None, "hid"),
        P(None, None, "hid"),
        P(None, None, "hid"),
        P(None, "hid", None),
        P(),
    )
    return jax.shard_map(
        local,
        mesh=mesh,
        in_specs=placed,
        out_specs=(
            P(),
            P(),
            P(None, None, None, "hid"),
            P(None, "rows", None, "hid"),
            P(None, None, "hid"),
            P(None, None, "hid"),
            P(None, "hid", None),
            P(),
        ),
        check_vma=False,
    )
```

```python
import functools
from typing import NamedTuple

import jax
import jax.numpy as jnp
from jax import lax
from jax.experimental import pallas as pl
from jax.experimental.pallas import tpu as pltpu
from jax.sharding import PartitionSpec as P

MESH = pl.DeviceIdType.MESH
F32 = jnp.float32
BF16 = jnp.bfloat16
masked_value = -1000000000.0
AHEAD = 4
BATCHES = 2


def ceil_to(n, m):
    return (n + m - 1) // m * m


class Dims(NamedTuple):
    R: int
    RR: int
    Hy: int
    H: int
    KR: int
    U: int
    RL: int
    L: int
    V: int
    E: int
    LANGS: int
    scale: float

    @property
    def U2(self):
        return 2 * self.U

    @property
    def NR(self):
        return 2 * self.RL

    @property
    def VP(self):
        return ceil_to(self.V, 128)

    @property
    def RB(self):
        return self.NR // BATCHES

    @property
    def QN(self):
        return 1 if self.RR <= 2 else 4

    @property
    def N_IN(self):
        return ceil_to(4 * self.EW, 16 * self.RR)

    @property
    def N_DEC(self):
        return ceil_to(self.V, 16 * self.RR)

    @property
    def P8(self):
        return ceil_to(self.L, 8)

    @property
    def EP(self):
        return ceil_to(self.E + 2, 128)

    @property
    def EW(self):
        return ceil_to(self.E + 2, 16)

    @property
    def V8(self):
        return ceil_to(self.V, 8)

    @property
    def VS(self):
        return ceil_to(self.V8 + 8, 16)

    @property
    def peers(self):
        far = [(1, k) for k in range(1, self.Hy)]
        beside = [(0, k) for k in range(1, self.Hy)]
        return far + beside + [(1, 0)]


Z_STEPS = ((1, 0), (1, 1), (0, 1))


def dot(a, b):
    return jnp.dot(a, b, preferred_element_type=F32)


def dot_nt(a, b):
    return lax.dot_general(a, b, (((1,), (1,)), ((), ())), preferred_element_type=F32)


def dot_tn(a, b):
    return lax.dot_general(a, b, (((0,), (0,)), ((), ())), preferred_element_type=F32)


def flip(bit, step):
    return 1 - bit if step else bit


def kernel(
    dims,
    chars_ref, targets_ref, lang_ref, bias_ref, win_in, wrec_in, wdec_in, emb_ref, bdec_ref, mask_ref,
    grec_out, gwin_out, gwd_out, small_out,
    idsrc, idsall, idtmp, ids, bias, win, W, wd, x, xp, allowed, acc, st, stp, gs, cell, lg, lgp, lossv, gb,
    dh, cg, pg, pgx, psend, precv, dW, gwin, gemb, gwd, gwd_s, gwd_r, gwd_all, gwin_s, gwin_r, gwin_all,
    recvB, epart, esend, erecv, eall,
    lsem, ids_s, ids_r, win_s2, win_r2, bias_s, bias_r, wdy_s, wdy_r, wdc_s, wdc_r, wz_s, wz_r, wx_s, wx_r, wc_s, wc_r,
    xp_s, xp_r, f_s, f_r, stp_s, stp_r, lgp_s, lgp_r, b_s, b_r, pgx_s, pgx_r,
    gwd_sems, gwin_sems, B_s, B_r, C_s, C_r, e_s, e_r,
):
    R, RR, Hy, U, U2, NR, L, VP = dims.R, dims.RR, dims.Hy, dims.U, dims.U2, dims.NR, dims.L, dims.VP
    KR, EW, V8, VS, RL, RB, QN = dims.KR, dims.EW, dims.V8, dims.VS, dims.RL, dims.RB, dims.QN
    peers = dims.peers
    pieces = 4 // QN
    rho, hid = lax.axis_index("rows"), lax.axis_index("hid")
    d, g, r = rho // (R // 2), lax.rem(rho // RR, 2), lax.rem(rho, RR)
    y, c = hid // 2, lax.rem(hid, 2)
    mine = y * 2 + g
    part = d * 2 + g

    def dev(dd, gg, rr, yy, cc):
        return (dd * (R // 2) + gg * RR + rr, yy * 2 + cc)

    def copy_to(src, dst, send, recv, device):
        return pltpu.make_async_remote_copy(
            src_ref=src, dst_ref=dst, send_sem=send, recv_sem=recv, device_id=device, device_id_type=MESH
        )

    def add_r(step):
        return lax.rem(r + step, RR)

    def add_y(step):
        return lax.rem(y + step, Hy)

    def rows_of(dd, gg, rr):
        index = dd * (R // 2) + gg * RR + rr
        per = U // KR
        block = index // per
        hid_of, g_of = block // 2, lax.rem(block, 2)
        chip = (hid_of // 2) * 2 + g_of
        row = chip * U2 + lax.rem(hid_of, 2) * U + lax.rem(index, per) * KR
        return pl.ds(pl.multiple_of(row, KR), KR)

    def chip_rows(m):
        return pl.ds(pl.multiple_of(m * U2, U2), U2)

    partner = dev(d, g, r, y, 1 - c)
    half = pl.ds(pl.multiple_of(g * U, U), U)

    def z_dev(j):
        return dev(flip(d, Z_STEPS[j][0]), flip(g, Z_STEPS[j][1]), r, y, c)

    def r_dev(step):
        return dev(d, g, add_r(step), y, c)

    def y_dev(step):
        return dev(d, g, r, add_y(step), c)

    def peer_dev(p):
        return dev(d, flip(g, peers[p][0]), r, add_y(peers[p][1]), c)

    barrier = pltpu.get_barrier_semaphore()
    greeted = [z_dev(j) for j in range(3)] + [r_dev(k) for k in range(1, RR)] + [partner]
    greeted += [peer_dev(p) for p in range(len(peers)) if peers[p] != (1, 0)]
    for device in greeted:
        pl.semaphore_signal(barrier, inc=1, device_id=device, device_id_type=MESH)
    pl.semaphore_wait(barrier, len(greeted))

    def ids_copy(j):
        return copy_to(idsrc.at[flip(d, Z_STEPS[j][0])], idsall.at[part], ids_s.at[j], ids_r.at[j], z_dev(j))

    def gates_of(n):
        return pl.ds(n * QN, QN)

    def wz_copy(j, n):
        columns = pl.ds(pl.multiple_of(flip(g, Z_STEPS[j][1]) * U, U), U)
        there = wrec_in.at[flip(d, Z_STEPS[j][0]), gates_of(n), :, columns]
        return copy_to(there, W.at[c, gates_of(n), rows_of(d, g, r), :], wz_s.at[j, n], wz_r.at[j, n], z_dev(j))

    def z_block(j):
        steps = Z_STEPS[j] if j < 3 else (0, 0)
        return flip(d, steps[0]), flip(g, steps[1])

    def w_block(core, j, k, n):
        dd, gg = z_block(j)
        return W.at[core, gates_of(n), rows_of(dd, gg, lax.rem(r + RR - k, RR)), :]

    def wx_copy(j, k, n):
        block = w_block(c, j, 0, n)
        return copy_to(block, block, wx_s.at[j, k - 1, n], wx_r.at[j, k - 1, n], r_dev(k))

    def wc_copy(j, k, n, core):
        block = w_block(core, j, k, n)
        return copy_to(block, block, wc_s.at[j, k, n], wc_r.at[j, k, n], partner)

    def wd_rows(yy):
        return wd.at[pl.ds(yy * 2, 2), c]

    def wdy_copy(k):
        return copy_to(wdec_in.at[d], wd_rows(y), wdy_s.at[k - 1], wdy_r.at[k - 1], y_dev(k))

    def wdc_copy(k):
        yy = lax.rem(y + Hy - k, Hy)
        return copy_to(wd_rows(yy), wd_rows(yy), wdc_s.at[k], wdc_r.at[k], partner)

    win_copy = copy_to(win_in.at[d, :, :, half], win.at[c], win_s2.at[0], win_r2.at[0], partner)
    bias_copy = copy_to(bias.at[c], bias.at[c], bias_s.at[0], bias_r.at[0], partner)
    own_win = pltpu.make_async_copy(win_in.at[d, :, :, half], win.at[c], lsem.at[1])
    own_wd = pltpu.make_async_copy(wdec_in.at[d], wd_rows(y), lsem.at[2])
    own_w = pltpu.make_async_copy(
        wrec_in.at[d, :, :, half], W.at[c, :, rows_of(d, g, r), :], lsem.at[3]
    )

    own_w.start()
    for n in range(pieces):
        for j in range(3):
            wz_copy(j, n).start()
    own_win.start()
    win_copy.start()
    for k in range(1, Hy):
        wdy_copy(k).start()
    own_wd.start()

    P8 = dims.P8
    idsrc[...] = jnp.zeros_like(idsrc)
    for dd in range(2):
        idsrc[dd, 0:L, 0:RL] = chars_ref[...].astype(F32)
        idsrc[dd, P8 : P8 + L, 0:RL] = targets_ref[dd].astype(F32)
        idsrc[dd, 2 * P8 : 2 * P8 + 8, 0:RL] = jnp.broadcast_to(lang_ref[...].astype(F32), (8, RL))
    for j in range(3):
        ids_copy(j).start()
    bias[c, 0:4] = bias_ref[d, :, half]
    bias_copy.start()
    idsall[part] = idsrc[d]

    own_w.wait()
    for n in range(pieces):
        for k in range(1, RR):
            wx_copy(3, k, n).start()
        wc_copy(3, 0, n, c).start()

    dW[...] = jnp.zeros_like(dW)
    gwin[...] = jnp.zeros_like(gwin)
    gemb[...] = jnp.zeros_like(gemb)
    lossv[...] = jnp.zeros_like(lossv)
    gb[...] = jnp.zeros_like(gb)
    cg[...] = jnp.zeros_like(cg)
    cell[0] = jnp.zeros_like(cell[0])
    idtmp[...] = jnp.zeros_like(idtmp)

    for j in range(3):
        ids_copy(j).wait_recv()
    for n in range(4):
        idtmp[:, 0 : idsall.shape[1]] = idsall[n].T
        ids[n] = idtmp[pl.ds(pl.multiple_of(c * (RL // 2), RL // 2), RL // 2), :]

    lane = lax.broadcasted_iota(jnp.int32, (NR, 128), 1)
    vocab = lax.broadcasted_iota(jnp.int32, (NR, VP), 1).astype(F32)

    def id_column(at):
        held = ids[...].reshape(NR, 128)
        return jnp.sum(jnp.where(lane == at, held, 0.0), axis=1, keepdims=True)

    def place(t):
        return t + d * (L - 1 - 2 * t)

    def char_hot(t):
        return jnp.where(vocab == id_column(place(t)), 1.0, 0.0).astype(BF16)

    lang_lane = lax.broadcasted_iota(jnp.int32, (NR, mask_ref.shape[0]), 1).astype(F32)
    lang_hot = jnp.where(lang_lane == id_column(2 * P8), 1.0, 0.0).astype(BF16)
    allowed[...] = dot(lang_hot, mask_ref[...])

    @pl.loop(0, L)
    def _(t):
        x[t] = dot(char_hot(t), emb_ref[d]).astype(BF16)

    xp_copy = copy_to(x, xp, xp_s.at[0], xp_r.at[0], partner)
    xp_copy.start()

    own_wd.wait()
    wdc_copy(0).start()
    own_win.wait()
    win_copy.wait_recv()
    bias_copy.wait_recv()

    def part_rows(b):
        return pl.ds(b * RB, RB)

    def f_copy(t, b, p):
        slot = lax.rem(t, 2)
        block = st.at[t, mine, part_rows(b), :]
        return copy_to(block, block, f_s.at[slot, b, p], f_r.at[slot, b, p], peer_dev(p))

    def gates(t, b):
        rows = part_rows(b)
        for cc in range(2):
            si = jax.nn.sigmoid(acc[cc, 0])
            sf = jax.nn.sigmoid(acc[cc, 1])
            tg = jnp.tanh(acc[cc, 2])
            so = jax.nn.sigmoid(acc[cc, 3])
            new = sf * cell[t, cc, rows] + si * tg
            cell[t + 1, cc, rows] = new
            st[t, mine, rows, cc * U : (cc + 1) * U] = (so * jnp.tanh(new)).astype(BF16)
            gs[t, 0, cc, rows] = si
            gs[t, 1, cc, rows] = sf
            gs[t, 2, cc, rows] = tg
            gs[t, 3, cc, rows] = so

    def peer_block(p):
        yy = lax.rem(y + Hy - peers[p][1], Hy)
        return yy * 2 + flip(g, peers[p][0])

    for b in range(BATCHES):
        for cc in range(2):
            for q in range(4):
                acc[cc, q] = dot(x[0, part_rows(b)], win[cc, q]) + bias[cc, q : q + 1]
        gates(0, b)
        for p in range(len(peers)):
            f_copy(0, b, p).start()

    for k in range(1, Hy):
        wdy_copy(k).wait_recv()
        wdc_copy(k).start()
    from_z = [(j, n) for n in range(pieces) for j in (2, 0, 1)]
    from_x = [(3, n) for n in range(pieces)] + from_z
    for at in range(len(from_x)):
        if at < len(from_z):
            j, n = from_z[at]
            wz_copy(j, n).wait_recv()
            for k in range(1, RR):
                wx_copy(j, k, n).start()
            wc_copy(j, 0, n, c).start()
        j, n = from_x[at]
        for k in range(1, RR):
            wx_copy(j, k, n).wait_recv()
            wc_copy(j, k, n, c).start()
    for j, n in from_x:
        for k in range(RR):
            wc_copy(j, k, n, 1 - c).wait_recv()
    for k in range(Hy):
        yy = lax.rem(y + Hy - k, Hy)
        other = wd.at[pl.ds(yy * 2, 2), 1 - c]
        copy_to(other, other, wdc_s.at[k], wdc_r.at[k], partner).wait_recv()

    def stp_copy(t):
        return copy_to(st.at[t], stp.at[t], stp_s.at[t], stp_r.at[t], partner)

    def lgp_copy(t):
        return copy_to(lg.at[t], lgp.at[t], lgp_s.at[t], lgp_r.at[t], partner)

    def decode(t):
        stp_copy(t).start()
        logits = bdec_ref[d]
        for m in range(2 * Hy):
            logits = logits + dot(st[t, m], wd[m].reshape(U2, VP))
        masked = jnp.where(allowed[...] > 0.5, logits, masked_value)
        top = jnp.max(masked, axis=1, keepdims=True)
        powers = jnp.exp(masked - top)
        total = jnp.sum(powers, axis=1, keepdims=True)
        hot = vocab == id_column(P8 + place(t))
        picked = jnp.sum(jnp.where(hot, logits, 0.0), axis=1, keepdims=True)
        lossv[...] += jnp.broadcast_to(top + jnp.log(total) - picked, (NR, 128))
        grad = ((powers / total - jnp.where(hot, 1.0, 0.0)) * dims.scale).astype(BF16)
        lg[t] = grad
        gb[0:1, :] += jnp.sum(grad.astype(F32), axis=0, keepdims=True)
        lgp_copy(t).start()

    @pl.loop(1, L)
    def _(t):
        for b in range(BATCHES):
            rows = part_rows(b)
            for cc in range(2):
                for q in range(4):
                    start = dot(x[t, rows], win[cc, q]) + bias[cc, q : q + 1]
                    acc[cc, q] = start + dot(st[t - 1, mine, rows], W[cc, q, chip_rows(mine), :])
            for p in reversed(range(len(peers))):
                f_copy(t - 1, b, p).wait_recv()
                m = peer_block(p)
                for cc in range(2):
                    for q in range(4):
                        acc[cc, q] += dot(st[t - 1, m, rows], W[cc, q, chip_rows(m), :])
            gates(t, b)
            for p in range(len(peers)):
                f_copy(t - 1, b, p).wait_send()
            for p in range(len(peers)):
                f_copy(t, b, p).start()
        decode(t - 1)

    for j, n in from_x:
        if j < 3:
            wz_copy(j, n).wait_send()
        for k in range(1, RR):
            wx_copy(j, k, n).wait_send()
        for k in range(RR):
            wc_copy(j, k, n, c).wait_send()

    @pl.loop(0, dims.H // U)
    def _(k):
        rows = pl.ds(pl.multiple_of(k * U, U), U)
        for cc in range(2):
            for q in range(4):
                W[cc, q, rows, :] = W[cc, q, rows, :].T

    for b in range(BATCHES):
        for p in reversed(range(len(peers))):
            f_copy(L - 1, b, p).wait_recv()
    decode(L - 1)

    def dec_back(t, cc):
        return dot_nt(lg[t], wd[mine, cc])

    def b_copy(t, b, p):
        slot = lax.rem(t, 2)
        there = precv.at[slot, p, part_rows(b), :]
        return copy_to(
            psend.at[slot, p, part_rows(b), :], there, b_s.at[slot, b, p], b_r.at[slot, b, p], peer_dev(p)
        )

    def pgx_copy(t):
        slot = lax.rem(t, 2)
        return copy_to(pg.at[slot, 1 - c], pgx.at[slot], pgx_s.at[slot], pgx_r.at[slot], partner)

    def preact_grads(t, b):
        slot = lax.rem(t, 2)
        rows = part_rows(b)
        for cc in range(2):
            h = dh[cc, rows]
            si, sf, tg, so = (gs[t, q, cc, rows] for q in range(4))
            tc = jnp.tanh(cell[t + 1, cc, rows])
            total = cg[cc, rows] + h * so * (1.0 - tc * tc)
            pg[slot, cc, 0, rows] = (total * tg * si * (1.0 - si)).astype(BF16)
            pg[slot, cc, 1, rows] = (total * cell[t, cc, rows] * sf * (1.0 - sf)).astype(BF16)
            pg[slot, cc, 2, rows] = (total * si * (1.0 - tg * tg)).astype(BF16)
            pg[slot, cc, 3, rows] = (h * tc * so * (1.0 - so)).astype(BF16)
            cg[cc, rows] = total * sf

    def partial(t, b, m, cc):
        slot = lax.rem(t, 2)
        rows = pl.ds(pl.multiple_of(m * U2 + cc * U, U), U)
        total = None
        for kk in range(2):
            for q in range(4):
                term = dot(pg[slot, kk, q, part_rows(b)], W[kk, q, rows, :])
                total = term if total is None else total + term
        return total

    def take_state_grad(t, b):
        slot = lax.rem(t, 2)
        rows = part_rows(b)
        for p in reversed(range(len(peers))):
            b_copy(t, b, p).wait_recv()
            for cc in range(2):
                dh[cc, rows] += precv[slot, p, rows, cc * U : (cc + 1) * U].astype(F32)

    def weight_grads(t, with_rec):
        slot = lax.rem(t, 2)
        pgx_copy(t).wait_recv()
        for q in range(4):
            both = jnp.concatenate([pg[slot, c, q], pgx[slot, q]], axis=0)
            gwin[q] += dot_tn(jnp.concatenate([x[t], xp[t]], axis=0), both)
            if with_rec:
                for m in range(2 * Hy):
                    states = jnp.concatenate([st[t - 1, m], stp[t - 1, m]], axis=0)
                    dW[q, m * U2 : (m + 1) * U2, :] += dot_tn(states, both)
        back = None
        for cc in range(2):
            for q in range(4):
                term = dot_nt(pg[slot, cc, q], win[cc, q])
                back = term if back is None else back + term
        high = back.astype(BF16)
        rest = (back - high.astype(F32)).astype(BF16)
        hot = char_hot(t)
        gemb[...] += dot_tn(hot, high) + dot_tn(hot, rest)

    class SmallSum:
        def __init__(self, send, recv, whole, out, sems, own_sem):
            self.send, self.recv, self.whole, self.out, self.sems, self.own = send, recv, whole, out, sems, own_sem
            self.share = whole.shape[1] // RR

        def rows(self, rr):
            return pl.ds(pl.multiple_of(rr * self.share, 16), self.share)

        def pair(self, at):
            return self.sems.at[0, at], self.sems.at[1, at]

        def first(self, k):
            return copy_to(self.send.at[self.rows(add_r(k)), :], self.recv.at[k - 1], *self.pair(k - 1), r_dev(k))

        def block(self, dd, gg):
            return self.whole.at[dd, self.rows(r), pl.ds(pl.multiple_of(gg * U, U), U)]

        def along(self, j):
            block = self.block(1 - d, g) if j == 1 else self.block(d, g)
            return copy_to(block, block, *self.pair(RR - 1 + j), z_dev(0 if j == 0 else 2))

        def last(self, k):
            block = self.whole.at[:, self.rows(r), :]
            return copy_to(block, block, *self.pair(RR + 2 + k - 1), r_dev(k))

        def to_out(self):
            return pltpu.make_async_copy(self.whole, self.out, self.own)

        def start(self):
            for k in range(1, RR):
                self.first(k).start()

        def add(self, value):
            for k in range(1, RR):
                self.first(k).wait_recv()
                value = value + self.recv[k - 1].astype(F32)
            self.whole[d, self.rows(r), half] = value.astype(BF16)
            self.along(0).start()
            self.along(2).start()

        def relay(self):
            self.along(0).wait_recv()
            self.along(1).start()

        def spread(self):
            self.along(2).wait_recv()
            self.along(1).wait_recv()
            for k in range(1, RR):
                self.last(k).start()

        def finish(self):
            for k in range(1, RR):
                self.last(k).wait_recv()
            self.to_out().start()

        def drain(self):
            for k in range(1, RR):
                self.first(k).wait_send()
                self.last(k).wait_send()
            for j in range(3):
                self.along(j).wait_send()
            self.to_out().wait()

    dec_sum = SmallSum(gwd_s, gwd_r, gwd_all, gwd_out, gwd_sems, lsem.at[0])
    in_sum = SmallSum(gwin_s, gwin_r, gwin_all, gwin_out, gwin_sems, lsem.at[1])

    def decoder_grad():
        gwd[...] = jnp.zeros_like(gwd)

        @pl.loop(0, L)
        def _(t):
            columns = pl.ds(pl.multiple_of(c * U, U), U)
            states = jnp.concatenate([st[t, mine, :, columns], stp[t, mine, :, columns]], axis=0)
            gwd[...] += dot_tn(jnp.concatenate([lg[t], lgp[t]], axis=0), states)

        gwd_s[...] = gwd[0 : dims.N_DEC].astype(BF16)
        dec_sum.start()

    for cc in range(2):
        dh[cc] = dec_back(L - 1, cc)

    @pl.loop(0, L)
    def _(t):
        stp_copy(t).wait()
        lgp_copy(t).wait()

    xp_copy.wait()

    @pl.loop(0, L - 1)
    def _(i):
        t = L - 1 - i
        slot = lax.rem(t, 2)

        @pl.when(i > 1)
        def _():
            pgx_copy(t + 2).wait_send()

        for b in range(BATCHES):
            rows = part_rows(b)

            @pl.when(i > 0)
            def _():
                take_state_grad(t + 1, b)

            @pl.when(i > 1)
            def _():
                for p in range(len(peers)):
                    b_copy(t + 2, b, p).wait_send()

            preact_grads(t, b)
            for p in range(len(peers)):
                m = add_y(peers[p][1]) * 2 + flip(g, peers[p][0])
                for cc in range(2):
                    psend[slot, p, rows, cc * U : (cc + 1) * U] = partial(t, b, m, cc).astype(BF16)
                b_copy(t, b, p).start()
            for cc in range(2):
                dh[cc, rows] = partial(t, b, mine, cc)
        pgx_copy(t).start()
        for cc in range(2):
            dh[cc] += dec_back(t - 1, cc)
        weight_grads(t, True)

        @pl.when(i == 0)
        def _():
            decoder_grad()

        @pl.when(i == 1)
        def _():
            dec_sum.add(gwd[dec_sum.rows(r), :])

        @pl.when(i == 2)
        def _():
            dec_sum.relay()

        @pl.when(i == 3)
        def _():
            dec_sum.spread()

        @pl.when(i == 4)
        def _():
            dec_sum.finish()

    out_steps = ((1, 0), (1, 1), (0, 1), (0, 0))

    def out_rows(i, step):
        dd, gg = flip(d, out_steps[i][0]), flip(g, out_steps[i][1])
        return rows_of(dd, gg, add_r(step))

    def b_out(i, k, n):
        return copy_to(
            W.at[0, gates_of(n), out_rows(i, k), :], recvB.at[k - 1, i, gates_of(n)],
            B_s.at[k - 1, i, n], B_r.at[k - 1, i, n], r_dev(k),
        )

    def c_out(i, n):
        there = grec_out.at[d, gates_of(n), :, half]
        return copy_to(W.at[1, gates_of(n), out_rows(i, 0), :], there, C_s.at[i, n], C_r.at[i, n], z_dev(i))

    def own_out(n):
        there = grec_out.at[d, gates_of(n), :, half]
        return pltpu.make_async_copy(W.at[1, gates_of(n), out_rows(3, 0), :], there, C_s.at[3, n])

    steps = [(i, n) for i in range(4) for n in range(pieces)]

    def send_over(at):
        i, n = steps[at]
        for k in range(1, RR):
            for q in range(n * QN, (n + 1) * QN):
                W[0, q, out_rows(i, k), :] = dW[q, out_rows(i, k), :].astype(BF16)
            b_out(i, k, n).start()

    def send_home(at):
        i, n = steps[at]
        for k in range(1, RR):
            b_out(i, k, n).wait_recv()
        for q in range(n * QN, (n + 1) * QN):
            total = dW[q, out_rows(i, 0), :]
            for k in range(1, RR):
                total = total + recvB[k - 1, i, q].astype(F32)
            W[1, q, out_rows(i, 0), :] = total.astype(BF16)
        if i < 3:
            c_out(i, n).start()
        else:
            own_out(n).start()

    ahead = min(AHEAD, len(steps))
    for at in range(ahead):
        send_over(at)

    pgx_copy(2).wait_send()
    for b in range(BATCHES):
        take_state_grad(1, b)
        preact_grads(0, b)
    pgx_copy(0).start()
    weight_grads(0, False)

    gwin_s[...] = jnp.zeros_like(gwin_s)
    for q in range(4):
        gwin_s[q * EW : (q + 1) * EW] = gwin[q, 0:EW].astype(BF16)
    in_sum.start()

    once = jnp.where(mine == 0, 1.0, 0.0).astype(F32)
    epart[0:V8] = gemb[0:V8]
    epart[V8:VS] = jnp.zeros((VS - V8, 128), F32)
    for k in range(VP // 128):
        epart[V8 + k : V8 + k + 1] = gb[0:1, k * 128 : (k + 1) * 128] * once
    at = V8 + VP // 128
    epart[at : at + 1] = jnp.sum(lossv[...], axis=0, keepdims=True) * (once * dims.scale)

    stages = [[partner], [r_dev(k) for k in range(1, RR)], [y_dev(k) for k in range(1, Hy)], [dev(d, 1 - g, r, y, c)]]
    first = [sum(len(s) for s in stages[:n]) for n in range(len(stages) + 1)]

    def e_half(core):
        return pl.ds(pl.multiple_of(core * (VS // 2), 8), VS // 2)

    def e_copy(n, k):
        at = first[n] + k
        there = epart.at[e_half(1 - c), :] if n == 0 else esend.at[n - 1]
        return copy_to(there, erecv.at[at], e_s.at[at], e_r.at[at], stages[n][k])

    def e_start(n):
        for k in range(len(stages[n])):
            e_copy(n, k).start()

    def e_take(n):
        total = epart[e_half(c), :] if n == 0 else esend[n - 1]
        for k in range(len(stages[n])):
            e_copy(n, k).wait_recv()
            total = total + erecv[first[n] + k]
        if n < 3:
            esend[n] = total
            e_start(n + 1)
        else:
            eall[d, e_half(c), :] = total
            e_cross.start()

    e_cross = copy_to(
        eall.at[d, e_half(c), :], eall.at[d, e_half(c), :], e_s.at[first[4]], e_r.at[first[4]], dev(1 - d, g, r, y, c)
    )
    e_core = copy_to(
        eall.at[:, e_half(c), :], eall.at[:, e_half(c), :], e_s.at[first[4] + 1], e_r.at[first[4] + 1], partner
    )
    own_small = pltpu.make_async_copy(eall, small_out, lsem.at[2])

    def in_share():
        in_f32 = jnp.concatenate([gwin[q, 0:EW] for q in range(4)], axis=0)
        if dims.N_IN > 4 * EW:
            in_f32 = jnp.concatenate([in_f32, jnp.zeros((dims.N_IN - 4 * EW, U), F32)], axis=0)
        share = in_sum.share
        total = in_f32[0:share]
        for k in range(1, RR):
            total = jnp.where(r == k, in_f32[k * share : (k + 1) * share], total)
        return total

    def e_gather():
        e_cross.wait_recv()
        e_core.start()

    def e_finish():
        e_core.wait_recv()
        own_small.start()

    e_start(0)
    between = [
        lambda: e_take(0), lambda: in_sum.add(in_share()), lambda: e_take(1), lambda: e_take(2), in_sum.relay,
        lambda: e_take(3), in_sum.spread, e_gather, in_sum.finish, e_finish,
    ]
    for at in range(len(steps)):
        send_home(at)
        if at + ahead < len(steps):
            send_over(at + ahead)
        if between:
            between.pop(0)()
    for event in between:
        event()

    for j in range(3):
        ids_copy(j).wait_send()
    win_copy.wait_send()
    bias_copy.wait_send()
    for k in range(1, Hy):
        wdy_copy(k).wait_send()
    for k in range(Hy):
        wdc_copy(k).wait_send()
    for b in range(BATCHES):
        for p in range(len(peers)):
            f_copy(L - 1, b, p).wait_send()
            b_copy(2, b, p).wait_send()
            b_copy(1, b, p).wait_send()
    pgx_copy(1).wait_send()
    pgx_copy(0).wait_send()
    for n in range(4):
        for k in range(len(stages[n])):
            e_copy(n, k).wait_send()
    e_cross.wait_send()
    e_core.wait_send()
    dec_sum.drain()
    in_sum.drain()
    for i, n in steps:
        for k in range(1, RR):
            b_out(i, k, n).wait_send()
        if i < 3:
            c_out(i, n).wait()
        else:
            own_out(n).wait()
    own_small.wait()


def call_kernel(dims, *operands):
    R, RR, Hy, U, U2, NR, L, VP = dims.R, dims.RR, dims.Hy, dims.U, dims.U2, dims.NR, dims.L, dims.VP
    KR, EP, VS, H, RB, N_IN, N_DEC = dims.KR, dims.EP, dims.VS, dims.H, dims.RB, dims.N_IN, dims.N_DEC
    chips, peers, pieces = 2 * Hy, len(dims.peers), 4 // dims.QN
    vmem, sem = pltpu.VMEM, pltpu.SemaphoreType.DMA
    apart = pl.BlockSpec(memory_space=pl.ANY)
    inside = pl.BlockSpec(memory_space=pltpu.VMEM)
    groups = max(RR - 1, 1)
    along = max(Hy - 1, 1)
    stages = 1 + (RR - 1) + (Hy - 1) + 1
    id_rows = 2 * dims.P8 + 8
    scratch = [
        vmem((2, id_rows, 128), F32),
        vmem((4, id_rows, 128), F32),
        vmem((128, 128), F32),
        vmem((4, dims.RL // 2, 128), F32),
        vmem((2, 8, U), F32),
        vmem((2, 4, EP, U), BF16),
        vmem((2, 4, H, U), BF16),
        vmem((chips, 2, U, VP), BF16),
        vmem((L, NR, EP), BF16),
        vmem((L, NR, EP), BF16),
        vmem((NR, VP), F32),
        vmem((2, 4, RB, U), F32),
        vmem((L, chips, NR, U2), BF16),
        vmem((L, chips, NR, U2), BF16),
        vmem((L, 4, 2, NR, U), F32),
        vmem((L + 1, 2, NR, U), F32),
        vmem((L, NR, VP), BF16),
        vmem((L, NR, VP), BF16),
        vmem((NR, 128), F32),
        vmem((8, VP), F32),
        vmem((2, NR, U), F32),
        vmem((2, NR, U), F32),
        vmem((2, 2, 4, NR, U), BF16),
        vmem((2, 4, NR, U), BF16),
        vmem((2, peers, NR, U2), BF16),
        vmem((2, peers, NR, U2), BF16),
        vmem((4, H, U), F32),
        vmem((4, EP, U), F32),
        vmem((VP, EP), F32),
        vmem((max(VP, N_DEC), U), F32),
        vmem((N_DEC, U), BF16),
        vmem((groups, N_DEC // RR, U), BF16),
        vmem((2, N_DEC, 2 * U), BF16),
        vmem((N_IN, U), BF16),
        vmem((groups, N_IN // RR, U), BF16),
        vmem((2, N_IN, 2 * U), BF16),
        vmem((groups, 4, 4, KR, U), BF16),
        vmem((VS, 128), F32),
        vmem((3, VS // 2, 128), F32),
        vmem((stages, VS // 2, 128), F32),
        vmem((2, VS, 128), F32),
        sem((4,)),
        sem((3,)), sem((3,)),
        sem((1,)), sem((1,)),
        sem((1,)), sem((1,)),
        sem((along,)), sem((along,)),
        sem((Hy,)), sem((Hy,)),
        sem((3, pieces)), sem((3, pieces)),
        sem((4, groups, pieces)), sem((4, groups, pieces)),
        sem((4, RR, pieces)), sem((4, RR, pieces)),
        sem((1,)), sem((1,)),
        sem((2, BATCHES, peers)), sem((2, BATCHES, peers)),
        sem((L,)), sem((L,)),
        sem((L,)), sem((L,)),
        sem((2, BATCHES, peers)), sem((2, BATCHES, peers)),
        sem((2,)), sem((2,)),
        sem((2, 2 * groups + 3)),
        sem((2, 2 * groups + 3)),
        sem((groups, 4, pieces)), sem((groups, 4, pieces)),
        sem((4, pieces)), sem((4, pieces)),
        sem((stages + 2,)), sem((stages + 2,)),
    ]
    rows = NR * L
    flops = 2 * rows * (3 * H * 8 * U + 3 * H * VP)
    return pl.pallas_call(
        functools.partial(kernel, dims),
        out_shape=(
            jax.ShapeDtypeStruct((2, 4, KR, 2 * U), BF16),
            jax.ShapeDtypeStruct((2, N_IN, 2 * U), BF16),
            jax.ShapeDtypeStruct((2, N_DEC, 2 * U), BF16),
            jax.ShapeDtypeStruct((2, VS, 128), F32),
        ),
        in_specs=[inside] * 4 + [apart] * 3 + [inside] * 3,
        out_specs=(apart, apart, apart, apart),
        scratch_shapes=scratch,
        cost_estimate=pl.CostEstimate(flops=flops, bytes_accessed=8 << 20, transcendentals=rows * U2 * 8),
        compiler_params=pltpu.CompilerParams(
            collective_id=0, has_side_effects=True, vmem_limit_bytes=62 << 20
        ),
        name="train_step",
    )(*operands)


def local(
    char_ids, lang_ids, vocab_masks, targets, embedding, w_in, w_rec, b_in, b_rec, w_dec, b_dec
):
    R, hid = lax.axis_size("rows"), lax.axis_size("hid")
    RL, L = char_ids.shape
    E, units = w_in.shape[1], w_in.shape[3]
    V = embedding.shape[1]
    KR = w_rec.shape[1]
    U = units // 2
    dims = Dims(
        R=R, RR=R // 4, Hy=hid // 2, H=units * hid, KR=KR, U=U, RL=RL, L=L, V=V, E=E,
        LANGS=vocab_masks.shape[0], scale=1.0 / (RL * R * L),
    )
    VP, EP, EW = dims.VP, dims.EP, dims.EW

    bias = b_in.astype(F32) + b_rec.astype(F32)
    win = jnp.pad(w_in.transpose(0, 2, 1, 3), ((0, 0), (0, 0), (0, EP - E), (0, 0)))
    wrec = w_rec.transpose(0, 2, 1, 3)
    wdec = jnp.pad(w_dec, ((0, 0), (0, 0), (0, VP - V))).reshape(2, 2, U, VP)
    emb = jnp.concatenate([embedding, jnp.ones((2, V, 1), BF16)], axis=2)
    emb = jnp.pad(emb, ((0, 0), (0, VP - V), (0, EP - E - 1)))
    bdec = jnp.pad(b_dec.astype(F32), ((0, 0), (0, VP - V)))[:, None, :]
    lang_rows = ceil_to(dims.LANGS, 16)
    mask = jnp.pad(vocab_masks.astype(BF16), ((0, lang_rows - dims.LANGS), (0, VP - V)))

    grec, gwin, gwd, small = call_kernel(
        dims, char_ids.T, targets.transpose(0, 2, 1), lang_ids[None], bias, win, wrec, wdec, emb, bdec, mask
    )

    grad_w_rec = grec.astype(F32).transpose(0, 2, 1, 3)
    gwin = gwin[:, : 4 * EW].reshape(2, 4, EW, units).astype(F32)
    grad_w_in = gwin[:, :, :E].transpose(0, 2, 1, 3)
    grad_bias = gwin[:, :, E]
    grad_w_dec = gwd[:, :V].astype(F32).transpose(0, 2, 1)
    V8 = dims.V8
    grad_embedding = small[:, :V, :E]
    grad_b_dec = small[:, V8 : V8 + VP // 128].reshape(2, VP)[:, :V]
    total_loss = jnp.sum(small[:, V8 + VP // 128, 0])
    return (
        total_loss,
        grad_embedding,
        grad_w_in,
        grad_w_rec,
        grad_bias,
        grad_bias,
        grad_w_dec,
        grad_b_dec,
    )


def solution(mesh):
    placed = (
        P("rows", None),
        P("rows"),
        P(),
        P(None, "rows", None),
        P(),
        P(None, None, None, "hid"),
        P(None, "rows", None, "hid"),
        P(None, None, "hid"),
        P(None, None, "hid"),
        P(None, "hid", None),
        P(),
    )
    return jax.shard_map(
        local,
        mesh=mesh,
        in_specs=placed,
        out_specs=(
            P(),
            P(),
            P(None, None, None, "hid"),
            P(None, "rows", None, "hid"),
            P(None, None, "hid"),
            P(None, None, "hid"),
            P(None, "hid", None),
            P(),
        ),
        check_vma=False,
    )
```

```python
import functools
from typing import NamedTuple

import jax
import jax.numpy as jnp
from jax import lax
from jax.experimental import pallas as pl
from jax.experimental.pallas import tpu as pltpu
from jax.sharding import PartitionSpec as P

MESH = pl.DeviceIdType.MESH
F32 = jnp.float32
BF16 = jnp.bfloat16
masked_value = -1000000000.0
ROW_PARTS = 2
AHEAD = 8
EARLY = 2
WINDOW = 2
BATCHES = 2


def ceil_to(n, m):
    return (n + m - 1) // m * m


class Dims(NamedTuple):
    R: int
    RR: int
    Hy: int
    H: int
    KR: int
    U: int
    RL: int
    L: int
    V: int
    E: int
    LANGS: int
    scale: float

    @property
    def U2(self):
        return 2 * self.U

    @property
    def NR(self):
        return 2 * self.RL

    @property
    def VP(self):
        return ceil_to(self.V, 128)

    @property
    def RB(self):
        return self.NR // BATCHES

    @property
    def QN(self):
        return 1 if self.RR <= 2 else 4

    @property
    def KP(self):
        return ROW_PARTS if self.RR <= 2 else 1

    @property
    def pieces(self):
        return 4 // self.QN * self.KP

    @property
    def KRP(self):
        return self.KR // self.KP

    @property
    def N_IN(self):
        return ceil_to(4 * self.EW, 16 * self.RR)

    @property
    def N_DEC(self):
        return ceil_to(self.V, 16 * self.RR)

    @property
    def P8(self):
        return ceil_to(self.L, 8)

    @property
    def EP(self):
        return ceil_to(self.E + 2, 128)

    @property
    def EW(self):
        return ceil_to(self.E + 2, 16)

    @property
    def V8(self):
        return ceil_to(self.V, 8)

    @property
    def VS(self):
        return ceil_to(self.V8 + 8, 16)

    @property
    def peers(self):
        far = [(1, k) for k in range(1, self.Hy)]
        beside = [(0, k) for k in range(1, self.Hy)]
        return far + beside + [(1, 0)]


Z_STEPS = ((1, 0), (1, 1), (0, 1))


def dot(a, b):
    return jnp.dot(a, b, preferred_element_type=F32)


def dot_nt(a, b):
    return lax.dot_general(a, b, (((1,), (1,)), ((), ())), preferred_element_type=F32)


def dot_tn(a, b):
    return lax.dot_general(a, b, (((0,), (0,)), ((), ())), preferred_element_type=F32)


def flip(bit, step):
    return 1 - bit if step else bit


def kernel(
    dims,
    chars_ref, targets_ref, lang_ref, bias_ref, win_in, wrec_in, wdec_in, emb_ref, bdec_ref, mask_ref,
    grec_out, gwin_out, gwd_out, small_out,
    idsrc, idsall, idtmp, ids, bias, win, W, wd, x, xp, allowed, acc, st, stp, gs, cell, lg, lgp, lossv, gb,
    dh, cg, pg, pgx, psend, precv, dW, gwin, gemb, gwd, gwd_s, gwd_r, gwd_all, gwin_s, gwin_r, gwin_all,
    recvB, epart, esend, erecv, eall,
    lsem, ids_s, ids_r, win_s2, win_r2, bias_s, bias_r, wdy_s, wdy_r, wdc_s, wdc_r, wz_s, wz_r, wx_s, wx_r, wc_s, wc_r,
    xp_s, xp_r, f_s, f_r, stp_s, stp_r, lgp_s, lgp_r, b_s, b_r, pgx_s, pgx_r,
    gwd_sems, gwin_sems, B_s, B_r, C_s, C_r, e_s, e_r,
):
    R, RR, Hy, U, U2, NR, L, VP = dims.R, dims.RR, dims.Hy, dims.U, dims.U2, dims.NR, dims.L, dims.VP
    KR, EW, V8, VS, RL, RB, QN = dims.KR, dims.EW, dims.V8, dims.VS, dims.RL, dims.RB, dims.QN
    peers = dims.peers
    KP, KRP, pieces = dims.KP, dims.KRP, dims.pieces
    rho, hid = lax.axis_index("rows"), lax.axis_index("hid")
    d, g, r = rho // (R // 2), lax.rem(rho // RR, 2), lax.rem(rho, RR)
    y, c = hid // 2, lax.rem(hid, 2)
    mine = y * 2 + g
    part = d * 2 + g

    def dev(dd, gg, rr, yy, cc):
        return (dd * (R // 2) + gg * RR + rr, yy * 2 + cc)

    def copy_to(src, dst, send, recv, device):
        return pltpu.make_async_remote_copy(
            src_ref=src, dst_ref=dst, send_sem=send, recv_sem=recv, device_id=device, device_id_type=MESH
        )

    def add_r(step):
        return lax.rem(r + step, RR)

    def add_y(step):
        return lax.rem(y + step, Hy)

    def place_of(dd, gg, rr):
        index = dd * (R // 2) + gg * RR + rr
        per = U // KR
        block = index // per
        hid_of, g_of = block // 2, lax.rem(block, 2)
        return (hid_of // 2) * 2 + g_of, lax.rem(hid_of, 2) * U + lax.rem(index, per) * KR

    def rows_of(dd, gg, rr, n=None):
        chip, unit = place_of(dd, gg, rr)
        row = chip * U2 + unit
        if n is None:
            return pl.ds(pl.multiple_of(row, KR), KR)
        return pl.ds(pl.multiple_of(row + n % KP * KRP, KRP), KRP)

    def rows_in(n):
        return pl.ds(n % KP * KRP, KRP)

    def chip_rows(m):
        return pl.ds(pl.multiple_of(m * U2, U2), U2)

    partner = dev(d, g, r, y, 1 - c)
    half = pl.ds(pl.multiple_of(g * U, U), U)

    def z_dev(j):
        return dev(flip(d, Z_STEPS[j][0]), flip(g, Z_STEPS[j][1]), r, y, c)

    def r_dev(step):
        return dev(d, g, add_r(step), y, c)

    def y_dev(step):
        return dev(d, g, r, add_y(step), c)

    def peer_dev(p):
        return dev(d, flip(g, peers[p][0]), r, add_y(peers[p][1]), c)

    barrier = pltpu.get_barrier_semaphore()
    greeted = [z_dev(j) for j in range(3)] + [r_dev(k) for k in range(1, RR)] + [partner]
    greeted += [peer_dev(p) for p in range(len(peers)) if peers[p] != (1, 0)]
    for device in greeted:
        pl.semaphore_signal(barrier, inc=1, device_id=device, device_id_type=MESH)
    pl.semaphore_wait(barrier, len(greeted))

    def ids_copy(j):
        return copy_to(idsrc.at[flip(d, Z_STEPS[j][0])], idsall.at[part], ids_s.at[j], ids_r.at[j], z_dev(j))

    def gates_of(n):
        return pl.ds(n // KP * QN, QN)

    def wz_copy(j, n):
        columns = pl.ds(pl.multiple_of(flip(g, Z_STEPS[j][1]) * U, U), U)
        there = wrec_in.at[flip(d, Z_STEPS[j][0]), gates_of(n), rows_in(n), columns]
        return copy_to(there, W.at[c, gates_of(n), rows_of(d, g, r, n), :], wz_s.at[j, n], wz_r.at[j, n], z_dev(j))

    def z_block(j):
        steps = Z_STEPS[j] if j < 3 else (0, 0)
        return flip(d, steps[0]), flip(g, steps[1])

    def w_block(core, j, k, n):
        dd, gg = z_block(j)
        return W.at[core, gates_of(n), rows_of(dd, gg, lax.rem(r + RR - k, RR), n), :]

    def wx_copy(j, k, n):
        block = w_block(c, j, 0, n)
        return copy_to(block, block, wx_s.at[j, k - 1, n], wx_r.at[j, k - 1, n], r_dev(k))

    def wc_copy(j, k, n, core):
        block = w_block(core, j, k, n)
        return copy_to(block, block, wc_s.at[j, k, n], wc_r.at[j, k, n], partner)

    def wd_rows(yy):
        return wd.at[pl.ds(yy * 2, 2), c]

    def wdy_copy(k):
        return copy_to(wdec_in.at[d], wd_rows(y), wdy_s.at[k - 1], wdy_r.at[k - 1], y_dev(k))

    def wdc_copy(k):
        yy = lax.rem(y + Hy - k, Hy)
        return copy_to(wd_rows(yy), wd_rows(yy), wdc_s.at[k], wdc_r.at[k], partner)

    win_copy = copy_to(win_in.at[d, :, :, half], win.at[c], win_s2.at[0], win_r2.at[0], partner)
    bias_copy = copy_to(bias.at[c], bias.at[c], bias_s.at[0], bias_r.at[0], partner)
    own_win = pltpu.make_async_copy(win_in.at[d, :, :, half], win.at[c], lsem.at[1])
    own_wd = pltpu.make_async_copy(wdec_in.at[d], wd_rows(y), lsem.at[2])
    own_w = pltpu.make_async_copy(
        wrec_in.at[d, :, :, half], W.at[c, :, rows_of(d, g, r), :], lsem.at[3]
    )

    own_w.start()
    for n in range(min(WINDOW, pieces)):
        for j in range(3):
            wz_copy(j, n).start()
    own_win.start()
    win_copy.start()
    for k in range(1, Hy):
        wdy_copy(k).start()
    own_wd.start()

    P8 = dims.P8
    idsrc[...] = jnp.zeros_like(idsrc)
    for dd in range(2):
        idsrc[dd, 0:L, 0:RL] = chars_ref[...].astype(F32)
        idsrc[dd, P8 : P8 + L, 0:RL] = targets_ref[dd].astype(F32)
        idsrc[dd, 2 * P8 : 2 * P8 + 8, 0:RL] = jnp.broadcast_to(lang_ref[...].astype(F32), (8, RL))
    for j in range(3):
        ids_copy(j).start()
    bias[c, 0:4] = bias_ref[d, :, half]
    bias_copy.start()
    idsall[part] = idsrc[d]

    own_w.wait()
    for n in range(pieces):
        for k in range(1, RR):
            wx_copy(3, k, n).start()
        wc_copy(3, 0, n, c).start()

    dW[...] = jnp.zeros_like(dW)
    gwin[...] = jnp.zeros_like(gwin)
    gemb[...] = jnp.zeros_like(gemb)
    lossv[...] = jnp.zeros_like(lossv)
    gb[...] = jnp.zeros_like(gb)
    cg[...] = jnp.zeros_like(cg)
    cell[0] = jnp.zeros_like(cell[0])
    idtmp[...] = jnp.zeros_like(idtmp)

    for j in range(3):
        ids_copy(j).wait_recv()
    for n in range(4):
        idtmp[:, 0 : idsall.shape[1]] = idsall[n].T
        ids[n] = idtmp[pl.ds(pl.multiple_of(c * (RL // 2), RL // 2), RL // 2), :]

    lane = lax.broadcasted_iota(jnp.int32, (NR, 128), 1)
    vocab = lax.broadcasted_iota(jnp.int32, (NR, VP), 1).astype(F32)

    def id_column(at):
        held = ids[...].reshape(NR, 128)
        return jnp.sum(jnp.where(lane == at, held, 0.0), axis=1, keepdims=True)

    def place(t):
        return t + d * (L - 1 - 2 * t)

    def char_hot(t):
        return jnp.where(vocab == id_column(place(t)), 1.0, 0.0).astype(BF16)

    lang_lane = lax.broadcasted_iota(jnp.int32, (NR, mask_ref.shape[0]), 1).astype(F32)
    lang_hot = jnp.where(lang_lane == id_column(2 * P8), 1.0, 0.0).astype(BF16)
    allowed[...] = dot(lang_hot, mask_ref[...])

    @pl.loop(0, L)
    def _(t):
        x[t] = dot(char_hot(t), emb_ref[d]).astype(BF16)

    xp_copy = copy_to(x, xp, xp_s.at[0], xp_r.at[0], partner)
    xp_copy.start()

    own_wd.wait()
    wdc_copy(0).start()
    own_win.wait()
    win_copy.wait_recv()
    bias_copy.wait_recv()

    def part_rows(b):
        return pl.ds(b * RB, RB)

    def f_copy(t, b, p):
        slot = lax.rem(t, 2)
        block = st.at[t, mine, part_rows(b), :]
        return copy_to(block, block, f_s.at[slot, b, p], f_r.at[slot, b, p], peer_dev(p))

    def gates(t, b):
        rows = part_rows(b)
        for cc in range(2):
            si = jax.nn.sigmoid(acc[cc, 0])
            sf = jax.nn.sigmoid(acc[cc, 1])
            tg = jnp.tanh(acc[cc, 2])
            so = jax.nn.sigmoid(acc[cc, 3])
            new = sf * cell[t, cc, rows] + si * tg
            cell[t + 1, cc, rows] = new
            st[t, mine, rows, cc * U : (cc + 1) * U] = (so * jnp.tanh(new)).astype(BF16)
            gs[t, 0, cc, rows] = si
            gs[t, 1, cc, rows] = sf
            gs[t, 2, cc, rows] = tg
            gs[t, 3, cc, rows] = so

    def peer_block(p):
        yy = lax.rem(y + Hy - peers[p][1], Hy)
        return yy * 2 + flip(g, peers[p][0])

    for b in range(BATCHES):
        for cc in range(2):
            for q in range(4):
                acc[cc, q] = dot(x[0, part_rows(b)], win[cc, q]) + bias[cc, q : q + 1]
        gates(0, b)
        for p in range(len(peers)):
            f_copy(0, b, p).start()

    for k in range(1, Hy):
        wdy_copy(k).wait_recv()
        wdc_copy(k).start()
    from_z, beside = [], [(2, n) for n in range(pieces)]
    for n in range(pieces):
        from_z += beside[2 * n : 2 * n + 2] + [(0, n), (1, n)]
    from_x = [(3, n) for n in range(pieces)] + from_z
    for at in range(len(from_x)):
        if at < len(from_z):
            j, n = from_z[at]
            wz_copy(j, n).wait_recv()
            for k in range(1, RR):
                wx_copy(j, k, n).start()
            wc_copy(j, 0, n, c).start()
            if n + WINDOW < pieces:
                wz_copy(j, n + WINDOW).start()
        j, n = from_x[at]
        for k in range(1, RR):
            wx_copy(j, k, n).wait_recv()
            wc_copy(j, k, n, c).start()
    for j, n in from_x:
        for k in range(RR):
            wc_copy(j, k, n, 1 - c).wait_recv()
    for k in range(Hy):
        yy = lax.rem(y + Hy - k, Hy)
        other = wd.at[pl.ds(yy * 2, 2), 1 - c]
        copy_to(other, other, wdc_s.at[k], wdc_r.at[k], partner).wait_recv()

    def stp_copy(t):
        return copy_to(st.at[t], stp.at[t], stp_s.at[t], stp_r.at[t], partner)

    def lgp_copy(t):
        return copy_to(lg.at[t], lgp.at[t], lgp_s.at[t], lgp_r.at[t], partner)

    def decode(t):
        stp_copy(t).start()
        logits = bdec_ref[d]
        for m in range(2 * Hy):
            logits = logits + dot(st[t, m], wd[m].reshape(U2, VP))
        masked = jnp.where(allowed[...] > 0.5, logits, masked_value)
        top = jnp.max(masked, axis=1, keepdims=True)
        powers = jnp.exp(masked - top)
        total = jnp.sum(powers, axis=1, keepdims=True)
        hot = vocab == id_column(P8 + place(t))
        picked = jnp.sum(jnp.where(hot, logits, 0.0), axis=1, keepdims=True)
        lossv[...] += jnp.broadcast_to(top + jnp.log(total) - picked, (NR, 128))
        grad = ((powers / total - jnp.where(hot, 1.0, 0.0)) * dims.scale).astype(BF16)
        lg[t] = grad
        gb[0:1, :] += jnp.sum(grad.astype(F32), axis=0, keepdims=True)
        lgp_copy(t).start()

    @pl.loop(1, L)
    def _(t):
        for b in range(BATCHES):
            rows = part_rows(b)
            for cc in range(2):
                for q in range(4):
                    start = dot(x[t, rows], win[cc, q]) + bias[cc, q : q + 1]
                    acc[cc, q] = start + dot(st[t - 1, mine, rows], W[cc, q, chip_rows(mine), :])
            for p in reversed(range(len(peers))):
                f_copy(t - 1, b, p).wait_recv()
                m = peer_block(p)
                for cc in range(2):
                    for q in range(4):
                        acc[cc, q] += dot(st[t - 1, m, rows], W[cc, q, chip_rows(m), :])
            gates(t, b)
            for p in range(len(peers)):
                f_copy(t - 1, b, p).wait_send()
            for p in range(len(peers)):
                f_copy(t, b, p).start()
        decode(t - 1)

    for j, n in from_x:
        if j < 3:
            wz_copy(j, n).wait_send()
        for k in range(1, RR):
            wx_copy(j, k, n).wait_send()
        for k in range(RR):
            wc_copy(j, k, n, c).wait_send()

    @pl.loop(0, dims.H // U)
    def _(k):
        rows = pl.ds(pl.multiple_of(k * U, U), U)
        for cc in range(2):
            for q in range(4):
                W[cc, q, rows, :] = W[cc, q, rows, :].T

    for b in range(BATCHES):
        for p in reversed(range(len(peers))):
            f_copy(L - 1, b, p).wait_recv()
    decode(L - 1)

    def dec_back(t, cc):
        return dot_nt(lg[t], wd[mine, cc])

    def b_copy(t, b, p):
        slot = lax.rem(t, 2)
        there = precv.at[slot, p, part_rows(b), :]
        return copy_to(
            psend.at[slot, p, part_rows(b), :], there, b_s.at[slot, b, p], b_r.at[slot, b, p], peer_dev(p)
        )

    def pgx_copy(t):
        return copy_to(pg.at[lax.rem(t, 2), 1 - c], pgx.at[t], pgx_s.at[t], pgx_r.at[t], partner)

    def preact_grads(t, b):
        slot = lax.rem(t, 2)
        rows = part_rows(b)
        for cc in range(2):
            h = dh[cc, rows]
            si, sf, tg, so = (gs[t, q, cc, rows] for q in range(4))
            tc = jnp.tanh(cell[t + 1, cc, rows])
            total = cg[cc, rows] + h * so * (1.0 - tc * tc)
            pg[slot, cc, 0, rows] = (total * tg * si * (1.0 - si)).astype(BF16)
            pg[slot, cc, 1, rows] = (total * cell[t, cc, rows] * sf * (1.0 - sf)).astype(BF16)
            pg[slot, cc, 2, rows] = (total * si * (1.0 - tg * tg)).astype(BF16)
            pg[slot, cc, 3, rows] = (h * tc * so * (1.0 - so)).astype(BF16)
            cg[cc, rows] = total * sf

    def partial(t, b, m, cc):
        slot = lax.rem(t, 2)
        rows = pl.ds(pl.multiple_of(m * U2 + cc * U, U), U)
        total = None
        for kk in range(2):
            for q in range(4):
                term = dot(pg[slot, kk, q, part_rows(b)], W[kk, q, rows, :])
                total = term if total is None else total + term
        return total

    def take_state_grad(t, b):
        slot = lax.rem(t, 2)
        rows = part_rows(b)
        for p in reversed(range(len(peers))):
            b_copy(t, b, p).wait_recv()
            for cc in range(2):
                dh[cc, rows] += precv[slot, p, rows, cc * U : (cc + 1) * U].astype(F32)

    def both_cores(t, q):
        return jnp.concatenate([pg[lax.rem(t, 2), c, q], pgx[t, q]], axis=0)

    def rec_grads(t):
        for q in range(4):
            both = both_cores(t, q)
            for m in range(2 * Hy):
                states = jnp.concatenate([st[t - 1, m], stp[t - 1, m]], axis=0)
                dW[q, m * U2 : (m + 1) * U2, :] += dot_tn(states, both)

    def in_grads(t):
        slot = lax.rem(t, 2)
        inputs = jnp.concatenate([x[t], xp[t]], axis=0)
        for q in range(4):
            gwin[q] += dot_tn(inputs, both_cores(t, q))
        back = None
        for cc in range(2):
            for q in range(4):
                term = dot_nt(pg[slot, cc, q], win[cc, q])
                back = term if back is None else back + term
        high = back.astype(BF16)
        rest = (back - high.astype(F32)).astype(BF16)
        hot = char_hot(t)
        gemb[...] += dot_tn(hot, high) + dot_tn(hot, rest)

    class SmallSum:
        def __init__(self, send, recv, whole, out, sems, own_sem):
            self.send, self.recv, self.whole, self.out, self.sems, self.own = send, recv, whole, out, sems, own_sem
            self.share = whole.shape[1] // RR

        def rows(self, rr):
            return pl.ds(pl.multiple_of(rr * self.share, 16), self.share)

        def pair(self, at):
            return self.sems.at[0, at], self.sems.at[1, at]

        def first(self, k):
            return copy_to(self.send.at[self.rows(add_r(k)), :], self.recv.at[k - 1], *self.pair(k - 1), r_dev(k))

        def block(self, dd, gg):
            return self.whole.at[dd, self.rows(r), pl.ds(pl.multiple_of(gg * U, U), U)]

        def along(self, j):
            block = self.block(1 - d, g) if j == 1 else self.block(d, g)
            return copy_to(block, block, *self.pair(RR - 1 + j), z_dev(0 if j == 0 else 2))

        def last(self, k):
            block = self.whole.at[:, self.rows(r), :]
            return copy_to(block, block, *self.pair(RR + 2 + k - 1), r_dev(k))

        def to_out(self):
            return pltpu.make_async_copy(self.whole, self.out, self.own)

        def start(self):
            for k in range(1, RR):
                self.first(k).start()

        def add(self, value):
            for k in range(1, RR):
                self.first(k).wait_recv()
                value = value + self.recv[k - 1].astype(F32)
            self.whole[d, self.rows(r), half] = value.astype(BF16)
            self.along(0).start()
            self.along(2).start()

        def relay(self):
            self.along(0).wait_recv()
            self.along(1).start()

        def spread(self):
            self.along(2).wait_recv()
            self.along(1).wait_recv()
            for k in range(1, RR):
                self.last(k).start()

        def finish(self):
            for k in range(1, RR):
                self.last(k).wait_recv()
            self.to_out().start()

        def drain(self):
            for k in range(1, RR):
                self.first(k).wait_send()
                self.last(k).wait_send()
            for j in range(3):
                self.along(j).wait_send()
            self.to_out().wait()

    dec_sum = SmallSum(gwd_s, gwd_r, gwd_all, gwd_out, gwd_sems, lsem.at[0])
    in_sum = SmallSum(gwin_s, gwin_r, gwin_all, gwin_out, gwin_sems, lsem.at[1])

    def decoder_grad():
        gwd[...] = jnp.zeros_like(gwd)

        @pl.loop(0, L)
        def _(t):
            columns = pl.ds(pl.multiple_of(c * U, U), U)
            states = jnp.concatenate([st[t, mine, :, columns], stp[t, mine, :, columns]], axis=0)
            gwd[...] += dot_tn(jnp.concatenate([lg[t], lgp[t]], axis=0), states)

        gwd_s[...] = gwd[0 : dims.N_DEC].astype(BF16)
        dec_sum.start()

    for cc in range(2):
        dh[cc] = dec_back(L - 1, cc)

    @pl.loop(0, L)
    def _(t):
        stp_copy(t).wait()
        lgp_copy(t).wait()

    xp_copy.wait()

    @pl.loop(0, L - 1)
    def _(i):
        t = L - 1 - i
        slot = lax.rem(t, 2)

        @pl.when(i > 1)
        def _():
            pgx_copy(t + 2).wait_send()

        for b in range(BATCHES):
            rows = part_rows(b)

            @pl.when(i > 0)
            def _():
                take_state_grad(t + 1, b)

            @pl.when(i > 1)
            def _():
                for p in range(len(peers)):
                    b_copy(t + 2, b, p).wait_send()

            preact_grads(t, b)
            for p in range(len(peers)):
                m = add_y(peers[p][1]) * 2 + flip(g, peers[p][0])
                for cc in range(2):
                    psend[slot, p, rows, cc * U : (cc + 1) * U] = partial(t, b, m, cc).astype(BF16)
                b_copy(t, b, p).start()
            for cc in range(2):
                dh[cc, rows] = partial(t, b, mine, cc)
        pgx_copy(t).start()
        for cc in range(2):
            dh[cc] += dec_back(t - 1, cc)

        @pl.when(i > 0)
        def _():
            pgx_copy(t + 1).wait_recv()
            rec_grads(t + 1)
            in_grads(t + 1)

        @pl.when(i == 0)
        def _():
            decoder_grad()

        @pl.when(i == 1)
        def _():
            dec_sum.add(gwd[dec_sum.rows(r), :])

        @pl.when(i == 2)
        def _():
            dec_sum.relay()

        @pl.when(i == 3)
        def _():
            dec_sum.spread()

        @pl.when(i == 4)
        def _():
            dec_sum.finish()

    out_steps = ((1, 0), (1, 1), (0, 1), (0, 0))

    def out_device(i, step):
        return flip(d, out_steps[i][0]), flip(g, out_steps[i][1]), add_r(step)

    def out_rows(i, step, n):
        return rows_of(*out_device(i, step), n)

    def b_out(i, k, n):
        return copy_to(
            W.at[0, gates_of(n), out_rows(i, k, n), :], recvB.at[k - 1, i, gates_of(n), rows_in(n), :],
            B_s.at[k - 1, i, n], B_r.at[k - 1, i, n], r_dev(k),
        )

    def c_out(i, n):
        there = grec_out.at[d, gates_of(n), rows_in(n), half]
        return copy_to(W.at[1, gates_of(n), out_rows(i, 0, n), :], there, C_s.at[i, n], C_r.at[i, n], z_dev(i))

    def own_out(n):
        there = grec_out.at[d, gates_of(n), rows_in(n), half]
        return pltpu.make_async_copy(W.at[1, gates_of(n), out_rows(3, 0, n), :], there, C_s.at[3, n])

    def gates_in(n):
        return range(n // KP * QN, (n // KP + 1) * QN)

    fused = KRP % 128 == 0

    def rec_piece(i, step, n, q):
        total = dW[q, out_rows(i, step, n), :]
        if fused:
            chip, unit = place_of(*out_device(i, step))
            units = pl.ds(pl.multiple_of(unit + n % KP * KRP, 128), KRP)
            states = jnp.concatenate([st[0, chip, :, units], stp[0, chip, :, units]], axis=0)
            total = total + dot_tn(states, both_cores(1, q))
        return total

    steps = [(i, n) for n in range(pieces) for i in (0, 2, 1, 3)]

    def send_over(at):
        i, n = steps[at]
        for k in range(1, RR):
            for q in gates_in(n):
                W[0, q, out_rows(i, k, n), :] = rec_piece(i, k, n, q).astype(BF16)
            b_out(i, k, n).start()

    def send_home(at):
        i, n = steps[at]
        for k in range(1, RR):
            b_out(i, k, n).wait_recv()
        for q in gates_in(n):
            total = rec_piece(i, 0, n, q)
            for k in range(1, RR):
                total = total + recvB[k - 1, i, q, rows_in(n), :].astype(F32)
            W[1, q, out_rows(i, 0, n), :] = total.astype(BF16)
        if i < 3:
            c_out(i, n).start()
        else:
            own_out(n).start()
        if at + ahead < len(steps):
            send_over(at + ahead)

    pgx_copy(1).wait_recv()
    if not fused:
        rec_grads(1)
    ahead = min(AHEAD, len(steps))
    for at in range(ahead):
        send_over(at)
    in_grads(1)

    pgx_copy(2).wait_send()
    sent = 0
    for b in range(BATCHES):
        take_state_grad(1, b)
        preact_grads(0, b)
        for at in range(sent, min(sent + EARLY, len(steps))):
            send_home(at)
        sent = min(sent + EARLY, len(steps))
    pgx_copy(0).start()
    for at in range(sent, min(sent + EARLY, len(steps))):
        send_home(at)
    sent = min(sent + EARLY, len(steps))
    pgx_copy(0).wait_recv()
    in_grads(0)

    gwin_s[...] = jnp.zeros_like(gwin_s)
    for q in range(4):
        gwin_s[q * EW : (q + 1) * EW] = gwin[q, 0:EW].astype(BF16)
    in_sum.start()

    once = jnp.where(mine == 0, 1.0, 0.0).astype(F32)
    epart[0:V8] = gemb[0:V8]
    epart[V8:VS] = jnp.zeros((VS - V8, 128), F32)
    for k in range(VP // 128):
        epart[V8 + k : V8 + k + 1] = gb[0:1, k * 128 : (k + 1) * 128] * once
    at = V8 + VP // 128
    epart[at : at + 1] = jnp.sum(lossv[...], axis=0, keepdims=True) * (once * dims.scale)

    stages = [[partner], [peer_dev(p) for p in range(len(peers))], [r_dev(k) for k in range(1, RR)]]
    first = [sum(len(s) for s in stages[:n]) for n in range(len(stages) + 1)]

    def e_half(core):
        return pl.ds(pl.multiple_of(core * (VS // 2), 8), VS // 2)

    def e_copy(n, k):
        at = first[n] + k
        there = epart.at[e_half(1 - c), :] if n == 0 else esend.at[n - 1]
        return copy_to(there, erecv.at[at], e_s.at[at], e_r.at[at], stages[n][k])

    def e_start(n):
        for k in range(len(stages[n])):
            e_copy(n, k).start()

    def e_take(n):
        total = epart[e_half(c), :] if n == 0 else esend[n - 1]
        for k in range(len(stages[n])):
            e_copy(n, k).wait_recv()
            total = total + erecv[first[n] + k]
        if n < 2:
            esend[n] = total
            e_start(n + 1)
        else:
            eall[d, e_half(c), :] = total
            e_cross.start()

    e_cross = copy_to(
        eall.at[d, e_half(c), :], eall.at[d, e_half(c), :], e_s.at[first[3]], e_r.at[first[3]], z_dev(0)
    )
    e_core = copy_to(
        eall.at[:, e_half(c), :], eall.at[:, e_half(c), :], e_s.at[first[3] + 1], e_r.at[first[3] + 1], partner
    )
    own_small = pltpu.make_async_copy(eall, small_out, lsem.at[2])

    def in_share():
        in_f32 = jnp.concatenate([gwin[q, 0:EW] for q in range(4)], axis=0)
        if dims.N_IN > 4 * EW:
            in_f32 = jnp.concatenate([in_f32, jnp.zeros((dims.N_IN - 4 * EW, U), F32)], axis=0)
        share = in_sum.share
        total = in_f32[0:share]
        for k in range(1, RR):
            total = jnp.where(r == k, in_f32[k * share : (k + 1) * share], total)
        return total

    def e_gather():
        e_cross.wait_recv()
        e_core.start()

    def e_finish():
        e_core.wait_recv()
        own_small.start()

    e_start(0)
    between = [
        (0.05, lambda: e_take(0)),
        (0.2, lambda: in_sum.add(in_share())),
        (0.2, lambda: e_take(1)),
        (0.35, lambda: e_take(2)),
        (0.5, in_sum.relay),
        (0.6, e_gather),
        (0.7, in_sum.spread),
        (0.8, e_finish),
        (1.0, in_sum.finish),
    ]
    for at in range(sent, len(steps)):
        send_home(at)
        while between and (at + 1 - sent) >= between[0][0] * (len(steps) - sent):
            between.pop(0)[1]()
    for _, event in between:
        event()

    for j in range(3):
        ids_copy(j).wait_send()
    win_copy.wait_send()
    bias_copy.wait_send()
    for k in range(1, Hy):
        wdy_copy(k).wait_send()
    for k in range(Hy):
        wdc_copy(k).wait_send()
    for b in range(BATCHES):
        for p in range(len(peers)):
            f_copy(L - 1, b, p).wait_send()
            b_copy(2, b, p).wait_send()
            b_copy(1, b, p).wait_send()
    pgx_copy(1).wait_send()
    pgx_copy(0).wait_send()
    for n in range(3):
        for k in range(len(stages[n])):
            e_copy(n, k).wait_send()
    e_cross.wait_send()
    e_core.wait_send()
    dec_sum.drain()
    in_sum.drain()
    for i, n in steps:
        for k in range(1, RR):
            b_out(i, k, n).wait_send()
        if i < 3:
            c_out(i, n).wait()
        else:
            own_out(n).wait()
    own_small.wait()


def call_kernel(dims, *operands):
    R, RR, Hy, U, U2, NR, L, VP = dims.R, dims.RR, dims.Hy, dims.U, dims.U2, dims.NR, dims.L, dims.VP
    KR, EP, VS, H, RB, N_IN, N_DEC = dims.KR, dims.EP, dims.VS, dims.H, dims.RB, dims.N_IN, dims.N_DEC
    chips, peers, pieces = 2 * Hy, len(dims.peers), dims.pieces
    vmem, sem = pltpu.VMEM, pltpu.SemaphoreType.DMA
    apart = pl.BlockSpec(memory_space=pl.ANY)
    inside = pl.BlockSpec(memory_space=pltpu.VMEM)
    groups = max(RR - 1, 1)
    along = max(Hy - 1, 1)
    stages = 1 + peers + (RR - 1)
    id_rows = 2 * dims.P8 + 8
    scratch = [
        vmem((2, id_rows, 128), F32),
        vmem((4, id_rows, 128), F32),
        vmem((128, 128), F32),
        vmem((4, dims.RL // 2, 128), F32),
        vmem((2, 8, U), F32),
        vmem((2, 4, EP, U), BF16),
        vmem((2, 4, H, U), BF16),
        vmem((chips, 2, U, VP), BF16),
        vmem((L, NR, EP), BF16),
        vmem((L, NR, EP), BF16),
        vmem((NR, VP), F32),
        vmem((2, 4, RB, U), F32),
        vmem((L, chips, NR, U2), BF16),
        vmem((L, chips, NR, U2), BF16),
        vmem((L, 4, 2, NR, U), F32),
        vmem((L + 1, 2, NR, U), F32),
        vmem((L, NR, VP), BF16),
        vmem((L, NR, VP), BF16),
        vmem((NR, 128), F32),
        vmem((8, VP), F32),
        vmem((2, NR, U), F32),
        vmem((2, NR, U), F32),
        vmem((2, 2, 4, NR, U), BF16),
        vmem((L, 4, NR, U), BF16),
        vmem((2, peers, NR, U2), BF16),
        vmem((2, peers, NR, U2), BF16),
        vmem((4, H, U), F32),
        vmem((4, EP, U), F32),
        vmem((VP, EP), F32),
        vmem((max(VP, N_DEC), U), F32),
        vmem((N_DEC, U), BF16),
        vmem((groups, N_DEC // RR, U), BF16),
        vmem((2, N_DEC, 2 * U), BF16),
        vmem((N_IN, U), BF16),
        vmem((groups, N_IN // RR, U), BF16),
        vmem((2, N_IN, 2 * U), BF16),
        vmem((groups, 4, 4, KR, U), BF16),
        vmem((VS, 128), F32),
        vmem((2, VS // 2, 128), F32),
        vmem((stages, VS // 2, 128), F32),
        vmem((2, VS, 128), F32),
        sem((4,)),
        sem((3,)), sem((3,)),
        sem((1,)), sem((1,)),
        sem((1,)), sem((1,)),
        sem((along,)), sem((along,)),
        sem((Hy,)), sem((Hy,)),
        sem((3, pieces)), sem((3, pieces)),
        sem((4, groups, pieces)), sem((4, groups, pieces)),
        sem((4, RR, pieces)), sem((4, RR, pieces)),
        sem((1,)), sem((1,)),
        sem((2, BATCHES, peers)), sem((2, BATCHES, peers)),
        sem((L,)), sem((L,)),
        sem((L,)), sem((L,)),
        sem((2, BATCHES, peers)), sem((2, BATCHES, peers)),
        sem((L,)), sem((L,)),
        sem((2, 2 * groups + 3)),
        sem((2, 2 * groups + 3)),
        sem((groups, 4, pieces)), sem((groups, 4, pieces)),
        sem((4, pieces)), sem((4, pieces)),
        sem((stages + 2,)), sem((stages + 2,)),
    ]
    rows = NR * L
    flops = 2 * rows * (3 * H * 8 * U + 3 * H * VP)
    return pl.pallas_call(
        functools.partial(kernel, dims),
        out_shape=(
            jax.ShapeDtypeStruct((2, 4, KR, 2 * U), BF16),
            jax.ShapeDtypeStruct((2, N_IN, 2 * U), BF16),
            jax.ShapeDtypeStruct((2, N_DEC, 2 * U), BF16),
            jax.ShapeDtypeStruct((2, VS, 128), F32),
        ),
        in_specs=[inside] * 4 + [apart] * 3 + [inside] * 3,
        out_specs=(apart, apart, apart, apart),
        scratch_shapes=scratch,
        cost_estimate=pl.CostEstimate(flops=flops, bytes_accessed=8 << 20, transcendentals=rows * U2 * 8),
        compiler_params=pltpu.CompilerParams(
            collective_id=0, has_side_effects=True, vmem_limit_bytes=62 << 20
        ),
        name="train_step",
    )(*operands)


def local(
    char_ids, lang_ids, vocab_masks, targets, embedding, w_in, w_rec, b_in, b_rec, w_dec, b_dec
):
    R, hid = lax.axis_size("rows"), lax.axis_size("hid")
    RL, L = char_ids.shape
    E, units = w_in.shape[1], w_in.shape[3]
    V = embedding.shape[1]
    KR = w_rec.shape[1]
    U = units // 2
    dims = Dims(
        R=R, RR=R // 4, Hy=hid // 2, H=units * hid, KR=KR, U=U, RL=RL, L=L, V=V, E=E,
        LANGS=vocab_masks.shape[0], scale=1.0 / (RL * R * L),
    )
    VP, EP, EW = dims.VP, dims.EP, dims.EW

    bias = b_in.astype(F32) + b_rec.astype(F32)
    win = jnp.pad(w_in.transpose(0, 2, 1, 3), ((0, 0), (0, 0), (0, EP - E), (0, 0)))
    wrec = w_rec.transpose(0, 2, 1, 3)
    wdec = jnp.pad(w_dec, ((0, 0), (0, 0), (0, VP - V))).reshape(2, 2, U, VP)
    emb = jnp.concatenate([embedding, jnp.ones((2, V, 1), BF16)], axis=2)
    emb = jnp.pad(emb, ((0, 0), (0, VP - V), (0, EP - E - 1)))
    bdec = jnp.pad(b_dec.astype(F32), ((0, 0), (0, VP - V)))[:, None, :]
    lang_rows = ceil_to(dims.LANGS, 16)
    mask = jnp.pad(vocab_masks.astype(BF16), ((0, lang_rows - dims.LANGS), (0, VP - V)))

    grec, gwin, gwd, small = call_kernel(
        dims, char_ids.T, targets.transpose(0, 2, 1), lang_ids[None], bias, win, wrec, wdec, emb, bdec, mask
    )

    grad_w_rec = grec.astype(F32).transpose(0, 2, 1, 3)
    gwin = gwin[:, : 4 * EW].reshape(2, 4, EW, units).astype(F32)
    grad_w_in = gwin[:, :, :E].transpose(0, 2, 1, 3)
    grad_bias = gwin[:, :, E]
    grad_w_dec = gwd[:, :V].astype(F32).transpose(0, 2, 1)
    V8 = dims.V8
    grad_embedding = small[:, :V, :E]
    grad_b_dec = small[:, V8 : V8 + VP // 128].reshape(2, VP)[:, :V]
    total_loss = jnp.sum(small[:, V8 + VP // 128, 0])
    return (
        total_loss,
        grad_embedding,
        grad_w_in,
        grad_w_rec,
        grad_bias,
        grad_bias,
        grad_w_dec,
        grad_b_dec,
    )


def solution(mesh):
    placed = (
        P("rows", None),
        P("rows"),
        P(),
        P(None, "rows", None),
        P(),
        P(None, None, None, "hid"),
        P(None, "rows", None, "hid"),
        P(None, None, "hid"),
        P(None, None, "hid"),
        P(None, "hid", None),
        P(),
    )
    return jax.shard_map(
        local,
        mesh=mesh,
        in_specs=placed,
        out_specs=(
            P(),
            P(),
            P(None, None, None, "hid"),
            P(None, "rows", None, "hid"),
            P(None, None, "hid"),
            P(None, None, "hid"),
            P(None, "hid", None),
            P(),
        ),
        check_vma=False,
    )
```

```python
import functools
from typing import NamedTuple

import jax
import jax.numpy as jnp
from jax import lax
from jax.experimental import pallas as pl
from jax.experimental.pallas import tpu as pltpu
from jax.sharding import PartitionSpec as P

MESH = pl.DeviceIdType.MESH
F32 = jnp.float32
BF16 = jnp.bfloat16
masked_value = -1000000000.0
ROW_PARTS = 2
AHEAD = 8
EARLY = 2
WINDOW = 2
BATCHES = 2


def ceil_to(n, m):
    return (n + m - 1) // m * m


class Dims(NamedTuple):
    R: int
    RR: int
    Hy: int
    H: int
    KR: int
    U: int
    RL: int
    L: int
    V: int
    E: int
    LANGS: int
    scale: float

    @property
    def U2(self):
        return 2 * self.U

    @property
    def NR(self):
        return 2 * self.RL

    @property
    def VP(self):
        return ceil_to(self.V, 128)

    @property
    def RB(self):
        return self.NR // BATCHES

    @property
    def QN(self):
        return 1 if self.RR <= 2 else 4

    @property
    def KP(self):
        return ROW_PARTS if self.RR <= 2 else 1

    @property
    def pieces(self):
        return 4 // self.QN * self.KP

    @property
    def KRP(self):
        return self.KR // self.KP

    @property
    def N_IN(self):
        return ceil_to(4 * self.EW, 16 * self.RR)

    @property
    def N_DEC(self):
        return ceil_to(self.V, 16 * self.RR)

    @property
    def P8(self):
        return ceil_to(self.L, 8)

    @property
    def EP(self):
        return ceil_to(self.E + 2, 128)

    @property
    def EW(self):
        return ceil_to(self.E + 2, 16)

    @property
    def V8(self):
        return ceil_to(self.V, 8)

    @property
    def VS(self):
        return ceil_to(self.V8 + 8, 16)

    @property
    def peers(self):
        far = [(1, k) for k in range(1, self.Hy)]
        beside = [(0, k) for k in range(1, self.Hy)]
        return far + beside + [(1, 0)]


Z_STEPS = ((1, 0), (1, 1), (0, 1))


def dot(a, b):
    return jnp.dot(a, b, preferred_element_type=F32)


def dot_nt(a, b):
    return lax.dot_general(a, b, (((1,), (1,)), ((), ())), preferred_element_type=F32)


def dot_tn(a, b):
    return lax.dot_general(a, b, (((0,), (0,)), ((), ())), preferred_element_type=F32)


def flip(bit, step):
    return 1 - bit if step else bit


def kernel(
    dims,
    chars_ref, targets_ref, lang_ref, b_in_ref, b_rec_ref, win_in, wrec_in, wdec_in, emb_ref, b_dec_ref, masks_ref,
    grec_out, gwin_out, gwd_out, small_out,
    idsrc, idsall, idtmp, ids, bdec, masks, bias, win, W, wd, x, xp, allowed, acc, st, stp, gs, cell, lg, lgp, lossv, gb,
    dh, cg, pg, pgx, psend, precv, dW, gwin, gemb, gwd, gwd_s, gwd_r, gwd_all, gwin_s, gwin_r, gwin_all,
    recvB, epart, esend, erecv, eall,
    lsem, ids_s, ids_r, win_s2, win_r2, bias_s, bias_r, wdy_s, wdy_r, wdc_s, wdc_r, wz_s, wz_r, wx_s, wx_r, wc_s, wc_r,
    xp_s, xp_r, f_s, f_r, stp_s, stp_r, lgp_s, lgp_r, b_s, b_r, pgx_s, pgx_r,
    gwd_sems, gwin_sems, B_s, B_r, C_s, C_r, e_s, e_r,
):
    R, RR, Hy, U, U2, NR, L, VP = dims.R, dims.RR, dims.Hy, dims.U, dims.U2, dims.NR, dims.L, dims.VP
    KR, EW, V8, VS, RL, RB, QN = dims.KR, dims.EW, dims.V8, dims.VS, dims.RL, dims.RB, dims.QN
    peers = dims.peers
    KP, KRP, pieces = dims.KP, dims.KRP, dims.pieces
    rho, hid = lax.axis_index("rows"), lax.axis_index("hid")
    d, g, r = rho // (R // 2), lax.rem(rho // RR, 2), lax.rem(rho, RR)
    y, c = hid // 2, lax.rem(hid, 2)
    mine = y * 2 + g
    part = d * 2 + g

    def dev(dd, gg, rr, yy, cc):
        return (dd * (R // 2) + gg * RR + rr, yy * 2 + cc)

    def copy_to(src, dst, send, recv, device):
        return pltpu.make_async_remote_copy(
            src_ref=src, dst_ref=dst, send_sem=send, recv_sem=recv, device_id=device, device_id_type=MESH
        )

    def add_r(step):
        return lax.rem(r + step, RR)

    def add_y(step):
        return lax.rem(y + step, Hy)

    def place_of(dd, gg, rr):
        index = dd * (R // 2) + gg * RR + rr
        per = U // KR
        block = index // per
        hid_of, g_of = block // 2, lax.rem(block, 2)
        return (hid_of // 2) * 2 + g_of, lax.rem(hid_of, 2) * U + lax.rem(index, per) * KR

    def rows_of(dd, gg, rr, n=None):
        chip, unit = place_of(dd, gg, rr)
        row = chip * U2 + unit
        if n is None:
            return pl.ds(pl.multiple_of(row, KR), KR)
        return pl.ds(pl.multiple_of(row + n % KP * KRP, KRP), KRP)

    def rows_in(n):
        return pl.ds(n % KP * KRP, KRP)

    def chip_rows(m):
        return pl.ds(pl.multiple_of(m * U2, U2), U2)

    partner = dev(d, g, r, y, 1 - c)
    half = pl.ds(pl.multiple_of(g * U, U), U)

    def z_dev(j):
        return dev(flip(d, Z_STEPS[j][0]), flip(g, Z_STEPS[j][1]), r, y, c)

    def r_dev(step):
        return dev(d, g, add_r(step), y, c)

    def y_dev(step):
        return dev(d, g, r, add_y(step), c)

    def peer_dev(p):
        return dev(d, flip(g, peers[p][0]), r, add_y(peers[p][1]), c)

    barrier = pltpu.get_barrier_semaphore()
    greeted = [z_dev(j) for j in range(3)] + [r_dev(k) for k in range(1, RR)] + [partner]
    greeted += [peer_dev(p) for p in range(len(peers)) if peers[p] != (1, 0)]
    for device in greeted:
        pl.semaphore_signal(barrier, inc=1, device_id=device, device_id_type=MESH)
    pl.semaphore_wait(barrier, len(greeted))

    def ids_copy(j):
        return copy_to(idsrc.at[flip(d, Z_STEPS[j][0])], idsall.at[part], ids_s.at[j], ids_r.at[j], z_dev(j))

    def gates_of(n):
        return pl.ds(n // KP * QN, QN)

    def wz_copy(j, n):
        columns = pl.ds(pl.multiple_of(flip(g, Z_STEPS[j][1]) * U, U), U)
        there = wrec_in.at[flip(d, Z_STEPS[j][0]), gates_of(n), rows_in(n), columns]
        return copy_to(there, W.at[c, gates_of(n), rows_of(d, g, r, n), :], wz_s.at[j], wz_r.at[j, n], z_dev(j))

    def z_block(j):
        steps = Z_STEPS[j] if j < 3 else (0, 0)
        return flip(d, steps[0]), flip(g, steps[1])

    def w_block(core, j, k, n):
        dd, gg = z_block(j)
        return W.at[core, gates_of(n), rows_of(dd, gg, lax.rem(r + RR - k, RR), n), :]

    def wx_copy(j, k, n):
        block = w_block(c, j, 0, n)
        return copy_to(block, block, wx_s.at[k - 1], wx_r.at[j, k - 1, n], r_dev(k))

    def wc_copy(j, k, n):
        block = w_block(c, j, k, n)
        return copy_to(block, block, wc_s.at[0], wc_r.at[0], partner)

    def wc_all(core):
        return copy_to(W.at[core], W.at[core], wc_s.at[0], wc_r.at[0], partner)

    def wd_rows(yy):
        return wd.at[pl.ds(yy * 2, 2), c]

    def wdy_copy(k):
        return copy_to(wdec_in.at[d], wd_rows(y), wdy_s.at[k - 1], wdy_r.at[k - 1], y_dev(k))

    def wdc_copy(k):
        yy = lax.rem(y + Hy - k, Hy)
        return copy_to(wd_rows(yy), wd_rows(yy), wdc_s.at[k], wdc_r.at[k], partner)

    win_copy = copy_to(win_in.at[d, :, :, half], win.at[c], win_s2.at[0], win_r2.at[0], partner)
    bias_copy = copy_to(bias.at[c], bias.at[c], bias_s.at[0], bias_r.at[0], partner)
    own_win = pltpu.make_async_copy(win_in.at[d, :, :, half], win.at[c], lsem.at[1])
    own_wd = pltpu.make_async_copy(wdec_in.at[d], wd_rows(y), lsem.at[2])
    own_w = pltpu.make_async_copy(
        wrec_in.at[d, :, :, half], W.at[c, :, rows_of(d, g, r), :], lsem.at[3]
    )

    own_w.start()
    for n in range(min(WINDOW, pieces)):
        for j in range(3):
            wz_copy(j, n).start()
    own_win.start()
    win_copy.start()
    for k in range(1, Hy):
        wdy_copy(k).start()
    own_wd.start()

    P8 = dims.P8
    idsrc[...] = jnp.zeros_like(idsrc)
    for dd in range(2):
        idsrc[dd, 0:L, 0:RL] = chars_ref[...].astype(F32)
        idsrc[dd, P8 : P8 + L, 0:RL] = targets_ref[dd].astype(F32)
        idsrc[dd, 2 * P8 : 2 * P8 + 8, 0:RL] = jnp.broadcast_to(lang_ref[...].astype(F32), (8, RL))
    for j in range(3):
        ids_copy(j).start()
    bias[c, 0:4] = b_in_ref[d, :, half].astype(F32) + b_rec_ref[d, :, half].astype(F32)
    bias_copy.start()
    idsall[part] = idsrc[d]

    own_w.wait()
    for n in range(pieces):
        for k in range(1, RR):
            wx_copy(3, k, n).start()
        wc_copy(3, 0, n).start()

    dW[...] = jnp.zeros_like(dW)
    gwin[...] = jnp.zeros_like(gwin)
    gemb[...] = jnp.zeros_like(gemb)
    lossv[...] = jnp.zeros_like(lossv)
    gb[...] = jnp.zeros_like(gb)
    cg[...] = jnp.zeros_like(cg)
    cell[0] = jnp.zeros_like(cell[0])
    bdec[...] = jnp.zeros_like(bdec)
    bdec[0:2, 0 : dims.V] = b_dec_ref[...].astype(F32)
    masks[...] = jnp.zeros_like(masks)
    masks[0 : dims.LANGS, 0 : dims.V] = masks_ref[...].astype(F32)
    idtmp[...] = jnp.zeros_like(idtmp)

    for j in range(3):
        ids_copy(j).wait_recv()
    for n in range(4):
        idtmp[:, 0 : idsall.shape[1]] = idsall[n].T
        ids[n] = idtmp[pl.ds(pl.multiple_of(c * (RL // 2), RL // 2), RL // 2), :]

    lane = lax.broadcasted_iota(jnp.int32, (NR, 128), 1)
    vocab = lax.broadcasted_iota(jnp.int32, (NR, VP), 1).astype(F32)

    def id_column(at):
        held = ids[...].reshape(NR, 128)
        return jnp.sum(jnp.where(lane == at, held, 0.0), axis=1, keepdims=True)

    def place(t):
        return t + d * (L - 1 - 2 * t)

    def char_hot(t):
        return jnp.where(vocab == id_column(place(t)), 1.0, 0.0).astype(BF16)

    lang_lane = lax.broadcasted_iota(jnp.int32, (NR, masks.shape[0]), 1).astype(F32)
    lang_hot = jnp.where(lang_lane == id_column(2 * P8), 1.0, 0.0).astype(BF16)
    allowed[...] = dot(lang_hot, masks[...].astype(BF16))

    @pl.loop(0, L)
    def _(t):
        x[t] = dot(char_hot(t), emb_ref[d]).astype(BF16)

    xp_copy = copy_to(x, xp, xp_s.at[0], xp_r.at[0], partner)
    xp_copy.start()

    own_wd.wait()
    wdc_copy(0).start()
    own_win.wait()
    win_copy.wait_recv()
    bias_copy.wait_recv()

    def part_rows(b):
        return pl.ds(b * RB, RB)

    def f_copy(t, b, p):
        slot = lax.rem(t, 2)
        block = st.at[t, mine, part_rows(b), :]
        return copy_to(block, block, f_s.at[slot, b, p], f_r.at[slot, b, p], peer_dev(p))

    def gates(t, b):
        rows = part_rows(b)
        for cc in range(2):
            si = jax.nn.sigmoid(acc[cc, 0])
            sf = jax.nn.sigmoid(acc[cc, 1])
            tg = jnp.tanh(acc[cc, 2])
            so = jax.nn.sigmoid(acc[cc, 3])
            new = sf * cell[t, cc, rows] + si * tg
            cell[t + 1, cc, rows] = new
            st[t, mine, rows, cc * U : (cc + 1) * U] = (so * jnp.tanh(new)).astype(BF16)
            gs[t, 0, cc, rows] = si
            gs[t, 1, cc, rows] = sf
            gs[t, 2, cc, rows] = tg
            gs[t, 3, cc, rows] = so

    def peer_block(p):
        yy = lax.rem(y + Hy - peers[p][1], Hy)
        return yy * 2 + flip(g, peers[p][0])

    for b in range(BATCHES):
        for cc in range(2):
            for q in range(4):
                acc[cc, q] = dot(x[0, part_rows(b)], win[cc, q]) + bias[cc, q : q + 1]
        gates(0, b)
        for p in range(len(peers)):
            f_copy(0, b, p).start()

    for k in range(1, Hy):
        wdy_copy(k).wait_recv()
        wdc_copy(k).start()
    from_z, beside = [], [(2, n) for n in range(pieces)]
    for n in range(pieces):
        from_z += beside[2 * n : 2 * n + 2] + [(0, n), (1, n)]
    from_x = [(3, n) for n in range(pieces)] + from_z
    for at in range(len(from_x)):
        if at < len(from_z):
            j, n = from_z[at]
            wz_copy(j, n).wait_recv()
            for k in range(1, RR):
                wx_copy(j, k, n).start()
            wc_copy(j, 0, n).start()
            if n + WINDOW < pieces:
                wz_copy(j, n + WINDOW).start()
        j, n = from_x[at]
        for k in range(1, RR):
            wx_copy(j, k, n).wait_recv()
            wc_copy(j, k, n).start()
    wc_all(1 - c).wait_recv()
    for k in range(Hy):
        yy = lax.rem(y + Hy - k, Hy)
        other = wd.at[pl.ds(yy * 2, 2), 1 - c]
        copy_to(other, other, wdc_s.at[k], wdc_r.at[k], partner).wait_recv()

    def stp_copy(t):
        return copy_to(st.at[t], stp.at[t], stp_s.at[t], stp_r.at[t], partner)

    def lgp_copy(t):
        return copy_to(lg.at[t], lgp.at[t], lgp_s.at[t], lgp_r.at[t], partner)

    def decode(t):
        stp_copy(t).start()
        logits = bdec[pl.ds(d, 1), :]
        for m in range(2 * Hy):
            logits = logits + dot(st[t, m], wd[m].reshape(U2, VP))
        masked = jnp.where(allowed[...] > 0.5, logits, masked_value)
        top = jnp.max(masked, axis=1, keepdims=True)
        powers = jnp.exp(masked - top)
        total = jnp.sum(powers, axis=1, keepdims=True)
        hot = vocab == id_column(P8 + place(t))
        picked = jnp.sum(jnp.where(hot, logits, 0.0), axis=1, keepdims=True)
        lossv[...] += jnp.broadcast_to(top + jnp.log(total) - picked, (NR, 128))
        grad = ((powers / total - jnp.where(hot, 1.0, 0.0)) * dims.scale).astype(BF16)
        lg[t] = grad
        gb[0:1, :] += jnp.sum(grad.astype(F32), axis=0, keepdims=True)
        lgp_copy(t).start()

    @pl.loop(1, L)
    def _(t):
        for b in range(BATCHES):
            rows = part_rows(b)
            for cc in range(2):
                for q in range(4):
                    start = dot(x[t, rows], win[cc, q]) + bias[cc, q : q + 1]
                    acc[cc, q] = start + dot(st[t - 1, mine, rows], W[cc, q, chip_rows(mine), :])
            for p in reversed(range(len(peers))):
                f_copy(t - 1, b, p).wait_recv()
                m = peer_block(p)
                for cc in range(2):
                    for q in range(4):
                        acc[cc, q] += dot(st[t - 1, m, rows], W[cc, q, chip_rows(m), :])
            gates(t, b)
            for p in range(len(peers)):
                f_copy(t - 1, b, p).wait_send()
            for p in range(len(peers)):
                f_copy(t, b, p).start()
        decode(t - 1)

    block = wrec_in.at[d, :, :, half]
    for j in range(3):
        copy_to(block, block, wz_s.at[j], wz_r.at[j, 0], z_dev(j)).wait_send()
    blocks = W.at[c, :, 0 : 4 * KR, :]
    for k in range(1, RR):
        copy_to(blocks, blocks, wx_s.at[k - 1], wx_r.at[0, k - 1, 0], r_dev(k)).wait_send()
    wc_all(c).wait_send()

    @pl.loop(0, dims.H // U)
    def _(k):
        rows = pl.ds(pl.multiple_of(k * U, U), U)
        for cc in range(2):
            for q in range(4):
                W[cc, q, rows, :] = W[cc, q, rows, :].T

    for b in range(BATCHES):
        for p in reversed(range(len(peers))):
            f_copy(L - 1, b, p).wait_recv()
    decode(L - 1)

    def dec_back(t, cc):
        return dot_nt(lg[t], wd[mine, cc])

    def b_copy(t, b, p):
        slot = lax.rem(t, 2)
        there = precv.at[slot, p, part_rows(b), :]
        return copy_to(
            psend.at[slot, p, part_rows(b), :], there, b_s.at[slot, b, p], b_r.at[slot, b, p], peer_dev(p)
        )

    def pgx_copy(t):
        return copy_to(pg.at[lax.rem(t, 2), 1 - c], pgx.at[t], pgx_s.at[t], pgx_r.at[t], partner)

    def preact_grads(t, b):
        slot = lax.rem(t, 2)
        rows = part_rows(b)
        for cc in range(2):
            h = dh[cc, rows]
            si, sf, tg, so = (gs[t, q, cc, rows] for q in range(4))
            tc = jnp.tanh(cell[t + 1, cc, rows])
            total = cg[cc, rows] + h * so * (1.0 - tc * tc)
            pg[slot, cc, 0, rows] = (total * tg * si * (1.0 - si)).astype(BF16)
            pg[slot, cc, 1, rows] = (total * cell[t, cc, rows] * sf * (1.0 - sf)).astype(BF16)
            pg[slot, cc, 2, rows] = (total * si * (1.0 - tg * tg)).astype(BF16)
            pg[slot, cc, 3, rows] = (h * tc * so * (1.0 - so)).astype(BF16)
            cg[cc, rows] = total * sf

    def partial(t, b, m, cc):
        slot = lax.rem(t, 2)
        rows = pl.ds(pl.multiple_of(m * U2 + cc * U, U), U)
        total = None
        for kk in range(2):
            for q in range(4):
                term = dot(pg[slot, kk, q, part_rows(b)], W[kk, q, rows, :])
                total = term if total is None else total + term
        return total

    def take_state_grad(t, b):
        slot = lax.rem(t, 2)
        rows = part_rows(b)
        for p in reversed(range(len(peers))):
            b_copy(t, b, p).wait_recv()
            for cc in range(2):
                dh[cc, rows] += precv[slot, p, rows, cc * U : (cc + 1) * U].astype(F32)

    def both_cores(t, q):
        return jnp.concatenate([pg[lax.rem(t, 2), c, q], pgx[t, q]], axis=0)

    def rec_grads(t):
        for q in range(4):
            both = both_cores(t, q)
            for m in range(2 * Hy):
                states = jnp.concatenate([st[t - 1, m], stp[t - 1, m]], axis=0)
                dW[q, m * U2 : (m + 1) * U2, :] += dot_tn(states, both)

    def in_grads(t):
        slot = lax.rem(t, 2)
        inputs = jnp.concatenate([x[t], xp[t]], axis=0)
        for q in range(4):
            gwin[q] += dot_tn(inputs, both_cores(t, q))
        back = None
        for cc in range(2):
            for q in range(4):
                term = dot_nt(pg[slot, cc, q], win[cc, q])
                back = term if back is None else back + term
        high = back.astype(BF16)
        rest = (back - high.astype(F32)).astype(BF16)
        hot = char_hot(t)
        gemb[...] += dot_tn(hot, high) + dot_tn(hot, rest)

    class SmallSum:
        def __init__(self, send, recv, whole, out, sems, own_sem):
            self.send, self.recv, self.whole, self.out, self.sems, self.own = send, recv, whole, out, sems, own_sem
            self.share = whole.shape[1] // RR

        def rows(self, rr):
            return pl.ds(pl.multiple_of(rr * self.share, 16), self.share)

        def pair(self, at):
            return self.sems.at[0, at], self.sems.at[1, at]

        def first(self, k):
            return copy_to(self.send.at[self.rows(add_r(k)), :], self.recv.at[k - 1], *self.pair(k - 1), r_dev(k))

        def block(self, dd, gg):
            return self.whole.at[dd, self.rows(r), pl.ds(pl.multiple_of(gg * U, U), U)]

        def along(self, j):
            block = self.block(1 - d, g) if j == 1 else self.block(d, g)
            return copy_to(block, block, *self.pair(RR - 1 + j), z_dev(0 if j == 0 else 2))

        def last(self, k):
            block = self.whole.at[:, self.rows(r), :]
            return copy_to(block, block, *self.pair(RR + 2 + k - 1), r_dev(k))

        def to_out(self):
            return pltpu.make_async_copy(self.whole, self.out, self.own)

        def start(self):
            for k in range(1, RR):
                self.first(k).start()

        def add(self, value):
            for k in range(1, RR):
                self.first(k).wait_recv()
                value = value + self.recv[k - 1].astype(F32)
            self.whole[d, self.rows(r), half] = value.astype(BF16)
            self.along(0).start()
            self.along(2).start()

        def relay(self):
            self.along(0).wait_recv()
            self.along(1).start()

        def spread(self):
            self.along(2).wait_recv()
            self.along(1).wait_recv()
            for k in range(1, RR):
                self.last(k).start()

        def finish(self):
            for k in range(1, RR):
                self.last(k).wait_recv()
            self.to_out().start()

        def drain(self):
            for k in range(1, RR):
                self.first(k).wait_send()
                self.last(k).wait_send()
            for j in range(3):
                self.along(j).wait_send()
            self.to_out().wait()

    dec_sum = SmallSum(gwd_s, gwd_r, gwd_all, gwd_out, gwd_sems, lsem.at[0])
    in_sum = SmallSum(gwin_s, gwin_r, gwin_all, gwin_out, gwin_sems, lsem.at[1])

    def decoder_grad():
        gwd[...] = jnp.zeros_like(gwd)

        @pl.loop(0, L)
        def _(t):
            columns = pl.ds(pl.multiple_of(c * U, U), U)
            states = jnp.concatenate([st[t, mine, :, columns], stp[t, mine, :, columns]], axis=0)
            gwd[...] += dot_tn(jnp.concatenate([lg[t], lgp[t]], axis=0), states)

        gwd_s[...] = gwd[0 : dims.N_DEC].astype(BF16)
        dec_sum.start()

    for cc in range(2):
        dh[cc] = dec_back(L - 1, cc)

    @pl.loop(0, L)
    def _(t):
        stp_copy(t).wait()
        lgp_copy(t).wait()

    xp_copy.wait()

    @pl.loop(0, L - 1)
    def _(i):
        t = L - 1 - i
        slot = lax.rem(t, 2)

        @pl.when(i > 1)
        def _():
            pgx_copy(t + 2).wait_send()

        for b in range(BATCHES):
            rows = part_rows(b)

            @pl.when(i > 0)
            def _():
                take_state_grad(t + 1, b)

            @pl.when(i > 1)
            def _():
                for p in range(len(peers)):
                    b_copy(t + 2, b, p).wait_send()

            preact_grads(t, b)
            for p in range(len(peers)):
                m = add_y(peers[p][1]) * 2 + flip(g, peers[p][0])
                for cc in range(2):
                    psend[slot, p, rows, cc * U : (cc + 1) * U] = partial(t, b, m, cc).astype(BF16)
                b_copy(t, b, p).start()
            for cc in range(2):
                dh[cc, rows] = partial(t, b, mine, cc)
        pgx_copy(t).start()
        for cc in range(2):
            dh[cc] += dec_back(t - 1, cc)

        @pl.when(i > 0)
        def _():
            pgx_copy(t + 1).wait_recv()
            rec_grads(t + 1)
            in_grads(t + 1)

        @pl.when(i == 0)
        def _():
            decoder_grad()

        @pl.when(i == 1)
        def _():
            dec_sum.add(gwd[dec_sum.rows(r), :])

        @pl.when(i == 2)
        def _():
            dec_sum.relay()

        @pl.when(i == 3)
        def _():
            dec_sum.spread()

        @pl.when(i == 4)
        def _():
            dec_sum.finish()

    out_steps = ((1, 0), (1, 1), (0, 1), (0, 0))

    def out_device(i, step):
        return flip(d, out_steps[i][0]), flip(g, out_steps[i][1]), add_r(step)

    def out_rows(i, step, n):
        return rows_of(*out_device(i, step), n)

    def b_out(i, k, n):
        return copy_to(
            W.at[0, gates_of(n), out_rows(i, k, n), :], recvB.at[k - 1, i, gates_of(n), rows_in(n), :],
            B_s.at[k - 1], B_r.at[k - 1, i, n], r_dev(k),
        )

    def c_out(i, n):
        there = grec_out.at[d, gates_of(n), rows_in(n), half]
        return copy_to(W.at[1, gates_of(n), out_rows(i, 0, n), :], there, C_s.at[i], C_r.at[i], z_dev(i))

    def own_out(n):
        there = grec_out.at[d, gates_of(n), rows_in(n), half]
        return pltpu.make_async_copy(W.at[1, gates_of(n), out_rows(3, 0, n), :], there, C_s.at[3])

    def gates_in(n):
        return range(n // KP * QN, (n // KP + 1) * QN)

    fused = KRP % 128 == 0

    def rec_piece(i, step, n, q):
        total = dW[q, out_rows(i, step, n), :]
        if fused:
            chip, unit = place_of(*out_device(i, step))
            units = pl.ds(pl.multiple_of(unit + n % KP * KRP, 128), KRP)
            states = jnp.concatenate([st[0, chip, :, units], stp[0, chip, :, units]], axis=0)
            total = total + dot_tn(states, both_cores(1, q))
        return total

    steps = [(i, n) for n in range(pieces) for i in (0, 2, 1, 3)]

    def send_over(at):
        i, n = steps[at]
        for k in range(1, RR):
            for q in gates_in(n):
                W[0, q, out_rows(i, k, n), :] = rec_piece(i, k, n, q).astype(BF16)
            b_out(i, k, n).start()

    def send_home(at):
        i, n = steps[at]
        for k in range(1, RR):
            b_out(i, k, n).wait_recv()
        for q in gates_in(n):
            total = rec_piece(i, 0, n, q)
            for k in range(1, RR):
                total = total + recvB[k - 1, i, q, rows_in(n), :].astype(F32)
            W[1, q, out_rows(i, 0, n), :] = total.astype(BF16)
        if i < 3:
            c_out(i, n).start()
        else:
            own_out(n).start()
        if at + ahead < len(steps):
            send_over(at + ahead)

    pgx_copy(1).wait_recv()
    if not fused:
        rec_grads(1)
    ahead = min(AHEAD, len(steps))
    for at in range(ahead):
        send_over(at)
    in_grads(1)

    pgx_copy(2).wait_send()
    sent = 0
    for b in range(BATCHES):
        take_state_grad(1, b)
        preact_grads(0, b)
        for at in range(sent, min(sent + EARLY, len(steps))):
            send_home(at)
        sent = min(sent + EARLY, len(steps))
    pgx_copy(0).start()
    for at in range(sent, min(sent + EARLY, len(steps))):
        send_home(at)
    sent = min(sent + EARLY, len(steps))
    pgx_copy(0).wait_recv()
    in_grads(0)

    gwin_s[...] = jnp.zeros_like(gwin_s)
    for q in range(4):
        gwin_s[q * EW : (q + 1) * EW] = gwin[q, 0:EW].astype(BF16)
    in_sum.start()

    once = jnp.where(mine == 0, 1.0, 0.0).astype(F32)
    epart[0:V8] = gemb[0:V8]
    epart[V8:VS] = jnp.zeros((VS - V8, 128), F32)
    for k in range(VP // 128):
        epart[V8 + k : V8 + k + 1] = gb[0:1, k * 128 : (k + 1) * 128] * once
    at = V8 + VP // 128
    epart[at : at + 1] = jnp.sum(lossv[...], axis=0, keepdims=True) * (once * dims.scale)

    stages = [[partner], [peer_dev(p) for p in range(len(peers))], [r_dev(k) for k in range(1, RR)]]
    first = [sum(len(s) for s in stages[:n]) for n in range(len(stages) + 1)]

    def e_half(core):
        return pl.ds(pl.multiple_of(core * (VS // 2), 8), VS // 2)

    def e_copy(n, k):
        at = first[n] + k
        there = epart.at[e_half(1 - c), :] if n == 0 else esend.at[n - 1]
        return copy_to(there, erecv.at[at], e_s.at[at], e_r.at[at], stages[n][k])

    def e_start(n):
        for k in range(len(stages[n])):
            e_copy(n, k).start()

    def e_take(n):
        total = epart[e_half(c), :] if n == 0 else esend[n - 1]
        for k in range(len(stages[n])):
            e_copy(n, k).wait_recv()
            total = total + erecv[first[n] + k]
        if n < 2:
            esend[n] = total
            e_start(n + 1)
        else:
            eall[d, e_half(c), :] = total
            e_cross.start()

    e_cross = copy_to(
        eall.at[d, e_half(c), :], eall.at[d, e_half(c), :], e_s.at[first[3]], e_r.at[first[3]], z_dev(0)
    )
    e_core = copy_to(
        eall.at[:, e_half(c), :], eall.at[:, e_half(c), :], e_s.at[first[3] + 1], e_r.at[first[3] + 1], partner
    )
    own_small = pltpu.make_async_copy(eall, small_out, lsem.at[2])

    def in_share():
        in_f32 = jnp.concatenate([gwin[q, 0:EW] for q in range(4)], axis=0)
        if dims.N_IN > 4 * EW:
            in_f32 = jnp.concatenate([in_f32, jnp.zeros((dims.N_IN - 4 * EW, U), F32)], axis=0)
        share = in_sum.share
        total = in_f32[0:share]
        for k in range(1, RR):
            total = jnp.where(r == k, in_f32[k * share : (k + 1) * share], total)
        return total

    def e_gather():
        e_cross.wait_recv()
        e_core.start()

    def e_finish():
        e_core.wait_recv()
        own_small.start()

    e_start(0)
    between = [
        (0.05, lambda: e_take(0)),
        (0.2, lambda: in_sum.add(in_share())),
        (0.2, lambda: e_take(1)),
        (0.35, lambda: e_take(2)),
        (0.5, in_sum.relay),
        (0.6, e_gather),
        (0.7, in_sum.spread),
        (0.8, e_finish),
        (1.0, in_sum.finish),
    ]
    for at in range(sent, len(steps)):
        send_home(at)
        while between and (at + 1 - sent) >= between[0][0] * (len(steps) - sent):
            between.pop(0)[1]()
    for _, event in between:
        event()

    for j in range(3):
        ids_copy(j).wait_send()
    win_copy.wait_send()
    bias_copy.wait_send()
    for k in range(1, Hy):
        wdy_copy(k).wait_send()
    for k in range(Hy):
        wdc_copy(k).wait_send()
    for b in range(BATCHES):
        for p in range(len(peers)):
            f_copy(L - 1, b, p).wait_send()
            b_copy(2, b, p).wait_send()
            b_copy(1, b, p).wait_send()
    pgx_copy(1).wait_send()
    pgx_copy(0).wait_send()
    for n in range(3):
        for k in range(len(stages[n])):
            e_copy(n, k).wait_send()
    e_cross.wait_send()
    e_core.wait_send()
    dec_sum.drain()
    in_sum.drain()
    for k in range(1, RR):
        copy_to(W.at[0, :, 0 : 4 * KR, :], W.at[0, :, 0 : 4 * KR, :], B_s.at[k - 1], B_r.at[k - 1, 0, 0], r_dev(k)).wait_send()
    kept = grec_out.at[d, :, :, half]
    for i in range(3):
        copy_to(kept, kept, C_s.at[i], C_r.at[i], z_dev(i)).wait()
    pltpu.make_async_copy(kept, kept, C_s.at[3]).wait()
    own_small.wait()


def call_kernel(dims, *operands):
    R, RR, Hy, U, U2, NR, L, VP = dims.R, dims.RR, dims.Hy, dims.U, dims.U2, dims.NR, dims.L, dims.VP
    KR, EP, VS, H, RB, N_IN, N_DEC = dims.KR, dims.EP, dims.VS, dims.H, dims.RB, dims.N_IN, dims.N_DEC
    chips, peers, pieces = 2 * Hy, len(dims.peers), dims.pieces
    vmem, sem = pltpu.VMEM, pltpu.SemaphoreType.DMA
    apart = pl.BlockSpec(memory_space=pl.ANY)
    inside = pl.BlockSpec(memory_space=pltpu.VMEM)
    groups = max(RR - 1, 1)
    along = max(Hy - 1, 1)
    stages = 1 + peers + (RR - 1)
    id_rows = 2 * dims.P8 + 8
    scratch = [
        vmem((2, id_rows, 128), F32),
        vmem((4, id_rows, 128), F32),
        vmem((128, 128), F32),
        vmem((4, dims.RL // 2, 128), F32),
        vmem((8, VP), F32),
        vmem((ceil_to(dims.LANGS, 16), VP), F32),
        vmem((2, 8, U), F32),
        vmem((2, 4, EP, U), BF16),
        vmem((2, 4, H, U), BF16),
        vmem((chips, 2, U, VP), BF16),
        vmem((L, NR, EP), BF16),
        vmem((L, NR, EP), BF16),
        vmem((NR, VP), F32),
        vmem((2, 4, RB, U), F32),
        vmem((L, chips, NR, U2), BF16),
        vmem((L, chips, NR, U2), BF16),
        vmem((L, 4, 2, NR, U), F32),
        vmem((L + 1, 2, NR, U), F32),
        vmem((L, NR, VP), BF16),
        vmem((L, NR, VP), BF16),
        vmem((NR, 128), F32),
        vmem((8, VP), F32),
        vmem((2, NR, U), F32),
        vmem((2, NR, U), F32),
        vmem((2, 2, 4, NR, U), BF16),
        vmem((L, 4, NR, U), BF16),
        vmem((2, peers, NR, U2), BF16),
        vmem((2, peers, NR, U2), BF16),
        vmem((4, H, U), F32),
        vmem((4, EP, U), F32),
        vmem((VP, EP), F32),
        vmem((max(VP, N_DEC), U), F32),
        vmem((N_DEC, U), BF16),
        vmem((groups, N_DEC // RR, U), BF16),
        vmem((2, N_DEC, 2 * U), BF16),
        vmem((N_IN, U), BF16),
        vmem((groups, N_IN // RR, U), BF16),
        vmem((2, N_IN, 2 * U), BF16),
        vmem((groups, 4, 4, KR, U), BF16),
        vmem((VS, 128), F32),
        vmem((2, VS // 2, 128), F32),
        vmem((stages, VS // 2, 128), F32),
        vmem((2, VS, 128), F32),
        sem((4,)),
        sem((3,)), sem((3,)),
        sem((1,)), sem((1,)),
        sem((1,)), sem((1,)),
        sem((along,)), sem((along,)),
        sem((Hy,)), sem((Hy,)),
        sem((3,)), sem((3, pieces)),
        sem((groups,)), sem((4, groups, pieces)),
        sem((1,)), sem((1,)),
        sem((1,)), sem((1,)),
        sem((2, BATCHES, peers)), sem((2, BATCHES, peers)),
        sem((L,)), sem((L,)),
        sem((L,)), sem((L,)),
        sem((2, BATCHES, peers)), sem((2, BATCHES, peers)),
        sem((L,)), sem((L,)),
        sem((2, 2 * groups + 3)),
        sem((2, 2 * groups + 3)),
        sem((groups,)), sem((groups, 4, pieces)),
        sem((4,)), sem((3,)),
        sem((stages + 2,)), sem((stages + 2,)),
    ]
    rows = NR * L
    flops = 2 * rows * (3 * H * 8 * U + 3 * H * VP)
    return pl.pallas_call(
        functools.partial(kernel, dims),
        out_shape=(
            jax.ShapeDtypeStruct((2, 4, KR, 2 * U), BF16),
            jax.ShapeDtypeStruct((2, N_IN, 2 * U), BF16),
            jax.ShapeDtypeStruct((2, N_DEC, 2 * U), BF16),
            jax.ShapeDtypeStruct((2, VS, 128), F32),
        ),
        in_specs=[inside] * 5 + [apart] * 3 + [inside] * 3,
        out_specs=(apart, apart, apart, apart),
        scratch_shapes=scratch,
        cost_estimate=pl.CostEstimate(flops=flops, bytes_accessed=8 << 20, transcendentals=rows * U2 * 8),
        compiler_params=pltpu.CompilerParams(
            collective_id=0, has_side_effects=True, vmem_limit_bytes=62 << 20
        ),
        name="train_step",
    )(*operands)


def outputs_kernel(
    dims, grec, gwin, gwd, small, w_rec_out, w_in_out, b_in_out, b_rec_out, w_dec_out, emb_out, b_dec_out, loss_out
):
    for d in range(2):
        for q in range(4):
            w_rec_out[d, :, q, :] = grec[d, q].astype(F32)

    @pl.when(pl.program_id(0) == 0)
    def _():
        E, EW, V, V8 = dims.E, dims.EW, dims.V, dims.V8
        for d in range(2):
            for q in range(4):
                w_in_out[d, :, q, :] = gwin[d, q * EW : q * EW + E].astype(F32)
                first = q * EW + E // 16 * 16
                row = gwin[d, first : first + 16].astype(F32)[E % 16 : E % 16 + 1]
                b_in_out[d, q : q + 1, :] = row
                b_rec_out[d, q : q + 1, :] = row
            w_dec_out[:, d, :] = gwd[d, 0:V].astype(F32)
            emb_out[:, d, :] = small[d, 0:V, 0:E]
            for k in range(dims.VP // 128):
                width = min(128, V - k * 128)
                b_dec_out[d : d + 1, k * 128 : k * 128 + width] = small[d, V8 + k : V8 + k + 1, 0:width]
        at = V8 + dims.VP // 128
        loss_out[...] = small[0, at : at + 1, 0:1] + small[1, at : at + 1, 0:1]


def call_outputs(dims, grec, gwin, gwd, small):
    KR, U2, E, V = dims.KR, dims.U2, dims.E, dims.V
    parts = 4 if KR % 64 == 0 else 1
    rows = KR // parts

    def whole(*shape):
        return pl.BlockSpec(shape, lambda i: (0,) * len(shape))

    shapes = ((2, E, 4, U2), (2, 4, U2), (2, 4, U2), (V, 2, U2), (V, 2, E), (2, V), (1, 1))
    return pl.pallas_call(
        functools.partial(outputs_kernel, dims),
        grid=(parts,),
        out_shape=[jax.ShapeDtypeStruct((2, KR, 4, U2), F32)] + [jax.ShapeDtypeStruct(s, F32) for s in shapes],
        in_specs=[
            pl.BlockSpec((2, 4, rows, U2), lambda i: (0, 0, i, 0)),
            whole(*gwin.shape), whole(*gwd.shape), whole(*small.shape),
        ],
        out_specs=[pl.BlockSpec((2, rows, 4, U2), lambda i: (0, i, 0, 0))] + [whole(*s) for s in shapes],
        compiler_params=pltpu.CompilerParams(vmem_limit_bytes=62 << 20),
        name="outputs",
    )(grec, gwin, gwd, small)


def local(
    char_ids, lang_ids, vocab_masks, targets, embedding, w_in, w_rec, b_in, b_rec, w_dec, b_dec
):
    R, hid = lax.axis_size("rows"), lax.axis_size("hid")
    RL, L = char_ids.shape
    E, units = w_in.shape[1], w_in.shape[3]
    V = embedding.shape[1]
    KR = w_rec.shape[1]
    U = units // 2
    dims = Dims(
        R=R, RR=R // 4, Hy=hid // 2, H=units * hid, KR=KR, U=U, RL=RL, L=L, V=V, E=E,
        LANGS=vocab_masks.shape[0], scale=1.0 / (RL * R * L),
    )
    VP, EP, EW = dims.VP, dims.EP, dims.EW

    win = jnp.pad(w_in.transpose(0, 2, 1, 3), ((0, 0), (0, 0), (0, EP - E), (0, 0)))
    wrec = w_rec.transpose(0, 2, 1, 3)
    wdec = jnp.pad(w_dec, ((0, 0), (0, 0), (0, VP - V))).reshape(2, 2, U, VP)
    emb = jnp.concatenate([embedding, jnp.ones((2, V, 1), BF16)], axis=2)
    emb = jnp.pad(emb, ((0, 0), (0, VP - V), (0, EP - E - 1)))

    sums = call_kernel(
        dims, char_ids.T, targets.transpose(0, 2, 1), lang_ids[None], b_in, b_rec, win, wrec, wdec, emb, b_dec,
        vocab_masks,
    )
    w_rec_grad, w_in_grad, b_in_grad, b_rec_grad, w_dec_grad, emb_grad, b_dec_grad, loss = call_outputs(dims, *sums)
    return (
        loss[0, 0],
        emb_grad.transpose(1, 0, 2),
        w_in_grad,
        w_rec_grad,
        b_in_grad,
        b_rec_grad,
        w_dec_grad.transpose(1, 2, 0),
        b_dec_grad,
    )


def solution(mesh):
    placed = (
        P("rows", None),
        P("rows"),
        P(),
        P(None, "rows", None),
        P(),
        P(None, None, None, "hid"),
        P(None, "rows", None, "hid"),
        P(None, None, "hid"),
        P(None, None, "hid"),
        P(None, "hid", None),
        P(),
    )
    return jax.shard_map(
        local,
        mesh=mesh,
        in_specs=placed,
        out_specs=(
            P(),
            P(),
            P(None, None, None, "hid"),
            P(None, "rows", None, "hid"),
            P(None, None, "hid"),
            P(None, None, "hid"),
            P(None, "hid", None),
            P(),
        ),
        check_vma=False,
    )
```

```python
import functools
from typing import NamedTuple

import jax
import jax.numpy as jnp
from jax import lax
from jax.experimental import pallas as pl
from jax.experimental.pallas import tpu as pltpu
from jax.sharding import PartitionSpec as P

MESH = pl.DeviceIdType.MESH
F32 = jnp.float32
BF16 = jnp.bfloat16
masked_value = -1000000000.0
ROW_PARTS = 2
AHEAD = 8
EARLY = 2
WINDOW = 3
BATCHES = 2


def ceil_to(n, m):
    return (n + m - 1) // m * m


class Dims(NamedTuple):
    R: int
    RR: int
    Hy: int
    H: int
    KR: int
    U: int
    RL: int
    L: int
    V: int
    E: int
    LANGS: int
    scale: float

    @property
    def U2(self):
        return 2 * self.U

    @property
    def NR(self):
        return 2 * self.RL

    @property
    def VP(self):
        return ceil_to(self.V, 128)

    @property
    def RB(self):
        return self.NR // BATCHES

    @property
    def QN(self):
        return 1 if self.RR <= 2 else 4

    @property
    def KP(self):
        return ROW_PARTS if self.RR <= 2 else 1

    @property
    def pieces(self):
        return 4 // self.QN * self.KP

    @property
    def KRP(self):
        return self.KR // self.KP

    @property
    def N_IN(self):
        return ceil_to(4 * self.EW, 16 * self.RR)

    @property
    def N_DEC(self):
        return ceil_to(self.V, 16 * self.RR)

    @property
    def P8(self):
        return ceil_to(self.L, 8)

    @property
    def EP(self):
        return ceil_to(self.E + 2, 128)

    @property
    def EW(self):
        return ceil_to(self.E + 2, 16)

    @property
    def V8(self):
        return ceil_to(self.V, 8)

    @property
    def VS(self):
        return ceil_to(self.V8 + 8, 16)

    @property
    def peers(self):
        far = [(1, k) for k in range(1, self.Hy)]
        beside = [(0, k) for k in range(1, self.Hy)]
        return far + beside + [(1, 0)]


Z_STEPS = ((1, 0), (1, 1), (0, 1))


def dot(a, b):
    return jnp.dot(a, b, preferred_element_type=F32)


def dot_nt(a, b):
    return lax.dot_general(a, b, (((1,), (1,)), ((), ())), preferred_element_type=F32)


def dot_tn(a, b):
    return lax.dot_general(a, b, (((0,), (0,)), ((), ())), preferred_element_type=F32)


def flip(bit, step):
    return 1 - bit if step else bit


def kernel(
    dims,
    chars_ref, targets_ref, lang_ref, b_in_ref, b_rec_ref, win_in, wrec_in, wdec_in, emb_ref, b_dec_ref, masks_ref,
    grec_out, gwin_out, gwd_out, small_out,
    idsrc, idsall, idtmp, ids, bdec, masks, bias, win, W, wd, x, xp, allowed, acc, st, stp, gs, cell, lg, lgp, lossv, gb,
    dh, cg, pg, pgx, psend, precv, dW, gwin, gemb, gwd, gwd_s, gwd_r, gwd_all, gwin_s, gwin_r, gwin_all,
    recvB, epart, esend, erecv, eall,
    lsem, ids_s, ids_r, win_s2, win_r2, bias_s, bias_r, wdy_s, wdy_r, wdc_s, wdc_r, wz_s, wz_r, wx_s, wx_r, wc_s, wc_r,
    xp_s, xp_r, f_s, f_r, stp_s, stp_r, lgp_s, lgp_r, b_s, b_r, pgx_s, pgx_r,
    gwd_sems, gwin_sems, B_s, B_r, C_s, C_r, e_s, e_r,
):
    R, RR, Hy, U, U2, NR, L, VP = dims.R, dims.RR, dims.Hy, dims.U, dims.U2, dims.NR, dims.L, dims.VP
    KR, EW, V8, VS, RL, RB, QN = dims.KR, dims.EW, dims.V8, dims.VS, dims.RL, dims.RB, dims.QN
    peers = dims.peers
    KP, KRP, pieces = dims.KP, dims.KRP, dims.pieces
    rho, hid = lax.axis_index("rows"), lax.axis_index("hid")
    d, g, r = rho // (R // 2), lax.rem(rho // RR, 2), lax.rem(rho, RR)
    y, c = hid // 2, lax.rem(hid, 2)
    mine = y * 2 + g
    part = d * 2 + g

    def dev(dd, gg, rr, yy, cc):
        return (dd * (R // 2) + gg * RR + rr, yy * 2 + cc)

    def copy_to(src, dst, send, recv, device):
        return pltpu.make_async_remote_copy(
            src_ref=src, dst_ref=dst, send_sem=send, recv_sem=recv, device_id=device, device_id_type=MESH
        )

    def add_r(step):
        return lax.rem(r + step, RR)

    def add_y(step):
        return lax.rem(y + step, Hy)

    def place_of(dd, gg, rr):
        index = dd * (R // 2) + gg * RR + rr
        per = U // KR
        block = index // per
        hid_of, g_of = block // 2, lax.rem(block, 2)
        return (hid_of // 2) * 2 + g_of, lax.rem(hid_of, 2) * U + lax.rem(index, per) * KR

    def rows_of(dd, gg, rr, n=None):
        chip, unit = place_of(dd, gg, rr)
        row = chip * U2 + unit
        if n is None:
            return pl.ds(pl.multiple_of(row, KR), KR)
        return pl.ds(pl.multiple_of(row + n % KP * KRP, KRP), KRP)

    def rows_in(n):
        return pl.ds(n % KP * KRP, KRP)

    def chip_rows(m):
        return pl.ds(pl.multiple_of(m * U2, U2), U2)

    partner = dev(d, g, r, y, 1 - c)
    half = pl.ds(pl.multiple_of(g * U, U), U)

    def z_dev(j):
        return dev(flip(d, Z_STEPS[j][0]), flip(g, Z_STEPS[j][1]), r, y, c)

    def r_dev(step):
        return dev(d, g, add_r(step), y, c)

    def y_dev(step):
        return dev(d, g, r, add_y(step), c)

    def peer_dev(p):
        return dev(d, flip(g, peers[p][0]), r, add_y(peers[p][1]), c)

    barrier = pltpu.get_barrier_semaphore()
    greeted = [z_dev(j) for j in range(3)] + [r_dev(k) for k in range(1, RR)] + [partner]
    greeted += [peer_dev(p) for p in range(len(peers)) if peers[p] != (1, 0)]
    for device in greeted:
        pl.semaphore_signal(barrier, inc=1, device_id=device, device_id_type=MESH)
    pl.semaphore_wait(barrier, len(greeted))

    def ids_copy(j):
        return copy_to(idsrc.at[flip(d, Z_STEPS[j][0])], idsall.at[part], ids_s.at[j], ids_r.at[j], z_dev(j))

    def gates_of(n):
        return pl.ds(n // KP * QN, QN)

    def wz_copy(j, n):
        columns = pl.ds(pl.multiple_of(flip(g, Z_STEPS[j][1]) * U, U), U)
        there = wrec_in.at[flip(d, Z_STEPS[j][0]), gates_of(n), rows_in(n), columns]
        return copy_to(there, W.at[c, gates_of(n), rows_of(d, g, r, n), :], wz_s.at[j], wz_r.at[j, n], z_dev(j))

    def z_block(j):
        steps = Z_STEPS[j] if j < 3 else (0, 0)
        return flip(d, steps[0]), flip(g, steps[1])

    def w_block(core, j, k, n):
        dd, gg = z_block(j)
        return W.at[core, gates_of(n), rows_of(dd, gg, lax.rem(r + RR - k, RR), n), :]

    def wx_copy(j, k, n):
        block = w_block(c, j, 0, n)
        return copy_to(block, block, wx_s.at[k - 1], wx_r.at[j, k - 1, n], r_dev(k))

    def wc_copy(j, k, n):
        block = w_block(c, j, k, n)
        return copy_to(block, block, wc_s.at[0], wc_r.at[0], partner)

    def wc_all(core):
        return copy_to(W.at[core], W.at[core], wc_s.at[0], wc_r.at[0], partner)

    def wd_rows(yy):
        return wd.at[pl.ds(yy * 2, 2), c]

    def wdy_copy(k):
        return copy_to(wdec_in.at[d], wd_rows(y), wdy_s.at[k - 1], wdy_r.at[k - 1], y_dev(k))

    def wdc_copy(k):
        yy = lax.rem(y + Hy - k, Hy)
        return copy_to(wd_rows(yy), wd_rows(yy), wdc_s.at[k], wdc_r.at[k], partner)

    win_copy = copy_to(win_in.at[d, :, :, half], win.at[c], win_s2.at[0], win_r2.at[0], partner)
    bias_copy = copy_to(bias.at[c], bias.at[c], bias_s.at[0], bias_r.at[0], partner)
    own_win = pltpu.make_async_copy(win_in.at[d, :, :, half], win.at[c], lsem.at[1])
    own_wd = pltpu.make_async_copy(wdec_in.at[d], wd_rows(y), lsem.at[2])
    own_w = pltpu.make_async_copy(
        wrec_in.at[d, :, :, half], W.at[c, :, rows_of(d, g, r), :], lsem.at[3]
    )

    own_w.start()
    for n in range(min(WINDOW, pieces)):
        for j in range(3):
            wz_copy(j, n).start()
    own_win.start()
    win_copy.start()
    for k in range(1, Hy):
        wdy_copy(k).start()
    own_wd.start()

    P8 = dims.P8
    idsrc[...] = jnp.zeros_like(idsrc)
    for dd in range(2):
        idsrc[dd, 0:L, 0:RL] = chars_ref[...].astype(F32)
        idsrc[dd, P8 : P8 + L, 0:RL] = targets_ref[dd].astype(F32)
        idsrc[dd, 2 * P8 : 2 * P8 + 8, 0:RL] = jnp.broadcast_to(lang_ref[...].astype(F32), (8, RL))
    for j in range(3):
        ids_copy(j).start()
    bias[c, 0:4] = b_in_ref[d, :, half].astype(F32) + b_rec_ref[d, :, half].astype(F32)
    bias_copy.start()
    idsall[part] = idsrc[d]

    own_w.wait()
    for n in range(pieces):
        for k in range(1, RR):
            wx_copy(3, k, n).start()
        wc_copy(3, 0, n).start()

    dW[...] = jnp.zeros_like(dW)
    gwin[...] = jnp.zeros_like(gwin)
    gemb[...] = jnp.zeros_like(gemb)
    lossv[...] = jnp.zeros_like(lossv)
    gb[...] = jnp.zeros_like(gb)
    cg[...] = jnp.zeros_like(cg)
    cell[0] = jnp.zeros_like(cell[0])
    bdec[...] = jnp.zeros_like(bdec)
    bdec[0:2, 0 : dims.V] = b_dec_ref[...].astype(F32)
    masks[...] = jnp.zeros_like(masks)
    masks[0 : dims.LANGS, 0 : dims.V] = masks_ref[...].astype(F32)
    idtmp[...] = jnp.zeros_like(idtmp)

    for j in range(3):
        ids_copy(j).wait_recv()
    for n in range(4):
        idtmp[:, 0 : idsall.shape[1]] = idsall[n].T
        ids[n] = idtmp[pl.ds(pl.multiple_of(c * (RL // 2), RL // 2), RL // 2), :]

    lane = lax.broadcasted_iota(jnp.int32, (NR, 128), 1)
    vocab = lax.broadcasted_iota(jnp.int32, (NR, VP), 1).astype(F32)

    def id_column(at):
        held = ids[...].reshape(NR, 128)
        return jnp.sum(jnp.where(lane == at, held, 0.0), axis=1, keepdims=True)

    def place(t):
        return t + d * (L - 1 - 2 * t)

    def char_hot(t):
        return jnp.where(vocab == id_column(place(t)), 1.0, 0.0).astype(BF16)

    lang_lane = lax.broadcasted_iota(jnp.int32, (NR, masks.shape[0]), 1).astype(F32)
    lang_hot = jnp.where(lang_lane == id_column(2 * P8), 1.0, 0.0).astype(BF16)
    allowed[...] = dot(lang_hot, masks[...].astype(BF16))

    @pl.loop(0, L)
    def _(t):
        x[t] = dot(char_hot(t), emb_ref[d]).astype(BF16)

    xp_copy = copy_to(x, xp, xp_s.at[0], xp_r.at[0], partner)
    xp_copy.start()

    own_wd.wait()
    wdc_copy(0).start()
    own_win.wait()
    win_copy.wait_recv()
    bias_copy.wait_recv()

    def part_rows(b):
        return pl.ds(b * RB, RB)

    def f_copy(t, b, p):
        slot = lax.rem(t, 2)
        block = st.at[t, mine, part_rows(b), :]
        return copy_to(block, block, f_s.at[slot, b, p], f_r.at[slot, b, p], peer_dev(p))

    def gates(t, b):
        rows = part_rows(b)
        for cc in range(2):
            si = jax.nn.sigmoid(acc[cc, 0, rows])
            sf = jax.nn.sigmoid(acc[cc, 1, rows])
            tg = jnp.tanh(acc[cc, 2, rows])
            so = jax.nn.sigmoid(acc[cc, 3, rows])
            new = sf * cell[t, cc, rows] + si * tg
            cell[t + 1, cc, rows] = new
            st[t, mine, rows, cc * U : (cc + 1) * U] = (so * jnp.tanh(new)).astype(BF16)
            gs[t, 0, cc, rows] = si
            gs[t, 1, cc, rows] = sf
            gs[t, 2, cc, rows] = tg
            gs[t, 3, cc, rows] = so

    def peer_block(p):
        yy = lax.rem(y + Hy - peers[p][1], Hy)
        return yy * 2 + flip(g, peers[p][0])

    for cc in range(2):
        for q in range(4):
            acc[cc, q] = dot(x[0], win[cc, q]) + bias[cc, q : q + 1]
    for b in range(BATCHES):
        gates(0, b)
        for p in range(len(peers)):
            f_copy(0, b, p).start()

    for k in range(1, Hy):
        wdy_copy(k).wait_recv()
        wdc_copy(k).start()
    from_z, beside = [], [(2, n) for n in range(pieces)]
    for n in range(pieces):
        from_z += beside[2 * n : 2 * n + 2] + [(0, n), (1, n)]
    from_x = [(3, n) for n in range(pieces)] + from_z
    for at in range(len(from_x)):
        if at < len(from_z):
            j, n = from_z[at]
            wz_copy(j, n).wait_recv()
            for k in range(1, RR):
                wx_copy(j, k, n).start()
            wc_copy(j, 0, n).start()
            if n + WINDOW < pieces:
                wz_copy(j, n + WINDOW).start()
        j, n = from_x[at]
        for k in range(1, RR):
            wx_copy(j, k, n).wait_recv()
            wc_copy(j, k, n).start()
    wc_all(1 - c).wait_recv()
    for k in range(Hy):
        yy = lax.rem(y + Hy - k, Hy)
        other = wd.at[pl.ds(yy * 2, 2), 1 - c]
        copy_to(other, other, wdc_s.at[k], wdc_r.at[k], partner).wait_recv()

    def stp_copy(t):
        return copy_to(st.at[t], stp.at[t], stp_s.at[t], stp_r.at[t], partner)

    def lgp_copy(t):
        return copy_to(lg.at[t], lgp.at[t], lgp_s.at[t], lgp_r.at[t], partner)

    def decode(t):
        stp_copy(t).start()
        logits = bdec[pl.ds(d, 1), :]
        for m in range(2 * Hy):
            logits = logits + dot(st[t, m], wd[m].reshape(U2, VP))
        masked = jnp.where(allowed[...] > 0.5, logits, masked_value)
        top = jnp.max(masked, axis=1, keepdims=True)
        powers = jnp.exp(masked - top)
        total = jnp.sum(powers, axis=1, keepdims=True)
        hot = vocab == id_column(P8 + place(t))
        picked = jnp.sum(jnp.where(hot, logits, 0.0), axis=1, keepdims=True)
        lossv[...] += jnp.broadcast_to(top + jnp.log(total) - picked, (NR, 128))
        grad = ((powers / total - jnp.where(hot, 1.0, 0.0)) * dims.scale).astype(BF16)
        lg[t] = grad
        gb[0:1, :] += jnp.sum(grad.astype(F32), axis=0, keepdims=True)
        lgp_copy(t).start()

    @pl.loop(1, L)
    def _(t):
        for cc in range(2):
            for q in range(4):
                start = dot(x[t], win[cc, q]) + bias[cc, q : q + 1]
                acc[cc, q] = start + dot(st[t - 1, mine], W[cc, q, chip_rows(mine), :])
        for b in range(BATCHES):
            rows = part_rows(b)
            for p in reversed(range(len(peers))):
                f_copy(t - 1, b, p).wait_recv()
                m = peer_block(p)
                for cc in range(2):
                    for q in range(4):
                        acc[cc, q, rows] += dot(st[t - 1, m, rows], W[cc, q, chip_rows(m), :])
            gates(t, b)
            for p in range(len(peers)):
                f_copy(t - 1, b, p).wait_send()
            for p in range(len(peers)):
                f_copy(t, b, p).start()
        decode(t - 1)

    block = wrec_in.at[d, :, :, half]
    for j in range(3):
        copy_to(block, block, wz_s.at[j], wz_r.at[j, 0], z_dev(j)).wait_send()
    blocks = W.at[c, :, 0 : 4 * KR, :]
    for k in range(1, RR):
        copy_to(blocks, blocks, wx_s.at[k - 1], wx_r.at[0, k - 1, 0], r_dev(k)).wait_send()
    wc_all(c).wait_send()

    @pl.loop(0, dims.H // U)
    def _(k):
        rows = pl.ds(pl.multiple_of(k * U, U), U)
        for cc in range(2):
            for q in range(4):
                W[cc, q, rows, :] = W[cc, q, rows, :].T

    for b in range(BATCHES):
        for p in reversed(range(len(peers))):
            f_copy(L - 1, b, p).wait_recv()
    decode(L - 1)

    def dec_back(t, cc):
        return dot_nt(lg[t], wd[mine, cc])

    def b_copy(t, b, p):
        slot = lax.rem(t, 2)
        there = precv.at[slot, p, part_rows(b), :]
        return copy_to(
            psend.at[slot, p, part_rows(b), :], there, b_s.at[slot, b, p], b_r.at[slot, b, p], peer_dev(p)
        )

    def pgx_copy(t):
        return copy_to(pg.at[lax.rem(t, 2), 1 - c], pgx.at[t], pgx_s.at[t], pgx_r.at[t], partner)

    def preact_grads(t, b):
        slot = lax.rem(t, 2)
        rows = part_rows(b)
        for cc in range(2):
            h = dh[cc, rows]
            si, sf, tg, so = (gs[t, q, cc, rows] for q in range(4))
            tc = jnp.tanh(cell[t + 1, cc, rows])
            total = cg[cc, rows] + h * so * (1.0 - tc * tc)
            pg[slot, cc, 0, rows] = (total * tg * si * (1.0 - si)).astype(BF16)
            pg[slot, cc, 1, rows] = (total * cell[t, cc, rows] * sf * (1.0 - sf)).astype(BF16)
            pg[slot, cc, 2, rows] = (total * si * (1.0 - tg * tg)).astype(BF16)
            pg[slot, cc, 3, rows] = (h * tc * so * (1.0 - so)).astype(BF16)
            cg[cc, rows] = total * sf

    def partial(t, rows_here, m, cc):
        slot = lax.rem(t, 2)
        rows = pl.ds(pl.multiple_of(m * U2 + cc * U, U), U)
        total = None
        for kk in range(2):
            for q in range(4):
                term = dot(pg[slot, kk, q, rows_here], W[kk, q, rows, :])
                total = term if total is None else total + term
        return total

    def take_state_grad(t, b):
        slot = lax.rem(t, 2)
        rows = part_rows(b)
        for p in reversed(range(len(peers))):
            b_copy(t, b, p).wait_recv()
            for cc in range(2):
                dh[cc, rows] += precv[slot, p, rows, cc * U : (cc + 1) * U].astype(F32)

    def both_cores(t, q):
        return jnp.concatenate([pg[lax.rem(t, 2), c, q], pgx[t, q]], axis=0)

    def rec_grads(t):
        for q in range(4):
            both = both_cores(t, q)
            for m in range(2 * Hy):
                states = jnp.concatenate([st[t - 1, m], stp[t - 1, m]], axis=0)
                dW[q, m * U2 : (m + 1) * U2, :] += dot_tn(states, both)

    def in_grads(t):
        slot = lax.rem(t, 2)
        inputs = jnp.concatenate([x[t], xp[t]], axis=0)
        for q in range(4):
            gwin[q] += dot_tn(inputs, both_cores(t, q))
        back = None
        for cc in range(2):
            for q in range(4):
                term = dot_nt(pg[slot, cc, q], win[cc, q])
                back = term if back is None else back + term
        high = back.astype(BF16)
        rest = (back - high.astype(F32)).astype(BF16)
        hot = char_hot(t)
        gemb[...] += dot_tn(hot, high) + dot_tn(hot, rest)

    class SmallSum:
        def __init__(self, send, recv, whole, out, sems, own_sem):
            self.send, self.recv, self.whole, self.out, self.sems, self.own = send, recv, whole, out, sems, own_sem
            self.share = whole.shape[1] // RR

        def rows(self, rr):
            return pl.ds(pl.multiple_of(rr * self.share, 16), self.share)

        def pair(self, at):
            return self.sems.at[0, at], self.sems.at[1, at]

        def first(self, k):
            return copy_to(self.send.at[self.rows(add_r(k)), :], self.recv.at[k - 1], *self.pair(k - 1), r_dev(k))

        def block(self, dd, gg):
            return self.whole.at[dd, self.rows(r), pl.ds(pl.multiple_of(gg * U, U), U)]

        def along(self, j):
            block = self.block(1 - d, g) if j == 1 else self.block(d, g)
            return copy_to(block, block, *self.pair(RR - 1 + j), z_dev(0 if j == 0 else 2))

        def last(self, k):
            block = self.whole.at[:, self.rows(r), :]
            return copy_to(block, block, *self.pair(RR + 2 + k - 1), r_dev(k))

        def to_out(self):
            return pltpu.make_async_copy(self.whole, self.out, self.own)

        def start(self):
            for k in range(1, RR):
                self.first(k).start()

        def add(self, value):
            for k in range(1, RR):
                self.first(k).wait_recv()
                value = value + self.recv[k - 1].astype(F32)
            self.whole[d, self.rows(r), half] = value.astype(BF16)
            self.along(0).start()
            self.along(2).start()

        def relay(self):
            self.along(0).wait_recv()
            self.along(1).start()

        def spread(self):
            self.along(2).wait_recv()
            self.along(1).wait_recv()
            for k in range(1, RR):
                self.last(k).start()

        def finish(self):
            for k in range(1, RR):
                self.last(k).wait_recv()
            self.to_out().start()

        def drain(self):
            for k in range(1, RR):
                self.first(k).wait_send()
                self.last(k).wait_send()
            for j in range(3):
                self.along(j).wait_send()
            self.to_out().wait()

    dec_sum = SmallSum(gwd_s, gwd_r, gwd_all, gwd_out, gwd_sems, lsem.at[0])
    in_sum = SmallSum(gwin_s, gwin_r, gwin_all, gwin_out, gwin_sems, lsem.at[1])

    def decoder_grad():
        gwd[...] = jnp.zeros_like(gwd)

        @pl.loop(0, L)
        def _(t):
            columns = pl.ds(pl.multiple_of(c * U, U), U)
            states = jnp.concatenate([st[t, mine, :, columns], stp[t, mine, :, columns]], axis=0)
            gwd[...] += dot_tn(jnp.concatenate([lg[t], lgp[t]], axis=0), states)

        gwd_s[...] = gwd[0 : dims.N_DEC].astype(BF16)
        dec_sum.start()

    for cc in range(2):
        dh[cc] = dec_back(L - 1, cc)

    @pl.loop(0, L - 1)
    def _(i):
        t = L - 1 - i
        slot = lax.rem(t, 2)

        @pl.when(i > 1)
        def _():
            pgx_copy(t + 2).wait_send()

        for b in range(BATCHES):
            rows = part_rows(b)

            @pl.when(i > 0)
            def _():
                take_state_grad(t + 1, b)

            @pl.when(i > 1)
            def _():
                for p in range(len(peers)):
                    b_copy(t + 2, b, p).wait_send()

            preact_grads(t, b)
            for p in range(len(peers)):
                m = add_y(peers[p][1]) * 2 + flip(g, peers[p][0])
                for cc in range(2):
                    psend[slot, p, rows, cc * U : (cc + 1) * U] = partial(t, rows, m, cc).astype(BF16)
                b_copy(t, b, p).start()
        pgx_copy(t).start()
        for cc in range(2):
            dh[cc] = partial(t, pl.ds(0, NR), mine, cc) + dec_back(t - 1, cc)

        @pl.when(i > 0)
        def _():
            pgx_copy(t + 1).wait_recv()
            rec_grads(t + 1)

        @pl.when((i > 0) & (i < L - 2))
        def _():
            in_grads(t + 1)

        @pl.when(i == 0)
        def _():
            xp_copy.wait()

            @pl.loop(0, L)
            def _(at):
                stp_copy(at).wait()
                lgp_copy(at).wait()

            decoder_grad()

        @pl.when(i == 1)
        def _():
            dec_sum.add(gwd[dec_sum.rows(r), :])

        @pl.when(i == 2)
        def _():
            dec_sum.relay()

        @pl.when(i == 3)
        def _():
            dec_sum.spread()

        @pl.when(i == 4)
        def _():
            dec_sum.finish()

    out_steps = ((1, 0), (1, 1), (0, 1), (0, 0))

    def out_device(i, step):
        return flip(d, out_steps[i][0]), flip(g, out_steps[i][1]), add_r(step)

    def out_rows(i, step, n):
        return rows_of(*out_device(i, step), n)

    def b_out(i, k, n):
        return copy_to(
            W.at[0, gates_of(n), out_rows(i, k, n), :], recvB.at[k - 1, i, gates_of(n), rows_in(n), :],
            B_s.at[k - 1], B_r.at[k - 1, i, n], r_dev(k),
        )

    def c_out(i, n):
        there = grec_out.at[d, gates_of(n), rows_in(n), half]
        return copy_to(W.at[1, gates_of(n), out_rows(i, 0, n), :], there, C_s.at[i], C_r.at[i], z_dev(i))

    def own_out(n):
        there = grec_out.at[d, gates_of(n), rows_in(n), half]
        return pltpu.make_async_copy(W.at[1, gates_of(n), out_rows(3, 0, n), :], there, C_s.at[3])

    def gates_in(n):
        return range(n // KP * QN, (n // KP + 1) * QN)

    fused = KRP % 128 == 0

    def rec_piece(i, step, n, q):
        total = dW[q, out_rows(i, step, n), :]
        if fused:
            chip, unit = place_of(*out_device(i, step))
            units = pl.ds(pl.multiple_of(unit + n % KP * KRP, 128), KRP)
            states = jnp.concatenate([st[0, chip, :, units], stp[0, chip, :, units]], axis=0)
            total = total + dot_tn(states, both_cores(1, q))
        return total

    steps = [(i, n) for n in range(pieces) for i in (0, 2, 1, 3)]

    def send_over(at):
        i, n = steps[at]
        for k in range(1, RR):
            for q in gates_in(n):
                W[0, q, out_rows(i, k, n), :] = rec_piece(i, k, n, q).astype(BF16)
            b_out(i, k, n).start()

    def send_home(at):
        i, n = steps[at]
        for k in range(1, RR):
            b_out(i, k, n).wait_recv()
        for q in gates_in(n):
            total = rec_piece(i, 0, n, q)
            for k in range(1, RR):
                total = total + recvB[k - 1, i, q, rows_in(n), :].astype(F32)
            W[1, q, out_rows(i, 0, n), :] = total.astype(BF16)
        if i < 3:
            c_out(i, n).start()
        else:
            own_out(n).start()
        if at + ahead < len(steps):
            send_over(at + ahead)

    pgx_copy(1).wait_recv()
    if not fused:
        rec_grads(1)
    ahead = min(AHEAD, len(steps))
    for at in range(ahead):
        send_over(at)
    in_grads(2)
    in_grads(1)

    pgx_copy(2).wait_send()
    sent = 0
    for b in range(BATCHES):
        take_state_grad(1, b)
        preact_grads(0, b)
        for at in range(sent, min(sent + EARLY, len(steps))):
            send_home(at)
        sent = min(sent + EARLY, len(steps))
    pgx_copy(0).start()
    for at in range(sent, min(sent + EARLY, len(steps))):
        send_home(at)
    sent = min(sent + EARLY, len(steps))
    pgx_copy(0).wait_recv()
    in_grads(0)

    gwin_s[...] = jnp.zeros_like(gwin_s)
    for q in range(4):
        gwin_s[q * EW : (q + 1) * EW] = gwin[q, 0:EW].astype(BF16)
    in_sum.start()

    once = jnp.where(mine == 0, 1.0, 0.0).astype(F32)
    epart[0:V8] = gemb[0:V8]
    epart[V8:VS] = jnp.zeros((VS - V8, 128), F32)
    for k in range(VP // 128):
        epart[V8 + k : V8 + k + 1] = gb[0:1, k * 128 : (k + 1) * 128] * once
    at = V8 + VP // 128
    epart[at : at + 1] = jnp.sum(lossv[...], axis=0, keepdims=True) * (once * dims.scale)

    stages = [[partner], [peer_dev(p) for p in range(len(peers))], [r_dev(k) for k in range(1, RR)]]
    first = [sum(len(s) for s in stages[:n]) for n in range(len(stages) + 1)]

    def e_half(core):
        return pl.ds(pl.multiple_of(core * (VS // 2), 8), VS // 2)

    def e_copy(n, k):
        at = first[n] + k
        there = epart.at[e_half(1 - c), :] if n == 0 else esend.at[n - 1]
        return copy_to(there, erecv.at[at], e_s.at[at], e_r.at[at], stages[n][k])

    def e_start(n):
        for k in range(len(stages[n])):
            e_copy(n, k).start()

    def e_take(n):
        total = epart[e_half(c), :] if n == 0 else esend[n - 1]
        for k in range(len(stages[n])):
            e_copy(n, k).wait_recv()
            total = total + erecv[first[n] + k]
        if n < 2:
            esend[n] = total
            e_start(n + 1)
        else:
            eall[d, e_half(c), :] = total
            e_cross.start()

    e_cross = copy_to(
        eall.at[d, e_half(c), :], eall.at[d, e_half(c), :], e_s.at[first[3]], e_r.at[first[3]], z_dev(0)
    )
    e_core = copy_to(
        eall.at[:, e_half(c), :], eall.at[:, e_half(c), :], e_s.at[first[3] + 1], e_r.at[first[3] + 1], partner
    )
    own_small = pltpu.make_async_copy(eall, small_out, lsem.at[2])

    def in_share():
        in_f32 = jnp.concatenate([gwin[q, 0:EW] for q in range(4)], axis=0)
        if dims.N_IN > 4 * EW:
            in_f32 = jnp.concatenate([in_f32, jnp.zeros((dims.N_IN - 4 * EW, U), F32)], axis=0)
        share = in_sum.share
        total = in_f32[0:share]
        for k in range(1, RR):
            total = jnp.where(r == k, in_f32[k * share : (k + 1) * share], total)
        return total

    def e_gather():
        e_cross.wait_recv()
        e_core.start()

    def e_finish():
        e_core.wait_recv()
        own_small.start()

    e_start(0)
    between = [
        (0.05, lambda: e_take(0)),
        (0.2, lambda: in_sum.add(in_share())),
        (0.2, lambda: e_take(1)),
        (0.35, lambda: e_take(2)),
        (0.5, in_sum.relay),
        (0.6, e_gather),
        (0.7, in_sum.spread),
        (0.8, e_finish),
        (1.0, in_sum.finish),
    ]
    for at in range(sent, len(steps)):
        send_home(at)
        while between and (at + 1 - sent) >= between[0][0] * (len(steps) - sent):
            between.pop(0)[1]()
    for _, event in between:
        event()

    for j in range(3):
        ids_copy(j).wait_send()
    win_copy.wait_send()
    bias_copy.wait_send()
    for k in range(1, Hy):
        wdy_copy(k).wait_send()
    for k in range(Hy):
        wdc_copy(k).wait_send()
    for b in range(BATCHES):
        for p in range(len(peers)):
            f_copy(L - 1, b, p).wait_send()
            b_copy(2, b, p).wait_send()
            b_copy(1, b, p).wait_send()
    pgx_copy(1).wait_send()
    pgx_copy(0).wait_send()
    for n in range(3):
        for k in range(len(stages[n])):
            e_copy(n, k).wait_send()
    e_cross.wait_send()
    e_core.wait_send()
    dec_sum.drain()
    in_sum.drain()
    for k in range(1, RR):
        copy_to(W.at[0, :, 0 : 4 * KR, :], W.at[0, :, 0 : 4 * KR, :], B_s.at[k - 1], B_r.at[k - 1, 0, 0], r_dev(k)).wait_send()
    kept = grec_out.at[d, :, :, half]
    for i in range(3):
        copy_to(kept, kept, C_s.at[i], C_r.at[i], z_dev(i)).wait()
    pltpu.make_async_copy(kept, kept, C_s.at[3]).wait()
    own_small.wait()


def call_kernel(dims, *operands):
    R, RR, Hy, U, U2, NR, L, VP = dims.R, dims.RR, dims.Hy, dims.U, dims.U2, dims.NR, dims.L, dims.VP
    KR, EP, VS, H, RB, N_IN, N_DEC = dims.KR, dims.EP, dims.VS, dims.H, dims.RB, dims.N_IN, dims.N_DEC
    chips, peers, pieces = 2 * Hy, len(dims.peers), dims.pieces
    vmem, sem = pltpu.VMEM, pltpu.SemaphoreType.DMA
    apart = pl.BlockSpec(memory_space=pl.ANY)
    inside = pl.BlockSpec(memory_space=pltpu.VMEM)
    groups = max(RR - 1, 1)
    along = max(Hy - 1, 1)
    stages = 1 + peers + (RR - 1)
    id_rows = 2 * dims.P8 + 8
    scratch = [
        vmem((2, id_rows, 128), F32),
        vmem((4, id_rows, 128), F32),
        vmem((128, 128), F32),
        vmem((4, dims.RL // 2, 128), F32),
        vmem((8, VP), F32),
        vmem((ceil_to(dims.LANGS, 16), VP), F32),
        vmem((2, 8, U), F32),
        vmem((2, 4, EP, U), BF16),
        vmem((2, 4, H, U), BF16),
        vmem((chips, 2, U, VP), BF16),
        vmem((L, NR, EP), BF16),
        vmem((L, NR, EP), BF16),
        vmem((NR, VP), F32),
        vmem((2, 4, NR, U), F32),
        vmem((L, chips, NR, U2), BF16),
        vmem((L, chips, NR, U2), BF16),
        vmem((L, 4, 2, NR, U), F32),
        vmem((L + 1, 2, NR, U), F32),
        vmem((L, NR, VP), BF16),
        vmem((L, NR, VP), BF16),
        vmem((NR, 128), F32),
        vmem((8, VP), F32),
        vmem((2, NR, U), F32),
        vmem((2, NR, U), F32),
        vmem((2, 2, 4, NR, U), BF16),
        vmem((L, 4, NR, U), BF16),
        vmem((2, peers, NR, U2), BF16),
        vmem((2, peers, NR, U2), BF16),
        vmem((4, H, U), F32),
        vmem((4, EP, U), F32),
        vmem((VP, EP), F32),
        vmem((max(VP, N_DEC), U), F32),
        vmem((N_DEC, U), BF16),
        vmem((groups, N_DEC // RR, U), BF16),
        vmem((2, N_DEC, 2 * U), BF16),
        vmem((N_IN, U), BF16),
        vmem((groups, N_IN // RR, U), BF16),
        vmem((2, N_IN, 2 * U), BF16),
        vmem((groups, 4, 4, KR, U), BF16),
        vmem((VS, 128), F32),
        vmem((2, VS // 2, 128), F32),
        vmem((stages, VS // 2, 128), F32),
        vmem((2, VS, 128), F32),
        sem((4,)),
        sem((3,)), sem((3,)),
        sem((1,)), sem((1,)),
        sem((1,)), sem((1,)),
        sem((along,)), sem((along,)),
        sem((Hy,)), sem((Hy,)),
        sem((3,)), sem((3, pieces)),
        sem((groups,)), sem((4, groups, pieces)),
        sem((1,)), sem((1,)),
        sem((1,)), sem((1,)),
        sem((2, BATCHES, peers)), sem((2, BATCHES, peers)),
        sem((L,)), sem((L,)),
        sem((L,)), sem((L,)),
        sem((2, BATCHES, peers)), sem((2, BATCHES, peers)),
        sem((L,)), sem((L,)),
        sem((2, 2 * groups + 3)),
        sem((2, 2 * groups + 3)),
        sem((groups,)), sem((groups, 4, pieces)),
        sem((4,)), sem((3,)),
        sem((stages + 2,)), sem((stages + 2,)),
    ]
    rows = NR * L
    flops = 2 * rows * (3 * H * 8 * U + 3 * H * VP)
    return pl.pallas_call(
        functools.partial(kernel, dims),
        out_shape=(
            jax.ShapeDtypeStruct((2, 4, KR, 2 * U), BF16),
            jax.ShapeDtypeStruct((2, N_IN, 2 * U), BF16),
            jax.ShapeDtypeStruct((2, N_DEC, 2 * U), BF16),
            jax.ShapeDtypeStruct((2, VS, 128), F32),
        ),
        in_specs=[inside] * 5 + [apart] * 3 + [inside] * 3,
        out_specs=(apart, apart, apart, apart),
        scratch_shapes=scratch,
        cost_estimate=pl.CostEstimate(flops=flops, bytes_accessed=8 << 20, transcendentals=rows * U2 * 8),
        compiler_params=pltpu.CompilerParams(
            collective_id=0, has_side_effects=True, vmem_limit_bytes=62 << 20
        ),
        name="train_step",
    )(*operands)


def outputs_kernel(
    dims, grec, gwin, gwd, small, w_rec_out, w_in_out, b_in_out, b_rec_out, w_dec_out, emb_out, b_dec_out, loss_out
):
    for d in range(2):
        for q in range(4):
            w_rec_out[d, :, q, :] = grec[d, q].astype(F32)

    E, EW, V, V8 = dims.E, dims.EW, dims.V, dims.V8
    steps = pl.num_programs(0)

    @pl.when(pl.program_id(0) == 0)
    def _():
        for d in range(2):
            for q in range(4):
                w_in_out[d, :, q, :] = gwin[d, q * EW : q * EW + E].astype(F32)
                first = q * EW + E // 16 * 16
                row = gwin[d, first : first + 16].astype(F32)[E % 16 : E % 16 + 1]
                b_in_out[d, q : q + 1, :] = row
                b_rec_out[d, q : q + 1, :] = row

    @pl.when(pl.program_id(0) == steps // 4)
    def _():
        for d in range(2):
            w_dec_out[:, d, :] = gwd[d, 0:V].astype(F32)

    @pl.when(pl.program_id(0) == steps // 2)
    def _():
        for d in range(2):
            emb_out[:, d, :] = small[d, 0:V, 0:E]
            for k in range(dims.VP // 128):
                width = min(128, V - k * 128)
                b_dec_out[d : d + 1, k * 128 : k * 128 + width] = small[d, V8 + k : V8 + k + 1, 0:width]
        at = V8 + dims.VP // 128
        loss_out[...] = small[0, at : at + 1, 0:1] + small[1, at : at + 1, 0:1]


def call_outputs(dims, grec, gwin, gwd, small):
    KR, U2, E, V = dims.KR, dims.U2, dims.E, dims.V
    parts = 4 if KR % 64 == 0 else 1
    rows = KR // parts

    def whole(*shape):
        return pl.BlockSpec(shape, lambda i: (0,) * len(shape))

    shapes = ((2, E, 4, U2), (2, 4, U2), (2, 4, U2), (V, 2, U2), (V, 2, E), (2, V), (1, 1))
    return pl.pallas_call(
        functools.partial(outputs_kernel, dims),
        grid=(parts,),
        out_shape=[jax.ShapeDtypeStruct((2, KR, 4, U2), F32)] + [jax.ShapeDtypeStruct(s, F32) for s in shapes],
        in_specs=[
            pl.BlockSpec((2, 4, rows, U2), lambda i: (0, 0, i, 0)),
            whole(*gwin.shape), whole(*gwd.shape), whole(*small.shape),
        ],
        out_specs=[pl.BlockSpec((2, rows, 4, U2), lambda i: (0, i, 0, 0))] + [whole(*s) for s in shapes],
        compiler_params=pltpu.CompilerParams(vmem_limit_bytes=62 << 20),
        name="outputs",
    )(grec, gwin, gwd, small)


def local(
    char_ids, lang_ids, vocab_masks, targets, embedding, w_in, w_rec, b_in, b_rec, w_dec, b_dec
):
    R, hid = lax.axis_size("rows"), lax.axis_size("hid")
    RL, L = char_ids.shape
    E, units = w_in.shape[1], w_in.shape[3]
    V = embedding.shape[1]
    KR = w_rec.shape[1]
    U = units // 2
    dims = Dims(
        R=R, RR=R // 4, Hy=hid // 2, H=units * hid, KR=KR, U=U, RL=RL, L=L, V=V, E=E,
        LANGS=vocab_masks.shape[0], scale=1.0 / (RL * R * L),
    )
    VP, EP, EW = dims.VP, dims.EP, dims.EW

    win = jnp.pad(w_in.transpose(0, 2, 1, 3), ((0, 0), (0, 0), (0, EP - E), (0, 0)))
    wrec = w_rec.transpose(0, 2, 1, 3)
    wdec = jnp.pad(w_dec, ((0, 0), (0, 0), (0, VP - V))).reshape(2, 2, U, VP)
    emb = jnp.concatenate([embedding, jnp.ones((2, V, 1), BF16)], axis=2)
    emb = jnp.pad(emb, ((0, 0), (0, VP - V), (0, EP - E - 1)))

    sums = call_kernel(
        dims, char_ids.T, targets.transpose(0, 2, 1), lang_ids[None], b_in, b_rec, win, wrec, wdec, emb, b_dec,
        vocab_masks,
    )
    w_rec_grad, w_in_grad, b_in_grad, b_rec_grad, w_dec_grad, emb_grad, b_dec_grad, loss = call_outputs(dims, *sums)
    return (
        loss[0, 0],
        emb_grad.transpose(1, 0, 2),
        w_in_grad,
        w_rec_grad,
        b_in_grad,
        b_rec_grad,
        w_dec_grad.transpose(1, 2, 0),
        b_dec_grad,
    )


def solution(mesh):
    placed = (
        P("rows", None),
        P("rows"),
        P(),
        P(None, "rows", None),
        P(),
        P(None, None, None, "hid"),
        P(None, "rows", None, "hid"),
        P(None, None, "hid"),
        P(None, None, "hid"),
        P(None, "hid", None),
        P(),
    )
    return jax.shard_map(
        local,
        mesh=mesh,
        in_specs=placed,
        out_specs=(
            P(),
            P(),
            P(None, None, None, "hid"),
            P(None, "rows", None, "hid"),
            P(None, None, "hid"),
            P(None, None, "hid"),
            P(None, "hid", None),
            P(),
        ),
        check_vma=False,
    )
```

```python
import functools
from typing import NamedTuple

import jax
import jax.numpy as jnp
from jax import lax
from jax.experimental import pallas as pl
from jax.experimental.pallas import tpu as pltpu
from jax.sharding import PartitionSpec as P

MESH = pl.DeviceIdType.MESH
F32 = jnp.float32
BF16 = jnp.bfloat16
masked_value = -1000000000.0
ROW_PARTS = 2
AHEAD = 8
EARLY = 2
WINDOW = 3
BATCHES = 2


def ceil_to(n, m):
    return (n + m - 1) // m * m


class Dims(NamedTuple):
    R: int
    RR: int
    Hy: int
    H: int
    KR: int
    U: int
    RL: int
    L: int
    V: int
    E: int
    LANGS: int
    scale: float

    @property
    def U2(self):
        return 2 * self.U

    @property
    def NR(self):
        return 2 * self.RL

    @property
    def VP(self):
        return ceil_to(self.V, 128)

    @property
    def RB(self):
        return self.NR // BATCHES

    @property
    def QN(self):
        return 1 if self.RR <= 2 else 4

    @property
    def KP(self):
        return ROW_PARTS if self.RR <= 2 else 1

    @property
    def pieces(self):
        return 4 // self.QN * self.KP

    @property
    def KRP(self):
        return self.KR // self.KP

    @property
    def N_IN(self):
        return ceil_to(4 * self.EW, 16 * self.RR)

    @property
    def N_DEC(self):
        return ceil_to(self.V, 16 * self.RR)

    @property
    def P8(self):
        return ceil_to(self.L, 8)

    @property
    def EP(self):
        return ceil_to(self.E + 2, 128)

    @property
    def EW(self):
        return ceil_to(self.E + 2, 16)

    @property
    def V8(self):
        return ceil_to(self.V, 8)

    @property
    def VS(self):
        return ceil_to(self.V8 + 8, 16)

    @property
    def peers(self):
        far = [(1, k) for k in range(1, self.Hy)]
        beside = [(0, k) for k in range(1, self.Hy)]
        return far + beside + [(1, 0)]


Z_STEPS = ((1, 0), (1, 1), (0, 1))


def dot(a, b):
    return jnp.dot(a, b, preferred_element_type=F32)


def dot_nt(a, b):
    return lax.dot_general(a, b, (((1,), (1,)), ((), ())), preferred_element_type=F32)


def dot_tn(a, b):
    return lax.dot_general(a, b, (((0,), (0,)), ((), ())), preferred_element_type=F32)


def flip(bit, step):
    return 1 - bit if step else bit


def kernel(
    dims,
    chars_ref, targets_ref, lang_ref, b_in_ref, b_rec_ref, win_in, wrec_in, wdec_in, emb_ref, b_dec_ref, masks_ref,
    grec_out, gwin_out, gwd_out, small_out,
    idsrc, idsall, idtmp, ids, bdec, masks, bias, win, W, wd, x, xp, allowed, acc, st, stp, gs, cell, lg, lgp, lossv, gb,
    dh, cg, pg, pgx, psend, precv, dW, gwin, gemb, gwd, gwd_s, gwd_r, gwd_all, gwin_s, gwin_r, gwin_all,
    recvB, epart, esend, erecv, eall,
    lsem, ids_s, ids_r, win_s2, win_r2, bias_s, bias_r, wdy_s, wdy_r, wdc_s, wdc_r, wz_s, wz_r, wx_s, wx_r, wc_s, wc_r,
    xp_s, xp_r, f_s, f_r, stp_s, stp_r, lgp_s, lgp_r, b_s, b_r, pgx_s, pgx_r,
    gwd_sems, gwin_sems, B_s, B_r, C_s, C_r, e_s, e_r,
):
    R, RR, Hy, U, U2, NR, L, VP = dims.R, dims.RR, dims.Hy, dims.U, dims.U2, dims.NR, dims.L, dims.VP
    KR, EW, V8, VS, RL, RB, QN = dims.KR, dims.EW, dims.V8, dims.VS, dims.RL, dims.RB, dims.QN
    peers = dims.peers
    KP, KRP, pieces = dims.KP, dims.KRP, dims.pieces
    rho, hid = lax.axis_index("rows"), lax.axis_index("hid")
    d, g, r = rho // (R // 2), lax.rem(rho // RR, 2), lax.rem(rho, RR)
    y, c = hid // 2, lax.rem(hid, 2)
    mine = y * 2 + g
    part = d * 2 + g

    def dev(dd, gg, rr, yy, cc):
        return (dd * (R // 2) + gg * RR + rr, yy * 2 + cc)

    def copy_to(src, dst, send, recv, device):
        return pltpu.make_async_remote_copy(
            src_ref=src, dst_ref=dst, send_sem=send, recv_sem=recv, device_id=device, device_id_type=MESH
        )

    def add_r(step):
        return lax.rem(r + step, RR)

    def add_y(step):
        return lax.rem(y + step, Hy)

    def place_of(dd, gg, rr):
        index = dd * (R // 2) + gg * RR + rr
        per = U // KR
        block = index // per
        hid_of, g_of = block // 2, lax.rem(block, 2)
        return (hid_of // 2) * 2 + g_of, lax.rem(hid_of, 2) * U + lax.rem(index, per) * KR

    def rows_of(dd, gg, rr, n=None):
        chip, unit = place_of(dd, gg, rr)
        row = chip * U2 + unit
        if n is None:
            return pl.ds(pl.multiple_of(row, KR), KR)
        return pl.ds(pl.multiple_of(row + n % KP * KRP, KRP), KRP)

    def rows_in(n):
        return pl.ds(n % KP * KRP, KRP)

    def chip_rows(m):
        return pl.ds(pl.multiple_of(m * U2, U2), U2)

    partner = dev(d, g, r, y, 1 - c)
    half = pl.ds(pl.multiple_of(g * U, U), U)

    def z_dev(j):
        return dev(flip(d, Z_STEPS[j][0]), flip(g, Z_STEPS[j][1]), r, y, c)

    def r_dev(step):
        return dev(d, g, add_r(step), y, c)

    def y_dev(step):
        return dev(d, g, r, add_y(step), c)

    def peer_dev(p):
        return dev(d, flip(g, peers[p][0]), r, add_y(peers[p][1]), c)

    barrier = pltpu.get_barrier_semaphore()
    greeted = [z_dev(j) for j in range(3)] + [r_dev(k) for k in range(1, RR)] + [partner]
    greeted += [peer_dev(p) for p in range(len(peers)) if peers[p] != (1, 0)]
    for device in greeted:
        pl.semaphore_signal(barrier, inc=1, device_id=device, device_id_type=MESH)
    pl.semaphore_wait(barrier, len(greeted))

    def ids_copy(j):
        return copy_to(idsrc.at[flip(d, Z_STEPS[j][0])], idsall.at[part], ids_s.at[j], ids_r.at[j], z_dev(j))

    def gates_of(n):
        return pl.ds(n // KP * QN, QN)

    def wz_copy(j, n):
        columns = pl.ds(pl.multiple_of(flip(g, Z_STEPS[j][1]) * U, U), U)
        there = wrec_in.at[flip(d, Z_STEPS[j][0]), gates_of(n), rows_in(n), columns]
        return copy_to(there, W.at[c, gates_of(n), rows_of(d, g, r, n), :], wz_s.at[j], wz_r.at[j, n], z_dev(j))

    def z_block(j):
        steps = Z_STEPS[j] if j < 3 else (0, 0)
        return flip(d, steps[0]), flip(g, steps[1])

    def w_block(core, j, k, n):
        dd, gg = z_block(j)
        return W.at[core, gates_of(n), rows_of(dd, gg, lax.rem(r + RR - k, RR), n), :]

    def wx_copy(j, k, n):
        block = w_block(c, j, 0, n)
        return copy_to(block, block, wx_s.at[k - 1], wx_r.at[j, k - 1, n], r_dev(k))

    def wc_copy(j, k, n):
        block = w_block(c, j, k, n)
        return copy_to(block, block, wc_s.at[0], wc_r.at[0], partner)

    def wc_all(core):
        return copy_to(W.at[core], W.at[core], wc_s.at[0], wc_r.at[0], partner)

    def wd_rows(yy):
        return wd.at[pl.ds(yy * 2, 2), c]

    def wdy_copy(k):
        return copy_to(wdec_in.at[d], wd_rows(y), wdy_s.at[k - 1], wdy_r.at[k - 1], y_dev(k))

    def wdc_copy(k):
        yy = lax.rem(y + Hy - k, Hy)
        return copy_to(wd_rows(yy), wd_rows(yy), wdc_s.at[k], wdc_r.at[k], partner)

    win_copy = copy_to(win_in.at[d, :, :, half], win.at[c], win_s2.at[0], win_r2.at[0], partner)
    bias_copy = copy_to(bias.at[c], bias.at[c], bias_s.at[0], bias_r.at[0], partner)
    own_win = pltpu.make_async_copy(win_in.at[d, :, :, half], win.at[c], lsem.at[1])
    own_wd = pltpu.make_async_copy(wdec_in.at[d], wd_rows(y), lsem.at[2])
    own_w = pltpu.make_async_copy(
        wrec_in.at[d, :, :, half], W.at[c, :, rows_of(d, g, r), :], lsem.at[3]
    )

    own_w.start()
    for n in range(min(WINDOW, pieces)):
        for j in range(3):
            wz_copy(j, n).start()
    own_win.start()
    win_copy.start()
    for k in range(1, Hy):
        wdy_copy(k).start()
    own_wd.start()

    P8 = dims.P8
    idsrc[...] = jnp.zeros_like(idsrc)
    for dd in range(2):
        idsrc[dd, 0:L, 0:RL] = chars_ref[...].astype(F32)
        idsrc[dd, P8 : P8 + L, 0:RL] = targets_ref[dd].astype(F32)
        idsrc[dd, 2 * P8 : 2 * P8 + 8, 0:RL] = jnp.broadcast_to(lang_ref[...].astype(F32), (8, RL))
    for j in range(3):
        ids_copy(j).start()
    bias[c, 0:4] = b_in_ref[d, :, half].astype(F32) + b_rec_ref[d, :, half].astype(F32)
    bias_copy.start()
    idsall[part] = idsrc[d]

    own_w.wait()
    for n in range(pieces):
        for k in range(1, RR):
            wx_copy(3, k, n).start()
        wc_copy(3, 0, n).start()

    dW[...] = jnp.zeros_like(dW)
    gwin[...] = jnp.zeros_like(gwin)
    gemb[...] = jnp.zeros_like(gemb)
    lossv[...] = jnp.zeros_like(lossv)
    gb[...] = jnp.zeros_like(gb)
    cg[...] = jnp.zeros_like(cg)
    cell[0] = jnp.zeros_like(cell[0])
    bdec[...] = jnp.zeros_like(bdec)
    bdec[0:2, 0 : dims.V] = b_dec_ref[...].astype(F32)
    masks[...] = jnp.zeros_like(masks)
    masks[0 : dims.LANGS, 0 : dims.V] = masks_ref[...].astype(F32)
    idtmp[...] = jnp.zeros_like(idtmp)

    for j in range(3):
        ids_copy(j).wait_recv()
    for n in range(4):
        idtmp[:, 0 : idsall.shape[1]] = idsall[n].T
        ids[n] = idtmp[pl.ds(pl.multiple_of(c * (RL // 2), RL // 2), RL // 2), :]

    lane = lax.broadcasted_iota(jnp.int32, (NR, 128), 1)
    vocab = lax.broadcasted_iota(jnp.int32, (NR, VP), 1).astype(F32)

    def id_column(at):
        held = ids[...].reshape(NR, 128)
        return jnp.sum(jnp.where(lane == at, held, 0.0), axis=1, keepdims=True)

    def place(t):
        return t + d * (L - 1 - 2 * t)

    def char_hot(t):
        return jnp.where(vocab == id_column(place(t)), 1.0, 0.0).astype(BF16)

    lang_lane = lax.broadcasted_iota(jnp.int32, (NR, masks.shape[0]), 1).astype(F32)
    lang_hot = jnp.where(lang_lane == id_column(2 * P8), 1.0, 0.0).astype(BF16)
    allowed[...] = dot(lang_hot, masks[...].astype(BF16))

    @pl.loop(0, L)
    def _(t):
        x[t] = dot(char_hot(t), emb_ref[d]).astype(BF16)

    xp_copy = copy_to(x, xp, xp_s.at[0], xp_r.at[0], partner)
    xp_copy.start()

    own_wd.wait()
    wdc_copy(0).start()
    own_win.wait()
    win_copy.wait_recv()
    bias_copy.wait_recv()

    def part_rows(b):
        return pl.ds(b * RB, RB)

    def f_copy(t, b, p):
        slot = lax.rem(t, 2)
        block = st.at[t, mine, part_rows(b), :]
        return copy_to(block, block, f_s.at[slot, b, p], f_r.at[slot, b, p], peer_dev(p))

    def gates(t, b):
        rows = part_rows(b)
        for cc in range(2):
            si = jax.nn.sigmoid(acc[cc, 0, rows])
            sf = jax.nn.sigmoid(acc[cc, 1, rows])
            tg = jnp.tanh(acc[cc, 2, rows])
            so = jax.nn.sigmoid(acc[cc, 3, rows])
            new = sf * cell[t, cc, rows] + si * tg
            cell[t + 1, cc, rows] = new
            st[t, mine, rows, cc * U : (cc + 1) * U] = (so * jnp.tanh(new)).astype(BF16)
            gs[t, 0, cc, rows] = si
            gs[t, 1, cc, rows] = sf
            gs[t, 2, cc, rows] = tg
            gs[t, 3, cc, rows] = so

    def peer_block(p):
        yy = lax.rem(y + Hy - peers[p][1], Hy)
        return yy * 2 + flip(g, peers[p][0])

    for cc in range(2):
        for q in range(4):
            acc[cc, q] = dot(x[0], win[cc, q]) + bias[cc, q : q + 1]
    for b in range(BATCHES):
        gates(0, b)
        for p in range(len(peers)):
            f_copy(0, b, p).start()

    for k in range(1, Hy):
        wdy_copy(k).wait_recv()
        wdc_copy(k).start()
    from_z, beside = [], [(2, n) for n in range(pieces)]
    for n in range(pieces):
        from_z += beside[2 * n : 2 * n + 2] + [(0, n), (1, n)]
    from_x = [(3, n) for n in range(pieces)] + from_z
    for at in range(len(from_x)):
        if at < len(from_z):
            j, n = from_z[at]
            wz_copy(j, n).wait_recv()
            for k in range(1, RR):
                wx_copy(j, k, n).start()
            wc_copy(j, 0, n).start()
            if n + WINDOW < pieces:
                wz_copy(j, n + WINDOW).start()
        j, n = from_x[at]
        for k in range(1, RR):
            wx_copy(j, k, n).wait_recv()
            wc_copy(j, k, n).start()
    wc_all(1 - c).wait_recv()
    for k in range(Hy):
        yy = lax.rem(y + Hy - k, Hy)
        other = wd.at[pl.ds(yy * 2, 2), 1 - c]
        copy_to(other, other, wdc_s.at[k], wdc_r.at[k], partner).wait_recv()

    def stp_copy(t):
        return copy_to(st.at[t], stp.at[t], stp_s.at[t], stp_r.at[t], partner)

    def lgp_copy(t):
        return copy_to(lg.at[t], lgp.at[t], lgp_s.at[t], lgp_r.at[t], partner)

    def decode(t):
        stp_copy(t).start()
        logits = bdec[pl.ds(d, 1), :]
        for m in range(2 * Hy):
            logits = logits + dot(st[t, m], wd[m].reshape(U2, VP))
        masked = jnp.where(allowed[...] > 0.5, logits, masked_value)
        top = jnp.max(masked, axis=1, keepdims=True)
        powers = jnp.exp(masked - top)
        total = jnp.sum(powers, axis=1, keepdims=True)
        hot = vocab == id_column(P8 + place(t))
        picked = jnp.sum(jnp.where(hot, logits, 0.0), axis=1, keepdims=True)
        lossv[...] += jnp.broadcast_to(top + jnp.log(total) - picked, (NR, 128))
        grad = ((powers / total - jnp.where(hot, 1.0, 0.0)) * dims.scale).astype(BF16)
        lg[t] = grad
        gb[0:1, :] += jnp.sum(grad.astype(F32), axis=0, keepdims=True)
        lgp_copy(t).start()

    @pl.loop(1, L)
    def _(t):
        for cc in range(2):
            for q in range(4):
                start = dot(x[t], win[cc, q]) + bias[cc, q : q + 1]
                acc[cc, q] = start + dot(st[t - 1, mine], W[cc, q, chip_rows(mine), :])
        for b in range(BATCHES):
            rows = part_rows(b)
            for p in reversed(range(len(peers))):
                f_copy(t - 1, b, p).wait_recv()
                m = peer_block(p)
                for cc in range(2):
                    for q in range(4):
                        acc[cc, q, rows] += dot(st[t - 1, m, rows], W[cc, q, chip_rows(m), :])
            gates(t, b)
            for p in range(len(peers)):
                f_copy(t - 1, b, p).wait_send()
            for p in reversed(range(len(peers))):
                f_copy(t, b, p).start()
        decode(t - 1)

    block = wrec_in.at[d, :, :, half]
    for j in range(3):
        copy_to(block, block, wz_s.at[j], wz_r.at[j, 0], z_dev(j)).wait_send()
    blocks = W.at[c, :, 0 : 4 * KR, :]
    for k in range(1, RR):
        copy_to(blocks, blocks, wx_s.at[k - 1], wx_r.at[0, k - 1, 0], r_dev(k)).wait_send()
    wc_all(c).wait_send()

    @pl.loop(0, dims.H // U)
    def _(k):
        rows = pl.ds(pl.multiple_of(k * U, U), U)
        for cc in range(2):
            for q in range(4):
                W[cc, q, rows, :] = W[cc, q, rows, :].T

    for b in range(BATCHES):
        for p in reversed(range(len(peers))):
            f_copy(L - 1, b, p).wait_recv()
    decode(L - 1)

    def dec_back(t, cc):
        return dot_nt(lg[t], wd[mine, cc])

    def b_copy(t, b, p):
        slot = lax.rem(t, 2)
        there = precv.at[slot, p, part_rows(b), :]
        return copy_to(
            psend.at[slot, p, part_rows(b), :], there, b_s.at[slot, b, p], b_r.at[slot, b, p], peer_dev(p)
        )

    def pgx_copy(t):
        return copy_to(pg.at[lax.rem(t, 2), 1 - c], pgx.at[t], pgx_s.at[t], pgx_r.at[t], partner)

    def preact_grads(t, b):
        slot = lax.rem(t, 2)
        rows = part_rows(b)
        for cc in range(2):
            h = dh[cc, rows]
            si, sf, tg, so = (gs[t, q, cc, rows] for q in range(4))
            tc = jnp.tanh(cell[t + 1, cc, rows])
            total = cg[cc, rows] + h * so * (1.0 - tc * tc)
            pg[slot, cc, 0, rows] = (total * tg * si * (1.0 - si)).astype(BF16)
            pg[slot, cc, 1, rows] = (total * cell[t, cc, rows] * sf * (1.0 - sf)).astype(BF16)
            pg[slot, cc, 2, rows] = (total * si * (1.0 - tg * tg)).astype(BF16)
            pg[slot, cc, 3, rows] = (h * tc * so * (1.0 - so)).astype(BF16)
            cg[cc, rows] = total * sf

    def partial(t, rows_here, m, cc):
        slot = lax.rem(t, 2)
        rows = pl.ds(pl.multiple_of(m * U2 + cc * U, U), U)
        total = None
        for kk in range(2):
            for q in range(4):
                term = dot(pg[slot, kk, q, rows_here], W[kk, q, rows, :])
                total = term if total is None else total + term
        return total

    def take_state_grad(t, b):
        slot = lax.rem(t, 2)
        rows = part_rows(b)
        for p in reversed(range(len(peers))):
            b_copy(t, b, p).wait_recv()
            for cc in range(2):
                dh[cc, rows] += precv[slot, p, rows, cc * U : (cc + 1) * U].astype(F32)

    def both_cores(t, q):
        return jnp.concatenate([pg[lax.rem(t, 2), c, q], pgx[t, q]], axis=0)

    def rec_grads(t):
        for q in range(4):
            both = both_cores(t, q)
            for m in range(2 * Hy):
                states = jnp.concatenate([st[t - 1, m], stp[t - 1, m]], axis=0)
                dW[q, m * U2 : (m + 1) * U2, :] += dot_tn(states, both)

    def in_grads(t):
        slot = lax.rem(t, 2)
        inputs = jnp.concatenate([x[t], xp[t]], axis=0)
        for q in range(4):
            gwin[q] += dot_tn(inputs, both_cores(t, q))
        back = None
        for cc in range(2):
            for q in range(4):
                term = dot_nt(pg[slot, cc, q], win[cc, q])
                back = term if back is None else back + term
        high = back.astype(BF16)
        rest = (back - high.astype(F32)).astype(BF16)
        hot = char_hot(t)
        gemb[...] += dot_tn(hot, high) + dot_tn(hot, rest)

    class SmallSum:
        def __init__(self, send, recv, whole, out, sems, own_sem):
            self.send, self.recv, self.whole, self.out, self.sems, self.own = send, recv, whole, out, sems, own_sem
            self.share = whole.shape[1] // RR

        def rows(self, rr):
            return pl.ds(pl.multiple_of(rr * self.share, 16), self.share)

        def pair(self, at):
            return self.sems.at[0, at], self.sems.at[1, at]

        def first(self, k):
            return copy_to(self.send.at[self.rows(add_r(k)), :], self.recv.at[k - 1], *self.pair(k - 1), r_dev(k))

        def block(self, dd, gg):
            return self.whole.at[dd, self.rows(r), pl.ds(pl.multiple_of(gg * U, U), U)]

        def along(self, j):
            block = self.block(1 - d, g) if j == 1 else self.block(d, g)
            return copy_to(block, block, *self.pair(RR - 1 + j), z_dev(0 if j == 0 else 2))

        def last(self, k):
            block = self.whole.at[:, self.rows(r), :]
            return copy_to(block, block, *self.pair(RR + 2 + k - 1), r_dev(k))

        def to_out(self):
            return pltpu.make_async_copy(self.whole, self.out, self.own)

        def start(self):
            for k in range(1, RR):
                self.first(k).start()

        def add(self, value):
            for k in range(1, RR):
                self.first(k).wait_recv()
                value = value + self.recv[k - 1].astype(F32)
            self.whole[d, self.rows(r), half] = value.astype(BF16)
            self.along(0).start()
            self.along(2).start()

        def relay(self):
            self.along(0).wait_recv()
            self.along(1).start()

        def spread(self):
            self.along(2).wait_recv()
            self.along(1).wait_recv()
            for k in range(1, RR):
                self.last(k).start()

        def finish(self):
            for k in range(1, RR):
                self.last(k).wait_recv()
            self.to_out().start()

        def drain(self):
            for k in range(1, RR):
                self.first(k).wait_send()
                self.last(k).wait_send()
            for j in range(3):
                self.along(j).wait_send()
            self.to_out().wait()

    dec_sum = SmallSum(gwd_s, gwd_r, gwd_all, gwd_out, gwd_sems, lsem.at[0])
    in_sum = SmallSum(gwin_s, gwin_r, gwin_all, gwin_out, gwin_sems, lsem.at[1])

    def decoder_grad():
        gwd[...] = jnp.zeros_like(gwd)

        @pl.loop(0, L)
        def _(t):
            columns = pl.ds(pl.multiple_of(c * U, U), U)
            states = jnp.concatenate([st[t, mine, :, columns], stp[t, mine, :, columns]], axis=0)
            gwd[...] += dot_tn(jnp.concatenate([lg[t], lgp[t]], axis=0), states)

        gwd_s[...] = gwd[0 : dims.N_DEC].astype(BF16)
        dec_sum.start()

    for cc in range(2):
        dh[cc] = dec_back(L - 1, cc)

    @pl.loop(0, L - 1)
    def _(i):
        t = L - 1 - i
        slot = lax.rem(t, 2)

        @pl.when(i > 1)
        def _():
            pgx_copy(t + 2).wait_send()

        for b in range(BATCHES):
            rows = part_rows(b)

            @pl.when(i > 0)
            def _():
                take_state_grad(t + 1, b)

            @pl.when(i > 1)
            def _():
                for p in range(len(peers)):
                    b_copy(t + 2, b, p).wait_send()

            preact_grads(t, b)
            for p in range(len(peers)):
                m = add_y(peers[p][1]) * 2 + flip(g, peers[p][0])
                for cc in range(2):
                    psend[slot, p, rows, cc * U : (cc + 1) * U] = partial(t, rows, m, cc).astype(BF16)
                b_copy(t, b, p).start()
        pgx_copy(t).start()
        for cc in range(2):
            dh[cc] = partial(t, pl.ds(0, NR), mine, cc) + dec_back(t - 1, cc)

        @pl.when(i > 0)
        def _():
            pgx_copy(t + 1).wait_recv()
            rec_grads(t + 1)

        @pl.when((i > 0) & (i < L - 2))
        def _():
            in_grads(t + 1)

        @pl.when(i == 0)
        def _():
            xp_copy.wait()

            @pl.loop(0, L)
            def _(at):
                stp_copy(at).wait()
                lgp_copy(at).wait()

            decoder_grad()

        @pl.when(i == 1)
        def _():
            dec_sum.add(gwd[dec_sum.rows(r), :])

        @pl.when(i == 2)
        def _():
            dec_sum.relay()

        @pl.when(i == 3)
        def _():
            dec_sum.spread()

        @pl.when(i == 4)
        def _():
            dec_sum.finish()

    out_steps = ((1, 0), (1, 1), (0, 1), (0, 0))

    def out_device(i, step):
        return flip(d, out_steps[i][0]), flip(g, out_steps[i][1]), add_r(step)

    def out_rows(i, step, n):
        return rows_of(*out_device(i, step), n)

    def b_out(i, k, n):
        return copy_to(
            W.at[0, gates_of(n), out_rows(i, k, n), :], recvB.at[k - 1, i, gates_of(n), rows_in(n), :],
            B_s.at[k - 1], B_r.at[k - 1, i, n], r_dev(k),
        )

    def c_out(i, n):
        there = grec_out.at[d, gates_of(n), rows_in(n), half]
        return copy_to(W.at[1, gates_of(n), out_rows(i, 0, n), :], there, C_s.at[i], C_r.at[i], z_dev(i))

    def own_out(n):
        there = grec_out.at[d, gates_of(n), rows_in(n), half]
        return pltpu.make_async_copy(W.at[1, gates_of(n), out_rows(3, 0, n), :], there, C_s.at[3])

    def gates_in(n):
        return range(n // KP * QN, (n // KP + 1) * QN)

    fused = KRP % 128 == 0

    def rec_piece(i, step, n, q):
        total = dW[q, out_rows(i, step, n), :]
        if fused:
            chip, unit = place_of(*out_device(i, step))
            units = pl.ds(pl.multiple_of(unit + n % KP * KRP, 128), KRP)
            states = jnp.concatenate([st[0, chip, :, units], stp[0, chip, :, units]], axis=0)
            total = total + dot_tn(states, both_cores(1, q))
        return total

    steps = [(i, n) for n in range(pieces) for i in (0, 2, 1, 3)]

    def send_over(at):
        i, n = steps[at]
        for k in range(1, RR):
            for q in gates_in(n):
                W[0, q, out_rows(i, k, n), :] = rec_piece(i, k, n, q).astype(BF16)
            b_out(i, k, n).start()

    def send_home(at):
        i, n = steps[at]
        for k in range(1, RR):
            b_out(i, k, n).wait_recv()
        for q in gates_in(n):
            total = rec_piece(i, 0, n, q)
            for k in range(1, RR):
                total = total + recvB[k - 1, i, q, rows_in(n), :].astype(F32)
            W[1, q, out_rows(i, 0, n), :] = total.astype(BF16)
        if i < 3:
            c_out(i, n).start()
        else:
            own_out(n).start()
        if at + ahead < len(steps):
            send_over(at + ahead)

    pgx_copy(1).wait_recv()
    if not fused:
        rec_grads(1)
    ahead = min(AHEAD, len(steps))
    for at in range(ahead):
        send_over(at)
    in_grads(2)
    in_grads(1)

    pgx_copy(2).wait_send()
    sent = 0
    for b in range(BATCHES):
        take_state_grad(1, b)
        preact_grads(0, b)
        for at in range(sent, min(sent + EARLY, len(steps))):
            send_home(at)
        sent = min(sent + EARLY, len(steps))
    pgx_copy(0).start()
    for at in range(sent, min(sent + EARLY, len(steps))):
        send_home(at)
    sent = min(sent + EARLY, len(steps))
    pgx_copy(0).wait_recv()
    in_grads(0)

    gwin_s[...] = jnp.zeros_like(gwin_s)
    for q in range(4):
        gwin_s[q * EW : (q + 1) * EW] = gwin[q, 0:EW].astype(BF16)
    in_sum.start()

    once = jnp.where(mine == 0, 1.0, 0.0).astype(F32)
    epart[0:V8] = gemb[0:V8]
    epart[V8:VS] = jnp.zeros((VS - V8, 128), F32)
    for k in range(VP // 128):
        epart[V8 + k : V8 + k + 1] = gb[0:1, k * 128 : (k + 1) * 128] * once
    at = V8 + VP // 128
    epart[at : at + 1] = jnp.sum(lossv[...], axis=0, keepdims=True) * (once * dims.scale)

    stages = [[partner], [peer_dev(p) for p in range(len(peers))], [r_dev(k) for k in range(1, RR)]]
    first = [sum(len(s) for s in stages[:n]) for n in range(len(stages) + 1)]

    def e_half(core):
        return pl.ds(pl.multiple_of(core * (VS // 2), 8), VS // 2)

    def e_copy(n, k):
        at = first[n] + k
        there = epart.at[e_half(1 - c), :] if n == 0 else esend.at[n - 1]
        return copy_to(there, erecv.at[at], e_s.at[at], e_r.at[at], stages[n][k])

    def e_start(n):
        for k in range(len(stages[n])):
            e_copy(n, k).start()

    def e_take(n):
        total = epart[e_half(c), :] if n == 0 else esend[n - 1]
        for k in range(len(stages[n])):
            e_copy(n, k).wait_recv()
            total = total + erecv[first[n] + k]
        if n < 2:
            esend[n] = total
            e_start(n + 1)
        else:
            eall[d, e_half(c), :] = total
            e_cross.start()

    e_cross = copy_to(
        eall.at[d, e_half(c), :], eall.at[d, e_half(c), :], e_s.at[first[3]], e_r.at[first[3]], z_dev(0)
    )
    e_core = copy_to(
        eall.at[:, e_half(c), :], eall.at[:, e_half(c), :], e_s.at[first[3] + 1], e_r.at[first[3] + 1], partner
    )
    own_small = pltpu.make_async_copy(eall, small_out, lsem.at[2])

    def in_share():
        in_f32 = jnp.concatenate([gwin[q, 0:EW] for q in range(4)], axis=0)
        if dims.N_IN > 4 * EW:
            in_f32 = jnp.concatenate([in_f32, jnp.zeros((dims.N_IN - 4 * EW, U), F32)], axis=0)
        share = in_sum.share
        total = in_f32[0:share]
        for k in range(1, RR):
            total = jnp.where(r == k, in_f32[k * share : (k + 1) * share], total)
        return total

    def e_gather():
        e_cross.wait_recv()
        e_core.start()

    def e_finish():
        e_core.wait_recv()
        own_small.start()

    e_start(0)
    between = [
        (0.1, lambda: e_take(0)),
        (0.3, lambda: in_sum.add(in_share())),
        (0.3, lambda: e_take(1)),
        (0.5, lambda: e_take(2)),
        (0.6, in_sum.relay),
        (0.8, e_gather),
        (0.85, in_sum.spread),
        (0.9, e_finish),
        (1.0, in_sum.finish),
    ]
    for at in range(sent, len(steps)):
        send_home(at)
        while between and (at + 1 - sent) >= between[0][0] * (len(steps) - sent):
            between.pop(0)[1]()
    for _, event in between:
        event()

    for j in range(3):
        ids_copy(j).wait_send()
    win_copy.wait_send()
    bias_copy.wait_send()
    for k in range(1, Hy):
        wdy_copy(k).wait_send()
    for k in range(Hy):
        wdc_copy(k).wait_send()
    for b in range(BATCHES):
        for p in range(len(peers)):
            f_copy(L - 1, b, p).wait_send()
            b_copy(2, b, p).wait_send()
            b_copy(1, b, p).wait_send()
    pgx_copy(1).wait_send()
    pgx_copy(0).wait_send()
    for n in range(3):
        for k in range(len(stages[n])):
            e_copy(n, k).wait_send()
    e_cross.wait_send()
    e_core.wait_send()
    dec_sum.drain()
    in_sum.drain()
    for k in range(1, RR):
        copy_to(W.at[0, :, 0 : 4 * KR, :], W.at[0, :, 0 : 4 * KR, :], B_s.at[k - 1], B_r.at[k - 1, 0, 0], r_dev(k)).wait_send()
    kept = grec_out.at[d, :, :, half]
    for i in range(3):
        copy_to(kept, kept, C_s.at[i], C_r.at[i], z_dev(i)).wait()
    pltpu.make_async_copy(kept, kept, C_s.at[3]).wait()
    own_small.wait()


def call_kernel(dims, *operands):
    R, RR, Hy, U, U2, NR, L, VP = dims.R, dims.RR, dims.Hy, dims.U, dims.U2, dims.NR, dims.L, dims.VP
    KR, EP, VS, H, RB, N_IN, N_DEC = dims.KR, dims.EP, dims.VS, dims.H, dims.RB, dims.N_IN, dims.N_DEC
    chips, peers, pieces = 2 * Hy, len(dims.peers), dims.pieces
    vmem, sem = pltpu.VMEM, pltpu.SemaphoreType.DMA
    apart = pl.BlockSpec(memory_space=pl.ANY)
    inside = pl.BlockSpec(memory_space=pltpu.VMEM)
    groups = max(RR - 1, 1)
    along = max(Hy - 1, 1)
    stages = 1 + peers + (RR - 1)
    id_rows = 2 * dims.P8 + 8
    scratch = [
        vmem((2, id_rows, 128), F32),
        vmem((4, id_rows, 128), F32),
        vmem((128, 128), F32),
        vmem((4, dims.RL // 2, 128), F32),
        vmem((8, VP), F32),
        vmem((ceil_to(dims.LANGS, 16), VP), F32),
        vmem((2, 8, U), F32),
        vmem((2, 4, EP, U), BF16),
        vmem((2, 4, H, U), BF16),
        vmem((chips, 2, U, VP), BF16),
        vmem((L, NR, EP), BF16),
        vmem((L, NR, EP), BF16),
        vmem((NR, VP), F32),
        vmem((2, 4, NR, U), F32),
        vmem((L, chips, NR, U2), BF16),
        vmem((L, chips, NR, U2), BF16),
        vmem((L, 4, 2, NR, U), F32),
        vmem((L + 1, 2, NR, U), F32),
        vmem((L, NR, VP), BF16),
        vmem((L, NR, VP), BF16),
        vmem((NR, 128), F32),
        vmem((8, VP), F32),
        vmem((2, NR, U), F32),
        vmem((2, NR, U), F32),
        vmem((2, 2, 4, NR, U), BF16),
        vmem((L, 4, NR, U), BF16),
        vmem((2, peers, NR, U2), BF16),
        vmem((2, peers, NR, U2), BF16),
        vmem((4, H, U), F32),
        vmem((4, EP, U), F32),
        vmem((VP, EP), F32),
        vmem((max(VP, N_DEC), U), F32),
        vmem((N_DEC, U), BF16),
        vmem((groups, N_DEC // RR, U), BF16),
        vmem((2, N_DEC, 2 * U), BF16),
        vmem((N_IN, U), BF16),
        vmem((groups, N_IN // RR, U), BF16),
        vmem((2, N_IN, 2 * U), BF16),
        vmem((groups, 4, 4, KR, U), BF16),
        vmem((VS, 128), F32),
        vmem((2, VS // 2, 128), F32),
        vmem((stages, VS // 2, 128), F32),
        vmem((2, VS, 128), F32),
        sem((4,)),
        sem((3,)), sem((3,)),
        sem((1,)), sem((1,)),
        sem((1,)), sem((1,)),
        sem((along,)), sem((along,)),
        sem((Hy,)), sem((Hy,)),
        sem((3,)), sem((3, pieces)),
        sem((groups,)), sem((4, groups, pieces)),
        sem((1,)), sem((1,)),
        sem((1,)), sem((1,)),
        sem((2, BATCHES, peers)), sem((2, BATCHES, peers)),
        sem((L,)), sem((L,)),
        sem((L,)), sem((L,)),
        sem((2, BATCHES, peers)), sem((2, BATCHES, peers)),
        sem((L,)), sem((L,)),
        sem((2, 2 * groups + 3)),
        sem((2, 2 * groups + 3)),
        sem((groups,)), sem((groups, 4, pieces)),
        sem((4,)), sem((3,)),
        sem((stages + 2,)), sem((stages + 2,)),
    ]
    rows = NR * L
    flops = 2 * rows * (3 * H * 8 * U + 3 * H * VP)
    return pl.pallas_call(
        functools.partial(kernel, dims),
        out_shape=(
            jax.ShapeDtypeStruct((2, 4, KR, 2 * U), BF16),
            jax.ShapeDtypeStruct((2, N_IN, 2 * U), BF16),
            jax.ShapeDtypeStruct((2, N_DEC, 2 * U), BF16),
            jax.ShapeDtypeStruct((2, VS, 128), F32),
        ),
        in_specs=[inside] * 5 + [apart] * 3 + [inside] * 3,
        out_specs=(apart, apart, apart, apart),
        scratch_shapes=scratch,
        cost_estimate=pl.CostEstimate(flops=flops, bytes_accessed=8 << 20, transcendentals=rows * U2 * 8),
        compiler_params=pltpu.CompilerParams(
            collective_id=0, has_side_effects=True, vmem_limit_bytes=62 << 20
        ),
        name="train_step",
    )(*operands)


def outputs_kernel(
    dims, grec, gwin, gwd, small, w_rec_out, w_in_out, b_in_out, b_rec_out, w_dec_out, emb_out, b_dec_out, loss_out
):
    for d in range(2):
        for q in range(4):
            w_rec_out[d, :, q, :] = grec[d, q].astype(F32)

    E, EW, V, V8 = dims.E, dims.EW, dims.V, dims.V8
    steps = pl.num_programs(0)

    @pl.when(pl.program_id(0) == 0)
    def _():
        for d in range(2):
            for q in range(4):
                w_in_out[d, :, q, :] = gwin[d, q * EW : q * EW + E].astype(F32)
                first = q * EW + E // 16 * 16
                row = gwin[d, first : first + 16].astype(F32)[E % 16 : E % 16 + 1]
                b_in_out[d, q : q + 1, :] = row
                b_rec_out[d, q : q + 1, :] = row

    @pl.when(pl.program_id(0) == steps // 4)
    def _():
        for d in range(2):
            w_dec_out[:, d, :] = gwd[d, 0:V].astype(F32)

    @pl.when(pl.program_id(0) == steps // 2)
    def _():
        for d in range(2):
            emb_out[:, d, :] = small[d, 0:V, 0:E]
            for k in range(dims.VP // 128):
                width = min(128, V - k * 128)
                b_dec_out[d : d + 1, k * 128 : k * 128 + width] = small[d, V8 + k : V8 + k + 1, 0:width]
        at = V8 + dims.VP // 128
        loss_out[...] = small[0, at : at + 1, 0:1] + small[1, at : at + 1, 0:1]


def call_outputs(dims, grec, gwin, gwd, small):
    KR, U2, E, V = dims.KR, dims.U2, dims.E, dims.V
    parts = 4 if KR % 64 == 0 else 1
    rows = KR // parts

    def whole(*shape):
        return pl.BlockSpec(shape, lambda i: (0,) * len(shape))

    shapes = ((2, E, 4, U2), (2, 4, U2), (2, 4, U2), (V, 2, U2), (V, 2, E), (2, V), (1, 1))
    return pl.pallas_call(
        functools.partial(outputs_kernel, dims),
        grid=(parts,),
        out_shape=[jax.ShapeDtypeStruct((2, KR, 4, U2), F32)] + [jax.ShapeDtypeStruct(s, F32) for s in shapes],
        in_specs=[
            pl.BlockSpec((2, 4, rows, U2), lambda i: (0, 0, i, 0)),
            whole(*gwin.shape), whole(*gwd.shape), whole(*small.shape),
        ],
        out_specs=[pl.BlockSpec((2, rows, 4, U2), lambda i: (0, i, 0, 0))] + [whole(*s) for s in shapes],
        compiler_params=pltpu.CompilerParams(vmem_limit_bytes=62 << 20),
        name="outputs",
    )(grec, gwin, gwd, small)


def local(
    char_ids, lang_ids, vocab_masks, targets, embedding, w_in, w_rec, b_in, b_rec, w_dec, b_dec
):
    R, hid = lax.axis_size("rows"), lax.axis_size("hid")
    RL, L = char_ids.shape
    E, units = w_in.shape[1], w_in.shape[3]
    V = embedding.shape[1]
    KR = w_rec.shape[1]
    U = units // 2
    dims = Dims(
        R=R, RR=R // 4, Hy=hid // 2, H=units * hid, KR=KR, U=U, RL=RL, L=L, V=V, E=E,
        LANGS=vocab_masks.shape[0], scale=1.0 / (RL * R * L),
    )
    VP, EP, EW = dims.VP, dims.EP, dims.EW

    win = jnp.pad(w_in.transpose(0, 2, 1, 3), ((0, 0), (0, 0), (0, EP - E), (0, 0)))
    wrec = w_rec.transpose(0, 2, 1, 3)
    wdec = jnp.pad(w_dec, ((0, 0), (0, 0), (0, VP - V))).reshape(2, 2, U, VP)
    emb = jnp.concatenate([embedding, jnp.ones((2, V, 1), BF16)], axis=2)
    emb = jnp.pad(emb, ((0, 0), (0, VP - V), (0, EP - E - 1)))

    sums = call_kernel(
        dims, char_ids.T, targets.transpose(0, 2, 1), lang_ids[None], b_in, b_rec, win, wrec, wdec, emb, b_dec,
        vocab_masks,
    )
    w_rec_grad, w_in_grad, b_in_grad, b_rec_grad, w_dec_grad, emb_grad, b_dec_grad, loss = call_outputs(dims, *sums)
    return (
        loss[0, 0],
        emb_grad.transpose(1, 0, 2),
        w_in_grad,
        w_rec_grad,
        b_in_grad,
        b_rec_grad,
        w_dec_grad.transpose(1, 2, 0),
        b_dec_grad,
    )


def solution(mesh):
    placed = (
        P("rows", None),
        P("rows"),
        P(),
        P(None, "rows", None),
        P(),
        P(None, None, None, "hid"),
        P(None, "rows", None, "hid"),
        P(None, None, "hid"),
        P(None, None, "hid"),
        P(None, "hid", None),
        P(),
    )
    return jax.shard_map(
        local,
        mesh=mesh,
        in_specs=placed,
        out_specs=(
            P(),
            P(),
            P(None, None, None, "hid"),
            P(None, "rows", None, "hid"),
            P(None, None, "hid"),
            P(None, None, "hid"),
            P(None, "hid", None),
            P(),
        ),
        check_vma=False,
    )
```

```python
import functools
from typing import NamedTuple

import jax
import jax.numpy as jnp
from jax import lax
from jax.experimental import pallas as pl
from jax.experimental.pallas import tpu as pltpu
from jax.sharding import PartitionSpec as P

MESH = pl.DeviceIdType.MESH
F32 = jnp.float32
BF16 = jnp.bfloat16
masked_value = -1000000000.0
ROW_PARTS = 2
AHEAD = 8
EARLY = 2
WINDOW = 3
BATCHES = 2


def ceil_to(n, m):
    return (n + m - 1) // m * m


class Dims(NamedTuple):
    R: int
    RR: int
    Hy: int
    H: int
    KR: int
    U: int
    RL: int
    L: int
    V: int
    E: int
    LANGS: int
    scale: float

    @property
    def U2(self):
        return 2 * self.U

    @property
    def NR(self):
        return 2 * self.RL

    @property
    def VP(self):
        return ceil_to(self.V, 128)

    @property
    def RB(self):
        return self.NR // BATCHES

    @property
    def QN(self):
        return 1 if self.RR <= 2 else 4

    @property
    def KP(self):
        return ROW_PARTS if self.RR <= 2 else 1

    @property
    def pieces(self):
        return 4 // self.QN * self.KP

    @property
    def KRP(self):
        return self.KR // self.KP

    @property
    def N_IN(self):
        return ceil_to(4 * self.EW, 16 * self.RR)

    @property
    def N_DEC(self):
        return ceil_to(self.V, 16 * self.RR)

    @property
    def P8(self):
        return ceil_to(self.L, 8)

    @property
    def EP(self):
        return ceil_to(self.E + 2, 128)

    @property
    def EW(self):
        return ceil_to(self.E + 2, 16)

    @property
    def V8(self):
        return ceil_to(self.V, 8)

    @property
    def VS(self):
        return ceil_to(self.V8 + 8, 16)

    @property
    def peers(self):
        far = [(1, k) for k in range(1, self.Hy)]
        beside = [(0, k) for k in range(1, self.Hy)]
        return far + beside + [(1, 0)]


Z_STEPS = ((1, 0), (1, 1), (0, 1))


def dot(a, b):
    return jnp.dot(a, b, preferred_element_type=F32)


def dot_nt(a, b):
    return lax.dot_general(a, b, (((1,), (1,)), ((), ())), preferred_element_type=F32)


def dot_tn(a, b):
    return lax.dot_general(a, b, (((0,), (0,)), ((), ())), preferred_element_type=F32)


def flip(bit, step):
    return 1 - bit if step else bit


def kernel(
    dims,
    chars_ref, targets_ref, lang_ref, b_in_ref, b_rec_ref, win_in, wrec_in, wdec_in, emb_ref, b_dec_ref, masks_ref,
    grec_out, gwin_out, gwd_out, small_out,
    idsrc, idsall, idtmp, ids, bdec, masks, bias, win, W, wd, x, xp, allowed, acc, st, stp, gs, cell, lg, lgp, lossv, gb,
    dh, cg, pg, pgx, psend, precv, dW, gwin, gemb, gwd, gwd_s, gwd_r, gwd_all, gwin_s, gwin_r, gwin_all,
    recvB, epart, esend, erecv, eall,
    lsem, ids_s, ids_r, win_s2, win_r2, bias_s, bias_r, wdy_s, wdy_r, wdc_s, wdc_r, wz_s, wz_r, wx_s, wx_r, wc_s, wc_r,
    xp_s, xp_r, f_s, f_r, stp_s, stp_r, lgp_s, lgp_r, b_s, b_r, pgx_s, pgx_r,
    gwd_sems, gwin_sems, B_s, B_r, C_s, C_r, e_s, e_r,
):
    R, RR, Hy, U, U2, NR, L, VP = dims.R, dims.RR, dims.Hy, dims.U, dims.U2, dims.NR, dims.L, dims.VP
    KR, EW, V8, VS, RL, RB, QN = dims.KR, dims.EW, dims.V8, dims.VS, dims.RL, dims.RB, dims.QN
    peers = dims.peers
    KP, KRP, pieces = dims.KP, dims.KRP, dims.pieces
    rho, hid = lax.axis_index("rows"), lax.axis_index("hid")
    d, g, r = rho // (R // 2), lax.rem(rho // RR, 2), lax.rem(rho, RR)
    y, c = hid // 2, lax.rem(hid, 2)
    mine = y * 2 + g
    part = d * 2 + g

    def dev(dd, gg, rr, yy, cc):
        return (dd * (R // 2) + gg * RR + rr, yy * 2 + cc)

    def copy_to(src, dst, send, recv, device):
        return pltpu.make_async_remote_copy(
            src_ref=src, dst_ref=dst, send_sem=send, recv_sem=recv, device_id=device, device_id_type=MESH
        )

    def add_r(step):
        return lax.rem(r + step, RR)

    def add_y(step):
        return lax.rem(y + step, Hy)

    def place_of(dd, gg, rr):
        index = dd * (R // 2) + gg * RR + rr
        per = U // KR
        block = index // per
        hid_of, g_of = block // 2, lax.rem(block, 2)
        return (hid_of // 2) * 2 + g_of, lax.rem(hid_of, 2) * U + lax.rem(index, per) * KR

    def rows_of(dd, gg, rr, n=None):
        chip, unit = place_of(dd, gg, rr)
        row = chip * U2 + unit
        if n is None:
            return pl.ds(pl.multiple_of(row, KR), KR)
        return pl.ds(pl.multiple_of(row + n % KP * KRP, KRP), KRP)

    def rows_in(n):
        return pl.ds(n % KP * KRP, KRP)

    def chip_rows(m):
        return pl.ds(pl.multiple_of(m * U2, U2), U2)

    partner = dev(d, g, r, y, 1 - c)
    half = pl.ds(pl.multiple_of(g * U, U), U)

    def z_dev(j):
        return dev(flip(d, Z_STEPS[j][0]), flip(g, Z_STEPS[j][1]), r, y, c)

    def r_dev(step):
        return dev(d, g, add_r(step), y, c)

    def y_dev(step):
        return dev(d, g, r, add_y(step), c)

    def peer_dev(p):
        return dev(d, flip(g, peers[p][0]), r, add_y(peers[p][1]), c)

    barrier = pltpu.get_barrier_semaphore()
    greeted = [z_dev(j) for j in range(3)] + [r_dev(k) for k in range(1, RR)] + [partner]
    greeted += [peer_dev(p) for p in range(len(peers)) if peers[p] != (1, 0)]
    for device in greeted:
        pl.semaphore_signal(barrier, inc=1, device_id=device, device_id_type=MESH)
    pl.semaphore_wait(barrier, len(greeted))

    def ids_copy(j):
        return copy_to(idsrc.at[flip(d, Z_STEPS[j][0])], idsall.at[part], ids_s.at[j], ids_r.at[j], z_dev(j))

    def gates_of(n):
        return pl.ds(n // KP * QN, QN)

    def wz_copy(j, n):
        columns = pl.ds(pl.multiple_of(flip(g, Z_STEPS[j][1]) * U, U), U)
        there = wrec_in.at[flip(d, Z_STEPS[j][0]), gates_of(n), rows_in(n), columns]
        return copy_to(there, W.at[c, gates_of(n), rows_of(d, g, r, n), :], wz_s.at[j], wz_r.at[j, n], z_dev(j))

    def z_block(j):
        steps = Z_STEPS[j] if j < 3 else (0, 0)
        return flip(d, steps[0]), flip(g, steps[1])

    def w_block(core, j, k, n):
        dd, gg = z_block(j)
        return W.at[core, gates_of(n), rows_of(dd, gg, lax.rem(r + RR - k, RR), n), :]

    def wx_copy(j, k, n):
        block = w_block(c, j, 0, n)
        return copy_to(block, block, wx_s.at[k - 1], wx_r.at[j, k - 1, n], r_dev(k))

    def wc_copy(j, k, n):
        block = w_block(c, j, k, n)
        return copy_to(block, block, wc_s.at[0], wc_r.at[0], partner)

    def wc_all(core):
        return copy_to(W.at[core], W.at[core], wc_s.at[0], wc_r.at[0], partner)

    def wd_rows(yy):
        return wd.at[pl.ds(yy * 2, 2), c]

    def wdy_copy(k):
        return copy_to(wdec_in.at[d], wd_rows(y), wdy_s.at[k - 1], wdy_r.at[k - 1], y_dev(k))

    def wdc_copy(k):
        yy = lax.rem(y + Hy - k, Hy)
        return copy_to(wd_rows(yy), wd_rows(yy), wdc_s.at[k], wdc_r.at[k], partner)

    win_copy = copy_to(win_in.at[d, :, :, half], win.at[c], win_s2.at[0], win_r2.at[0], partner)
    bias_copy = copy_to(bias.at[c], bias.at[c], bias_s.at[0], bias_r.at[0], partner)
    own_win = pltpu.make_async_copy(win_in.at[d, :, :, half], win.at[c], lsem.at[1])
    own_wd = pltpu.make_async_copy(wdec_in.at[d], wd_rows(y), lsem.at[2])
    own_w = pltpu.make_async_copy(
        wrec_in.at[d, :, :, half], W.at[c, :, rows_of(d, g, r), :], lsem.at[3]
    )

    own_w.start()
    for n in range(min(WINDOW, pieces)):
        for j in range(3):
            wz_copy(j, n).start()
    own_win.start()
    win_copy.start()
    for k in range(1, Hy):
        wdy_copy(k).start()
    own_wd.start()

    P8 = dims.P8
    idsrc[...] = jnp.zeros_like(idsrc)
    for dd in range(2):
        idsrc[dd, 0:L, 0:RL] = chars_ref[...].astype(F32)
        idsrc[dd, P8 : P8 + L, 0:RL] = targets_ref[dd].astype(F32)
        idsrc[dd, 2 * P8 : 2 * P8 + 8, 0:RL] = jnp.broadcast_to(lang_ref[...].astype(F32), (8, RL))
    for j in range(3):
        ids_copy(j).start()
    bias[c, 0:4] = b_in_ref[d, :, half].astype(F32) + b_rec_ref[d, :, half].astype(F32)
    bias_copy.start()
    idsall[part] = idsrc[d]

    own_w.wait()
    for n in range(pieces):
        for k in range(1, RR):
            wx_copy(3, k, n).start()
        wc_copy(3, 0, n).start()

    dW[...] = jnp.zeros_like(dW)
    gwin[...] = jnp.zeros_like(gwin)
    gemb[...] = jnp.zeros_like(gemb)
    lossv[...] = jnp.zeros_like(lossv)
    gb[...] = jnp.zeros_like(gb)
    cg[...] = jnp.zeros_like(cg)
    cell[0] = jnp.zeros_like(cell[0])
    bdec[...] = jnp.zeros_like(bdec)
    bdec[0:2, 0 : dims.V] = b_dec_ref[...].astype(F32)
    masks[...] = jnp.zeros_like(masks)
    masks[0 : dims.LANGS, 0 : dims.V] = masks_ref[...].astype(F32)
    idtmp[...] = jnp.zeros_like(idtmp)

    for j in range(3):
        ids_copy(j).wait_recv()
    for n in range(4):
        idtmp[:, 0 : idsall.shape[1]] = idsall[n].T
        ids[n] = idtmp[pl.ds(pl.multiple_of(c * (RL // 2), RL // 2), RL // 2), :]

    lane = lax.broadcasted_iota(jnp.int32, (NR, 128), 1)
    vocab = lax.broadcasted_iota(jnp.int32, (NR, VP), 1).astype(F32)

    def id_column(at):
        held = ids[...].reshape(NR, 128)
        return jnp.sum(jnp.where(lane == at, held, 0.0), axis=1, keepdims=True)

    def place(t):
        return t + d * (L - 1 - 2 * t)

    def char_hot(t):
        return jnp.where(vocab == id_column(place(t)), 1.0, 0.0).astype(BF16)

    lang_lane = lax.broadcasted_iota(jnp.int32, (NR, masks.shape[0]), 1).astype(F32)
    lang_hot = jnp.where(lang_lane == id_column(2 * P8), 1.0, 0.0).astype(BF16)
    allowed[...] = dot(lang_hot, masks[...].astype(BF16))

    @pl.loop(0, L)
    def _(t):
        x[t] = dot(char_hot(t), emb_ref[d]).astype(BF16)

    xp_copy = copy_to(x, xp, xp_s.at[0], xp_r.at[0], partner)
    xp_copy.start()

    own_wd.wait()
    wdc_copy(0).start()
    own_win.wait()
    win_copy.wait_recv()
    bias_copy.wait_recv()

    def part_rows(b):
        return pl.ds(b * RB, RB)

    def f_copy(t, b, p):
        slot = lax.rem(t, 2)
        block = st.at[t, mine, part_rows(b), :]
        return copy_to(block, block, f_s.at[slot, b, p], f_r.at[slot, b, p], peer_dev(p))

    def gates(t, b):
        rows = part_rows(b)
        for cc in range(2):
            si = jax.nn.sigmoid(acc[cc, 0, rows])
            sf = jax.nn.sigmoid(acc[cc, 1, rows])
            tg = jnp.tanh(acc[cc, 2, rows])
            so = jax.nn.sigmoid(acc[cc, 3, rows])
            new = sf * cell[t, cc, rows] + si * tg
            cell[t + 1, cc, rows] = new
            st[t, mine, rows, cc * U : (cc + 1) * U] = (so * jnp.tanh(new)).astype(BF16)
            gs[t, 0, cc, rows] = si
            gs[t, 1, cc, rows] = sf
            gs[t, 2, cc, rows] = tg
            gs[t, 3, cc, rows] = so

    def peer_block(p):
        yy = lax.rem(y + Hy - peers[p][1], Hy)
        return yy * 2 + flip(g, peers[p][0])

    for cc in range(2):
        for q in range(4):
            acc[cc, q] = dot(x[0], win[cc, q]) + bias[cc, q : q + 1]
    for b in range(BATCHES):
        gates(0, b)
        for p in range(len(peers)):
            f_copy(0, b, p).start()

    for k in range(1, Hy):
        wdy_copy(k).wait_recv()
        wdc_copy(k).start()
    from_z, beside = [], [(2, n) for n in range(pieces)]
    for n in range(pieces):
        from_z += beside[2 * n : 2 * n + 2] + [(0, n), (1, n)]
    from_x = [(3, n) for n in range(pieces)] + from_z
    for at in range(len(from_x)):
        if at < len(from_z):
            j, n = from_z[at]
            wz_copy(j, n).wait_recv()
            for k in range(1, RR):
                wx_copy(j, k, n).start()
            wc_copy(j, 0, n).start()
            if n + WINDOW < pieces:
                wz_copy(j, n + WINDOW).start()
        j, n = from_x[at]
        for k in range(1, RR):
            wx_copy(j, k, n).wait_recv()
            wc_copy(j, k, n).start()
    wc_all(1 - c).wait_recv()
    for k in range(Hy):
        yy = lax.rem(y + Hy - k, Hy)
        other = wd.at[pl.ds(yy * 2, 2), 1 - c]
        copy_to(other, other, wdc_s.at[k], wdc_r.at[k], partner).wait_recv()

    def stp_copy(t):
        return copy_to(st.at[t], stp.at[t], stp_s.at[t], stp_r.at[t], partner)

    def lgp_copy(t):
        return copy_to(lg.at[t], lgp.at[t], lgp_s.at[t], lgp_r.at[t], partner)

    def decode(t):
        stp_copy(t).start()
        logits = bdec[pl.ds(d, 1), :]
        for m in range(2 * Hy):
            logits = logits + dot(st[t, m], wd[m].reshape(U2, VP))
        masked = jnp.where(allowed[...] > 0.5, logits, masked_value)
        top = jnp.max(masked, axis=1, keepdims=True)
        powers = jnp.exp(masked - top)
        total = jnp.sum(powers, axis=1, keepdims=True)
        hot = vocab == id_column(P8 + place(t))
        picked = jnp.sum(jnp.where(hot, logits, 0.0), axis=1, keepdims=True)
        lossv[...] += jnp.broadcast_to(top + jnp.log(total) - picked, (NR, 128))
        grad = ((powers / total - jnp.where(hot, 1.0, 0.0)) * dims.scale).astype(BF16)
        lg[t] = grad
        gb[0:1, :] += jnp.sum(grad.astype(F32), axis=0, keepdims=True)
        lgp_copy(t).start()

    @pl.loop(1, L)
    def _(t):
        for cc in range(2):
            for q in range(4):
                start = dot(x[t], win[cc, q]) + bias[cc, q : q + 1]
                acc[cc, q] = start + dot(st[t - 1, mine], W[cc, q, chip_rows(mine), :])
        for b in range(BATCHES):
            rows = part_rows(b)
            for p in reversed(range(len(peers))):
                f_copy(t - 1, b, p).wait_recv()
                m = peer_block(p)
                for cc in range(2):
                    for q in range(4):
                        acc[cc, q, rows] += dot(st[t - 1, m, rows], W[cc, q, chip_rows(m), :])
            gates(t, b)
            for p in range(len(peers)):
                f_copy(t - 1, b, p).wait_send()
            for p in reversed(range(len(peers))):
                f_copy(t, b, p).start()
        decode(t - 1)

    block = wrec_in.at[d, :, :, half]
    for j in range(3):
        copy_to(block, block, wz_s.at[j], wz_r.at[j, 0], z_dev(j)).wait_send()
    blocks = W.at[c, :, 0 : 4 * KR, :]
    for k in range(1, RR):
        copy_to(blocks, blocks, wx_s.at[k - 1], wx_r.at[0, k - 1, 0], r_dev(k)).wait_send()
    wc_all(c).wait_send()

    @pl.loop(0, dims.H // U)
    def _(k):
        rows = pl.ds(pl.multiple_of(k * U, U), U)
        for cc in range(2):
            for q in range(4):
                W[cc, q, rows, :] = W[cc, q, rows, :].T

    for b in range(BATCHES):
        for p in reversed(range(len(peers))):
            f_copy(L - 1, b, p).wait_recv()
    decode(L - 1)

    def dec_back(t, cc):
        return dot_nt(lg[t], wd[mine, cc])

    def b_copy(t, b, p):
        slot = lax.rem(t, 2)
        there = precv.at[slot, p, part_rows(b), :]
        return copy_to(
            psend.at[slot, p, part_rows(b), :], there, b_s.at[slot, b, p], b_r.at[slot, b, p], peer_dev(p)
        )

    def pgx_copy(t):
        return copy_to(pg.at[lax.rem(t, 2), 1 - c], pgx.at[t], pgx_s.at[t], pgx_r.at[t], partner)

    def preact_grads(t, b):
        slot = lax.rem(t, 2)
        rows = part_rows(b)
        for cc in range(2):
            h = dh[cc, rows]
            si, sf, tg, so = (gs[t, q, cc, rows] for q in range(4))
            tc = jnp.tanh(cell[t + 1, cc, rows])
            total = cg[cc, rows] + h * so * (1.0 - tc * tc)
            pg[slot, cc, 0, rows] = (total * tg * si * (1.0 - si)).astype(BF16)
            pg[slot, cc, 1, rows] = (total * cell[t, cc, rows] * sf * (1.0 - sf)).astype(BF16)
            pg[slot, cc, 2, rows] = (total * si * (1.0 - tg * tg)).astype(BF16)
            pg[slot, cc, 3, rows] = (h * tc * so * (1.0 - so)).astype(BF16)
            cg[cc, rows] = total * sf

    def partial(t, rows_here, m, cc):
        slot = lax.rem(t, 2)
        rows = pl.ds(pl.multiple_of(m * U2 + cc * U, U), U)
        total = None
        for kk in range(2):
            for q in range(4):
                term = dot(pg[slot, kk, q, rows_here], W[kk, q, rows, :])
                total = term if total is None else total + term
        return total

    def take_state_grad(t, b):
        slot = lax.rem(t, 2)
        rows = part_rows(b)
        for p in reversed(range(len(peers))):
            b_copy(t, b, p).wait_recv()
            for cc in range(2):
                dh[cc, rows] += precv[slot, p, rows, cc * U : (cc + 1) * U].astype(F32)

    def both_cores(t, q):
        return jnp.concatenate([pg[lax.rem(t, 2), c, q], pgx[t, q]], axis=0)

    def rec_grads(t):
        for q in range(4):
            both = both_cores(t, q)
            for m in range(2 * Hy):
                states = jnp.concatenate([st[t - 1, m], stp[t - 1, m]], axis=0)
                dW[q, m * U2 : (m + 1) * U2, :] += dot_tn(states, both)

    def in_grads(t):
        slot = lax.rem(t, 2)
        inputs = jnp.concatenate([x[t], xp[t]], axis=0)
        for q in range(4):
            gwin[q] += dot_tn(inputs, both_cores(t, q))
        back = None
        for cc in range(2):
            for q in range(4):
                term = dot_nt(pg[slot, cc, q], win[cc, q])
                back = term if back is None else back + term
        high = back.astype(BF16)
        rest = (back - high.astype(F32)).astype(BF16)
        hot = char_hot(t)
        gemb[...] += dot_tn(hot, high) + dot_tn(hot, rest)

    class SmallSum:
        def __init__(self, send, recv, whole, out, sems, own_sem):
            self.send, self.recv, self.whole, self.out, self.sems, self.own = send, recv, whole, out, sems, own_sem
            self.share = whole.shape[1] // RR

        def rows(self, rr):
            return pl.ds(pl.multiple_of(rr * self.share, 16), self.share)

        def pair(self, at):
            return self.sems.at[0, at], self.sems.at[1, at]

        def first(self, k):
            return copy_to(self.send.at[self.rows(add_r(k)), :], self.recv.at[k - 1], *self.pair(k - 1), r_dev(k))

        def block(self, dd, gg):
            return self.whole.at[dd, self.rows(r), pl.ds(pl.multiple_of(gg * U, U), U)]

        def along(self, j):
            block = self.block(1 - d, g) if j == 1 else self.block(d, g)
            return copy_to(block, block, *self.pair(RR - 1 + j), z_dev(0 if j == 0 else 2))

        def last(self, k):
            block = self.whole.at[:, self.rows(r), :]
            return copy_to(block, block, *self.pair(RR + 2 + k - 1), r_dev(k))

        def to_out(self):
            return pltpu.make_async_copy(self.whole, self.out, self.own)

        def start(self):
            for k in range(1, RR):
                self.first(k).start()

        def add(self, value):
            for k in range(1, RR):
                self.first(k).wait_recv()
                value = value + self.recv[k - 1].astype(F32)
            self.whole[d, self.rows(r), half] = value.astype(BF16)
            self.along(0).start()
            self.along(2).start()

        def relay(self):
            self.along(0).wait_recv()
            self.along(1).start()

        def spread(self):
            self.along(2).wait_recv()
            self.along(1).wait_recv()
            for k in range(1, RR):
                self.last(k).start()

        def finish(self):
            for k in range(1, RR):
                self.last(k).wait_recv()
            self.to_out().start()

        def drain(self):
            for k in range(1, RR):
                self.first(k).wait_send()
                self.last(k).wait_send()
            for j in range(3):
                self.along(j).wait_send()
            self.to_out().wait()

    dec_sum = SmallSum(gwd_s, gwd_r, gwd_all, gwd_out, gwd_sems, lsem.at[0])
    in_sum = SmallSum(gwin_s, gwin_r, gwin_all, gwin_out, gwin_sems, lsem.at[1])

    def decoder_grad():
        gwd[...] = jnp.zeros_like(gwd)

        @pl.loop(0, L)
        def _(t):
            columns = pl.ds(pl.multiple_of(c * U, U), U)
            states = jnp.concatenate([st[t, mine, :, columns], stp[t, mine, :, columns]], axis=0)
            gwd[...] += dot_tn(jnp.concatenate([lg[t], lgp[t]], axis=0), states)

        gwd_s[...] = gwd[0 : dims.N_DEC].astype(BF16)
        dec_sum.start()

    for cc in range(2):
        dh[cc] = dec_back(L - 1, cc)

    @pl.loop(0, L - 1)
    def _(i):
        t = L - 1 - i
        slot = lax.rem(t, 2)

        @pl.when(i > 1)
        def _():
            pgx_copy(t + 2).wait_send()

        for b in range(BATCHES):
            rows = part_rows(b)

            @pl.when(i > 0)
            def _():
                take_state_grad(t + 1, b)

            @pl.when(i > 1)
            def _():
                for p in range(len(peers)):
                    b_copy(t + 2, b, p).wait_send()

            preact_grads(t, b)
            for p in range(len(peers)):
                m = add_y(peers[p][1]) * 2 + flip(g, peers[p][0])
                for cc in range(2):
                    psend[slot, p, rows, cc * U : (cc + 1) * U] = partial(t, rows, m, cc).astype(BF16)
                b_copy(t, b, p).start()
        pgx_copy(t).start()
        for cc in range(2):
            dh[cc] = partial(t, pl.ds(0, NR), mine, cc) + dec_back(t - 1, cc)

        @pl.when(i > 0)
        def _():
            pgx_copy(t + 1).wait_recv()
            rec_grads(t + 1)

        @pl.when((i > 0) & (i < L - 2))
        def _():
            in_grads(t + 1)

        @pl.when(i == 0)
        def _():
            xp_copy.wait()

            @pl.loop(0, L)
            def _(at):
                stp_copy(at).wait()
                lgp_copy(at).wait()

            decoder_grad()

        @pl.when(i == 1)
        def _():
            dec_sum.add(gwd[dec_sum.rows(r), :])

        @pl.when(i == 2)
        def _():
            dec_sum.relay()

        @pl.when(i == 3)
        def _():
            dec_sum.spread()

        @pl.when(i == 4)
        def _():
            dec_sum.finish()

    out_steps = ((1, 0), (1, 1), (0, 1), (0, 0))

    def out_device(i, step):
        return flip(d, out_steps[i][0]), flip(g, out_steps[i][1]), add_r(step)

    def out_rows(i, step, n):
        return rows_of(*out_device(i, step), n)

    def b_out(i, k, n):
        return copy_to(
            W.at[0, gates_of(n), out_rows(i, k, n), :], recvB.at[k - 1, i, gates_of(n), rows_in(n), :],
            B_s.at[k - 1], B_r.at[k - 1, i, n], r_dev(k),
        )

    def c_out(i, n):
        there = grec_out.at[d, gates_of(n), rows_in(n), half]
        return copy_to(W.at[1, gates_of(n), out_rows(i, 0, n), :], there, C_s.at[i], C_r.at[i], z_dev(i))

    def own_out(n):
        there = grec_out.at[d, gates_of(n), rows_in(n), half]
        return pltpu.make_async_copy(W.at[1, gates_of(n), out_rows(3, 0, n), :], there, C_s.at[3])

    def gates_in(n):
        return range(n // KP * QN, (n // KP + 1) * QN)

    fused = KRP % 128 == 0

    def rec_piece(i, step, n, q):
        total = dW[q, out_rows(i, step, n), :]
        if fused:
            chip, unit = place_of(*out_device(i, step))
            units = pl.ds(pl.multiple_of(unit + n % KP * KRP, 128), KRP)
            states = jnp.concatenate([st[0, chip, :, units], stp[0, chip, :, units]], axis=0)
            total = total + dot_tn(states, both_cores(1, q))
        return total

    steps = [(i, n) for n in range(pieces) for i in (0, 2, 1, 3)]

    def send_over(at):
        i, n = steps[at]
        for k in range(1, RR):
            for q in gates_in(n):
                W[0, q, out_rows(i, k, n), :] = rec_piece(i, k, n, q).astype(BF16)
            b_out(i, k, n).start()

    def send_home(at):
        i, n = steps[at]
        for k in range(1, RR):
            b_out(i, k, n).wait_recv()
        for q in gates_in(n):
            total = rec_piece(i, 0, n, q)
            for k in range(1, RR):
                total = total + recvB[k - 1, i, q, rows_in(n), :].astype(F32)
            W[1, q, out_rows(i, 0, n), :] = total.astype(BF16)
        if i < 3:
            c_out(i, n).start()
        else:
            own_out(n).start()
        if at + ahead < len(steps):
            send_over(at + ahead)

    pgx_copy(1).wait_recv()
    if not fused:
        rec_grads(1)
    ahead = min(AHEAD, len(steps))
    for at in range(ahead):
        send_over(at)
    in_grads(2)
    in_grads(1)

    pgx_copy(2).wait_send()
    sent = 0
    for b in range(BATCHES):
        take_state_grad(1, b)
        preact_grads(0, b)
        for at in range(sent, min(sent + EARLY, len(steps))):
            send_home(at)
        sent = min(sent + EARLY, len(steps))
    pgx_copy(0).start()
    for at in range(sent, min(sent + EARLY, len(steps))):
        send_home(at)
    sent = min(sent + EARLY, len(steps))
    pgx_copy(0).wait_recv()
    in_grads(0)

    gwin_s[...] = jnp.zeros_like(gwin_s)
    for q in range(4):
        gwin_s[q * EW : (q + 1) * EW] = gwin[q, 0:EW].astype(BF16)
    in_sum.start()

    once = jnp.where(mine == 0, 1.0, 0.0).astype(F32)
    epart[0:V8] = gemb[0:V8]
    epart[V8:VS] = jnp.zeros((VS - V8, 128), F32)
    for k in range(VP // 128):
        epart[V8 + k : V8 + k + 1] = gb[0:1, k * 128 : (k + 1) * 128] * once
    at = V8 + VP // 128
    epart[at : at + 1] = jnp.sum(lossv[...], axis=0, keepdims=True) * (once * dims.scale)

    stages = [[partner], [peer_dev(p) for p in range(len(peers))], [r_dev(k) for k in range(1, RR)]]
    first = [sum(len(s) for s in stages[:n]) for n in range(len(stages) + 1)]

    def e_half(core):
        return pl.ds(pl.multiple_of(core * (VS // 2), 8), VS // 2)

    def e_copy(n, k):
        at = first[n] + k
        there = epart.at[e_half(1 - c), :] if n == 0 else esend.at[n - 1]
        return copy_to(there, erecv.at[at], e_s.at[at], e_r.at[at], stages[n][k])

    def e_start(n):
        for k in range(len(stages[n])):
            e_copy(n, k).start()

    def e_take(n):
        total = epart[e_half(c), :] if n == 0 else esend[n - 1]
        for k in range(len(stages[n])):
            e_copy(n, k).wait_recv()
            total = total + erecv[first[n] + k]
        if n < 2:
            esend[n] = total
            e_start(n + 1)
        else:
            eall[d, e_half(c), :] = total
            e_cross.start()

    e_cross = copy_to(
        eall.at[d, e_half(c), :], eall.at[d, e_half(c), :], e_s.at[first[3]], e_r.at[first[3]], z_dev(0)
    )
    e_core = copy_to(
        eall.at[:, e_half(c), :], eall.at[:, e_half(c), :], e_s.at[first[3] + 1], e_r.at[first[3] + 1], partner
    )
    own_small = pltpu.make_async_copy(eall, small_out, lsem.at[2])

    def in_share():
        in_f32 = jnp.concatenate([gwin[q, 0:EW] for q in range(4)], axis=0)
        if dims.N_IN > 4 * EW:
            in_f32 = jnp.concatenate([in_f32, jnp.zeros((dims.N_IN - 4 * EW, U), F32)], axis=0)
        share = in_sum.share
        total = in_f32[0:share]
        for k in range(1, RR):
            total = jnp.where(r == k, in_f32[k * share : (k + 1) * share], total)
        return total

    def e_gather():
        e_cross.wait_recv()
        e_core.start()

    def e_finish():
        e_core.wait_recv()
        own_small.start()

    e_start(0)
    between = [
        (0.1, lambda: e_take(0)),
        (0.3, lambda: in_sum.add(in_share())),
        (0.3, lambda: e_take(1)),
        (0.5, lambda: e_take(2)),
        (0.6, in_sum.relay),
        (0.8, e_gather),
        (0.85, in_sum.spread),
        (0.9, e_finish),
        (1.0, in_sum.finish),
    ]
    for at in range(sent, len(steps)):
        send_home(at)
        while between and (at + 1 - sent) >= between[0][0] * (len(steps) - sent):
            between.pop(0)[1]()
    for _, event in between:
        event()

    for j in range(3):
        ids_copy(j).wait_send()
    win_copy.wait_send()
    bias_copy.wait_send()
    for k in range(1, Hy):
        wdy_copy(k).wait_send()
    for k in range(Hy):
        wdc_copy(k).wait_send()
    for b in range(BATCHES):
        for p in range(len(peers)):
            f_copy(L - 1, b, p).wait_send()
            b_copy(2, b, p).wait_send()
            b_copy(1, b, p).wait_send()
    pgx_copy(1).wait_send()
    pgx_copy(0).wait_send()
    for n in range(3):
        for k in range(len(stages[n])):
            e_copy(n, k).wait_send()
    e_cross.wait_send()
    e_core.wait_send()
    dec_sum.drain()
    in_sum.drain()
    for k in range(1, RR):
        copy_to(W.at[0, :, 0 : 4 * KR, :], W.at[0, :, 0 : 4 * KR, :], B_s.at[k - 1], B_r.at[k - 1, 0, 0], r_dev(k)).wait_send()
    kept = grec_out.at[d, :, :, half]
    for i in range(3):
        copy_to(kept, kept, C_s.at[i], C_r.at[i], z_dev(i)).wait()
    pltpu.make_async_copy(kept, kept, C_s.at[3]).wait()
    own_small.wait()


def call_kernel(dims, *operands):
    R, RR, Hy, U, U2, NR, L, VP = dims.R, dims.RR, dims.Hy, dims.U, dims.U2, dims.NR, dims.L, dims.VP
    KR, EP, VS, H, RB, N_IN, N_DEC = dims.KR, dims.EP, dims.VS, dims.H, dims.RB, dims.N_IN, dims.N_DEC
    chips, peers, pieces = 2 * Hy, len(dims.peers), dims.pieces
    vmem, sem = pltpu.VMEM, pltpu.SemaphoreType.DMA
    apart = pl.BlockSpec(memory_space=pl.ANY)
    inside = pl.BlockSpec(memory_space=pltpu.VMEM)
    groups = max(RR - 1, 1)
    along = max(Hy - 1, 1)
    stages = 1 + peers + (RR - 1)
    id_rows = 2 * dims.P8 + 8
    scratch = [
        vmem((2, id_rows, 128), F32),
        vmem((4, id_rows, 128), F32),
        vmem((128, 128), F32),
        vmem((4, dims.RL // 2, 128), F32),
        vmem((8, VP), F32),
        vmem((ceil_to(dims.LANGS, 16), VP), F32),
        vmem((2, 8, U), F32),
        vmem((2, 4, EP, U), BF16),
        vmem((2, 4, H, U), BF16),
        vmem((chips, 2, U, VP), BF16),
        vmem((L, NR, EP), BF16),
        vmem((L, NR, EP), BF16),
        vmem((NR, VP), F32),
        vmem((2, 4, NR, U), F32),
        vmem((L, chips, NR, U2), BF16),
        vmem((L, chips, NR, U2), BF16),
        vmem((L, 4, 2, NR, U), F32),
        vmem((L + 1, 2, NR, U), F32),
        vmem((L, NR, VP), BF16),
        vmem((L, NR, VP), BF16),
        vmem((NR, 128), F32),
        vmem((8, VP), F32),
        vmem((2, NR, U), F32),
        vmem((2, NR, U), F32),
        vmem((2, 2, 4, NR, U), BF16),
        vmem((L, 4, NR, U), BF16),
        vmem((2, peers, NR, U2), BF16),
        vmem((2, peers, NR, U2), BF16),
        vmem((4, H, U), F32),
        vmem((4, EP, U), F32),
        vmem((VP, EP), F32),
        vmem((max(VP, N_DEC), U), F32),
        vmem((N_DEC, U), BF16),
        vmem((groups, N_DEC // RR, U), BF16),
        vmem((2, N_DEC, 2 * U), BF16),
        vmem((N_IN, U), BF16),
        vmem((groups, N_IN // RR, U), BF16),
        vmem((2, N_IN, 2 * U), BF16),
        vmem((groups, 4, 4, KR, U), BF16),
        vmem((VS, 128), F32),
        vmem((2, VS // 2, 128), F32),
        vmem((stages, VS // 2, 128), F32),
        vmem((2, VS, 128), F32),
        sem((4,)),
        sem((3,)), sem((3,)),
        sem((1,)), sem((1,)),
        sem((1,)), sem((1,)),
        sem((along,)), sem((along,)),
        sem((Hy,)), sem((Hy,)),
        sem((3,)), sem((3, pieces)),
        sem((groups,)), sem((4, groups, pieces)),
        sem((1,)), sem((1,)),
        sem((1,)), sem((1,)),
        sem((2, BATCHES, peers)), sem((2, BATCHES, peers)),
        sem((L,)), sem((L,)),
        sem((L,)), sem((L,)),
        sem((2, BATCHES, peers)), sem((2, BATCHES, peers)),
        sem((L,)), sem((L,)),
        sem((2, 2 * groups + 3)),
        sem((2, 2 * groups + 3)),
        sem((groups,)), sem((groups, 4, pieces)),
        sem((4,)), sem((3,)),
        sem((stages + 2,)), sem((stages + 2,)),
    ]
    rows = NR * L
    flops = 2 * rows * (3 * H * 8 * U + 3 * H * VP)
    return pl.pallas_call(
        functools.partial(kernel, dims),
        out_shape=(
            jax.ShapeDtypeStruct((2, 4, KR, 2 * U), BF16),
            jax.ShapeDtypeStruct((2, N_IN, 2 * U), BF16),
            jax.ShapeDtypeStruct((2, N_DEC, 2 * U), BF16),
            jax.ShapeDtypeStruct((2, VS, 128), F32),
        ),
        in_specs=[inside] * 5 + [apart] * 3 + [inside] * 3,
        out_specs=(apart, apart, apart, apart),
        scratch_shapes=scratch,
        cost_estimate=pl.CostEstimate(flops=flops, bytes_accessed=8 << 20, transcendentals=rows * U2 * 8),
        compiler_params=pltpu.CompilerParams(
            collective_id=0, has_side_effects=True, vmem_limit_bytes=62 << 20
        ),
        name="train_step",
    )(*operands)


def outputs_kernel(
    dims, grec, gwin, gwd, small, w_rec_out, w_in_out, b_in_out, b_rec_out, w_dec_out, emb_out, b_dec_out, loss_out,
    w_in_all, w_dec_all, emb_all, sems,
):
    for d in range(2):
        for q in range(4):
            w_rec_out[d, :, q, :] = grec[d, q].astype(F32)

    E, EW, V, V8 = dims.E, dims.EW, dims.V, dims.V8
    steps = pl.num_programs(0)
    V8, E8 = dims.V8, w_in_all.shape[1]
    copies = [
        pltpu.make_async_copy(w_in_all.at[:, 0:E], w_in_out, sems.at[0]),
        pltpu.make_async_copy(w_dec_all.at[0:V], w_dec_out, sems.at[1]),
        pltpu.make_async_copy(emb_all.at[0:V], emb_out, sems.at[2]),
    ]

    @pl.when(pl.program_id(0) == 0)
    def _():
        for d in range(2):
            for q in range(4):
                w_in_all[d, :, q, :] = gwin[d, q * EW : q * EW + EW].astype(F32)[0:E8]
                first = q * EW + E // 16 * 16
                row = gwin[d, first : first + 16].astype(F32)[E % 16 : E % 16 + 1]
                b_in_out[d, q : q + 1, :] = row
                b_rec_out[d, q : q + 1, :] = row
        copies[0].start()

    @pl.when(pl.program_id(0) == steps // 4)
    def _():
        for d in range(2):
            w_dec_all[:, d, :] = gwd[d].astype(F32)[0:V8]
        copies[1].start()

    @pl.when(pl.program_id(0) == steps // 2)
    def _():
        for d in range(2):
            emb_all[:, d, :] = small[d, 0:V8, 0:E]
            for k in range(dims.VP // 128):
                width = min(128, V - k * 128)
                b_dec_out[d : d + 1, k * 128 : k * 128 + width] = small[d, V8 + k : V8 + k + 1, 0:width]
        at = V8 + dims.VP // 128
        loss_out[...] = small[0, at : at + 1, 0:1] + small[1, at : at + 1, 0:1]
        copies[2].start()

    @pl.when(pl.program_id(0) == steps - 1)
    def _():
        for copy in copies:
            copy.wait()


def call_outputs(dims, grec, gwin, gwd, small):
    KR, U2, E, V = dims.KR, dims.U2, dims.E, dims.V
    parts = 4 if KR % 64 == 0 else 1
    rows = KR // parts
    apart = pl.BlockSpec(memory_space=pl.ANY)

    def whole(*shape):
        return pl.BlockSpec(shape, lambda i: (0,) * len(shape))

    shapes = ((2, E, 4, U2), (2, 4, U2), (2, 4, U2), (V, 2, U2), (V, 2, E), (2, V), (1, 1))
    return pl.pallas_call(
        functools.partial(outputs_kernel, dims),
        grid=(parts,),
        out_shape=[jax.ShapeDtypeStruct((2, KR, 4, U2), F32)] + [jax.ShapeDtypeStruct(s, F32) for s in shapes],
        in_specs=[
            pl.BlockSpec((2, 4, rows, U2), lambda i: (0, 0, i, 0)),
            whole(*gwin.shape), whole(*gwd.shape), whole(*small.shape),
        ],
        out_specs=[pl.BlockSpec((2, rows, 4, U2), lambda i: (0, i, 0, 0))]
        + [apart if len(s) > 2 and E in s or s[0] == V else whole(*s) for s in shapes],
        scratch_shapes=[
            pltpu.VMEM((2, ceil_to(E, 8), 4, U2), F32),
            pltpu.VMEM((dims.V8, 2, U2), F32),
            pltpu.VMEM((dims.V8, 2, E), F32),
            pltpu.SemaphoreType.DMA((3,)),
        ],
        compiler_params=pltpu.CompilerParams(vmem_limit_bytes=62 << 20),
        name="outputs",
    )(grec, gwin, gwd, small)


def local(
    char_ids, lang_ids, vocab_masks, targets, embedding, w_in, w_rec, b_in, b_rec, w_dec, b_dec
):
    R, hid = lax.axis_size("rows"), lax.axis_size("hid")
    RL, L = char_ids.shape
    E, units = w_in.shape[1], w_in.shape[3]
    V = embedding.shape[1]
    KR = w_rec.shape[1]
    U = units // 2
    dims = Dims(
        R=R, RR=R // 4, Hy=hid // 2, H=units * hid, KR=KR, U=U, RL=RL, L=L, V=V, E=E,
        LANGS=vocab_masks.shape[0], scale=1.0 / (RL * R * L),
    )
    VP, EP, EW = dims.VP, dims.EP, dims.EW

    win = jnp.pad(w_in.transpose(0, 2, 1, 3), ((0, 0), (0, 0), (0, EP - E), (0, 0)))
    wrec = w_rec.transpose(0, 2, 1, 3)
    wdec = jnp.pad(w_dec, ((0, 0), (0, 0), (0, VP - V))).reshape(2, 2, U, VP)
    emb = jnp.concatenate([embedding, jnp.ones((2, V, 1), BF16)], axis=2)
    emb = jnp.pad(emb, ((0, 0), (0, VP - V), (0, EP - E - 1)))

    sums = call_kernel(
        dims, char_ids.T, targets.transpose(0, 2, 1), lang_ids[None], b_in, b_rec, win, wrec, wdec, emb, b_dec,
        vocab_masks,
    )
    w_rec_grad, w_in_grad, b_in_grad, b_rec_grad, w_dec_grad, emb_grad, b_dec_grad, loss = call_outputs(dims, *sums)
    return (
        loss[0, 0],
        emb_grad.transpose(1, 0, 2),
        w_in_grad,
        w_rec_grad,
        b_in_grad,
        b_rec_grad,
        w_dec_grad.transpose(1, 2, 0),
        b_dec_grad,
    )


def solution(mesh):
    placed = (
        P("rows", None),
        P("rows"),
        P(),
        P(None, "rows", None),
        P(),
        P(None, None, None, "hid"),
        P(None, "rows", None, "hid"),
        P(None, None, "hid"),
        P(None, None, "hid"),
        P(None, "hid", None),
        P(),
    )
    return jax.shard_map(
        local,
        mesh=mesh,
        in_specs=placed,
        out_specs=(
            P(),
            P(),
            P(None, None, None, "hid"),
            P(None, "rows", None, "hid"),
            P(None, None, "hid"),
            P(None, None, "hid"),
            P(None, "hid", None),
            P(),
        ),
        check_vma=False,
    )
```
